32 devices in a mesh: rep: 4 (over y, x), fsdp: 8 (over z, core).
Axes of the slice: x: 2, y: 2, z: 4, core: 2. Of those that a mesh axis runs over, the one named last changes fastest.
Arguments:
- tokens: bfloat16 [4, 2048, 768], P('rep', 'fsdp'), may hold values from -6 to 6
- cotangent: bfloat16 [4, 2048, 768], P('rep', 'fsdp'), may hold values from -6 to 6
- lengths: int32 [4], P('rep'), may hold values from 1024 to 2048, as said below
- routes: int32 [4, 2048, 2], P('rep', 'fsdp'), may hold values from 0 to 3, all different within a row; in each aligned block of 256 rows (0 to 255, 256 to 511, ..., all dimensions but the last counted through in order) at most 160 rows name the same one
- gain_attn: bfloat16 [768], P('fsdp'), may hold values from 0.25 to 1.75
- gain_ffn: bfloat16 [768], P('fsdp'), may hold values from 0.25 to 1.75
- w_query: bfloat16 [768, 768], P('fsdp'), may hold values from -0.21875 to 0.21875
- w_key: bfloat16 [768, 768], P('fsdp'), may hold values from -0.21875 to 0.21875
- w_value: bfloat16 [768, 768], P('fsdp'), may hold values from -0.21875 to 0.21875
- w_out: bfloat16 [768, 768], P('fsdp'), may hold values from -1.75 to 1.75
- w_router: bfloat16 [768, 4], P('fsdp'), may hold values from -0.21875 to 0.21875
- shared_gate: bfloat16 [768, 2048], P('fsdp'), may hold values from -0.21875 to 0.21875
- shared_up: bfloat16 [768, 2048], P('fsdp'), may hold values from -0.21875 to 0.21875
- shared_down: bfloat16 [2048, 768], P('fsdp'), may hold values from -0.125 to 0.125
- expert_gate: bfloat16 [768, 8192], P(None, 'fsdp'), may hold values from -0.21875 to 0.21875
- expert_up: bfloat16 [768, 8192], P(None, 'fsdp'), may hold values from -0.21875 to 0.21875
- expert_down: bfloat16 [8192, 768], P('fsdp'), may hold values from -0.5 to 0.5
Outputs:
- output: bfloat16 [4, 2048, 768], P('rep', 'fsdp')
- input_grad: float32 [4, 2048, 768], P('rep', 'fsdp')
- grad_gain_attn: float32 [768], P('fsdp')
- grad_gain_ffn: float32 [768], P('fsdp')
- grad_w_query: float32 [768, 768], P('fsdp')
- grad_w_key: float32 [768, 768], P('fsdp')
- grad_w_value: float32 [768, 768], P('fsdp')
- grad_w_out: float32 [768, 768], P('fsdp')
- grad_w_router: float32 [768, 4], P('fsdp')
- grad_shared_gate: float32 [768, 2048], P('fsdp')
- grad_shared_up: float32 [768, 2048], P('fsdp')
- grad_shared_down: float32 [2048, 768], P('fsdp')
- grad_expert_gate: float32 [768, 8192], P(None, 'fsdp')
- grad_expert_up: float32 [768, 8192], P(None, 'fsdp')
- grad_expert_down: float32 [8192, 768], P('fsdp')
The draws below stay inside these ranges and needn't reach their ends.
Inputs may be any that keep to these rules, and one draw needn't show every extreme that they name: `lengths`: each slot's live positions come first and its padded positions after them; in every draw one slot, drawn from the seed, is full. `routes`: each position names two different experts; in each aligned block of 256 positions of a slot no expert is named by more than 160 of them, and in some block one is named by exactly 160. Routes of padded positions are ignored.
All inputs are finite; a program needn't handle non-finite values.
Results may differ from the reference program's by a relative error of at most 0.02.
Values may be sent and summed in bfloat16 or wider, within the bound.
No kernel may reach another device: no remote copies, remote signals or barrier semaphores. Data moves between devices by JAX's collectives and lax.ppermute only.
A program may use at most 256 MiB of HBM per device.

```python
import math
import jax
import jax.numpy as jnp
import numpy as np
from jax import lax

D = 768
HEADS = 12
HEAD_DIM = 64
FFE = 2048
FFS = 2048
TOK_DEV = 256
MIN_LEN = 1024
SLOTS = 4
SEQ = 2048
EXPERTS = 4
CAP = 160
N_FSDP = 8


def draw_lengths(key, part):
    key = jax.random.fold_in(key, 11)
    pick_key, length_key = jax.random.split(key)
    lowest = min(MIN_LEN, SEQ)
    drawn = jax.random.randint(length_key, (SLOTS,), lowest, SEQ + 1, dtype=jnp.int32)
    full_slot = jax.random.randint(pick_key, (), 0, SLOTS, dtype=jnp.int32)
    return jnp.where(jnp.arange(SLOTS, dtype=jnp.int32) == full_slot, SEQ, drawn).astype(jnp.int32)


def shard_levels(own_key, shape, cuts, smallest, largest):
    def one(position, blocks):
        heights = jax.random.uniform(jax.random.fold_in(jax.random.fold_in(own_key, 6), position), (blocks,), jnp.float32, smallest / len(cuts), largest / len(cuts))
        return jnp.repeat(jnp.exp(heights), shape[position] // blocks).reshape((-1,) + (1,) * (len(shape) - position - 1))

    loudness = one(*cuts[0])
    for cut in cuts[1:]:
        loudness = loudness * one(*cut)
    return loudness


def assign_block(key, own, number, rows, number_of, top, bound, slope):
    order = jax.random.permutation(key, number_of)
    heavy_load, usual = load_shares(number_of, rows * top, bound, slope, True), load_shares(number_of, rows * top, bound, slope, False)
    places = jnp.arange(number_of)

    def named(tallies, offset_by):
        used = int((tallies > 0).sum())
        fixed = max(1, used // 4)
        moved = fixed + (places - fixed + offset_by * (used - fixed)) % max(1, number_of - fixed)
        return jnp.zeros((number_of,), jnp.int32).at[order[jnp.where(places < fixed, places, moved)]].set(jnp.asarray(tallies, jnp.int32))

    tallies = jnp.where(number % 4 == 0, named(heavy_load, number // 4), named(usual, number - number // 4 - 1))
    mixed = jax.random.permutation(jax.random.fold_in(own, 3), number_of)
    donor, taker = mixed[0:number_of // 2 * 2:2], mixed[1:number_of // 2 * 2:2]
    margin = jnp.minimum(tallies[donor] - 1, bound - tallies[taker]) // 2
    margin = jnp.where((donor == order[0]) | (taker == order[0]) | (tallies[taker] == 0), 0, jnp.maximum(margin, 0))
    moved = jax.random.randint(jax.random.fold_in(own, 4), (number_of // 2,), 0, 1 << 20) % (margin + 1)
    tallies = tallies.at[donor].add(-moved).at[taker].add(moved)
    labels = jnp.searchsorted(jnp.cumsum(tallies), jnp.arange(rows * top), side="right").astype(jnp.int32)
    table = labels.reshape(top, rows).T
    table = table[jax.random.permutation(jax.random.fold_in(own, 1), rows)]
    offset_by = jax.random.randint(jax.random.fold_in(own, 2), (rows, 1), 0, top)
    return jnp.take_along_axis(table, (jnp.arange(top)[None, :] + offset_by) % top, axis=1)


def load_shares(number_of, total, most, skew, full):
    portions = [(1 << 20) // math.isqrt(standing ** skew) + 1 for standing in range(1, number_of + 1)]
    largest = most if full else min(most, max(-(-total // number_of), total * portions[0] // sum(portions)))
    least = 1 if total - largest >= number_of - 1 else 0
    holding, rest = [largest] + [least] * (number_of - 1), total - largest - least * (number_of - 1)
    while rest > 0:
        candidates = [i for i in range(1, number_of) if holding[i] < largest] or [i for i in range(1, number_of) if holding[i] < most]
        pool, left = sum([portions[i] for i in candidates]), rest
        for i in candidates:
            more = min(most - holding[i], max(1, left * portions[i] // pool), rest)
            holding[i] = holding[i] + more
            rest = rest - more
    return np.array(holding)


def gaussian(stream_key, dims, spread, reach, cuts=(), kind=jnp.bfloat16):
    values = spread * jax.random.normal(stream_key, dims, jnp.float32)
    if cuts:
        values = values * shard_levels(stream_key, dims, cuts, -0.22, 0.18)
    return jnp.clip(values, -reach, reach).astype(kind)


def setup_inputs(seed: int = 0) -> dict:
    key_of = jax.random.split(jax.random.key(seed), 18)
    tokens = gaussian(key_of[0], (SLOTS, SEQ, D), 1.0, 6.0, ((0, 4), (1, 8)))
    cotangent = gaussian(key_of[1], (SLOTS, SEQ, D), 1.0, 6.0, ((0, 4), (1, 8)))
    lengths = draw_lengths(jax.random.fold_in(key_of[17], 71), 0)
    routes_keys = jax.random.split(jax.random.fold_in(key_of[3], 1), SLOTS * SEQ // TOK_DEV)
    routes_turns = jax.random.permutation(jax.random.fold_in(key_of[3], 3), SLOTS * SEQ // TOK_DEV)
    routes = jax.vmap(lambda own, number: assign_block(jax.random.fold_in(key_of[3], 2), own, number, TOK_DEV, EXPERTS, 2, CAP, 2))(routes_keys, routes_turns).reshape((SLOTS, SEQ, 2))
    gain_attn = jnp.clip(1.0 + 0.15 * jax.random.normal(key_of[4], (D,), jnp.float32), 0.25, 1.75).astype(jnp.bfloat16)
    gain_ffn = jnp.clip(1.0 + 0.15 * jax.random.normal(key_of[5], (D,), jnp.float32), 0.25, 1.75).astype(jnp.bfloat16)
    w_query = gaussian(key_of[6], (D, D), D ** -0.5, 0.21875, ((0, 8),))
    w_key = gaussian(key_of[7], (D, D), D ** -0.5, 0.21875, ((0, 8),))
    w_value = gaussian(key_of[8], (D, D), D ** -0.5, 0.21875, ((0, 8),))
    w_out = gaussian(key_of[9], (D, D), (D // 64) ** -0.5, 1.75, ((0, 8),))
    w_router = gaussian(key_of[10], (D, EXPERTS), D ** -0.5, 0.21875, ((0, 8),))
    shared_gate = gaussian(key_of[11], (D, FFS), D ** -0.5, 0.21875, ((0, 8),))
    shared_up = gaussian(key_of[12], (D, FFS), D ** -0.5, 0.21875, ((0, 8),))
    shared_down = gaussian(key_of[13], (FFS, D), FFS ** -0.5, 0.125, ((0, 8),))
    expert_gate = gaussian(key_of[14], (D, EXPERTS * FFE), D ** -0.5, 0.21875, ((1, 8),))
    expert_up = gaussian(key_of[15], (D, EXPERTS * FFE), D ** -0.5, 0.21875, ((1, 8),))
    expert_down = gaussian(key_of[16], (EXPERTS * FFE, D), (FFE // 16) ** -0.5, 0.5, ((0, 8),))
    return dict(tokens=tokens, cotangent=cotangent, lengths=lengths, routes=routes, gain_attn=gain_attn, gain_ffn=gain_ffn, w_query=w_query, w_key=w_key, w_value=w_value, w_out=w_out, w_router=w_router, shared_gate=shared_gate, shared_up=shared_up, shared_down=shared_down, expert_gate=expert_gate, expert_up=expert_up, expert_down=expert_down)


EPSILON = 1e-06
ROPE_BASE = 10000.0
NEG_FILL = -1e+30

@jax.custom_vjp
def low(v):
    return lax.optimization_barrier(v.astype(jnp.bfloat16)).astype(jnp.float32)

@jax.custom_vjp
def low_back(v):
    return v

def low_keep(v):
    return (low(v), None)

def low_pass(kept, grad):
    return (grad,)

def back_keep(v):
    return (v, None)

def back_low(kept, grad):
    return (low(grad),)
low.defvjp(low_keep, low_pass)
low_back.defvjp(back_keep, back_low)

def matmul(first_op, second_op):
    return jnp.dot(first_op, second_op, precision=lax.Precision.HIGHEST, preferred_element_type=jnp.float32)

def rms_norm(values, gain_vec):
    return values * lax.rsqrt(lax.optimization_barrier(jnp.mean(values * values, axis=-1, keepdims=True)) + EPSILON) * gain_vec

def rotate(values, positions, direction):
    half_dim = values.shape[-1] // 2
    frequency = ROPE_BASE ** (-jnp.arange(half_dim, dtype=jnp.float32) / half_dim)
    angles = positions.astype(jnp.float32)[:, None] * frequency[None, :]
    cosine = jnp.cos(angles)[:, None, :]
    sine_part = direction * jnp.sin(angles)[:, None, :]
    first_half = values[..., :half_dim]
    second = values[..., half_dim:]
    return jnp.concatenate([first_half * cosine - second * sine_part, second * cosine + first_half * sine_part], axis=-1)

def attend(queries, key_rows, value_rows, length):
    seq_len = queries.shape[0]
    rows_block = min(512, seq_len)
    key_pos = jnp.arange(seq_len, dtype=jnp.int32)

    def one_block(offset):
        query_blk = lax.dynamic_slice_in_dim(queries, offset, rows_block, 0)
        query_pos = offset + jnp.arange(rows_block, dtype=jnp.int32)
        scores = low_back(jnp.einsum('qhd,khd->hqk', query_blk, key_rows, precision=lax.Precision.HIGHEST) * 0.125)
        allowed = (key_pos[None, :] <= query_pos[:, None]) & (key_pos[None, :] < length)
        scores = jnp.where(allowed[None], scores, NEG_FILL)
        attention_weights_soft = jax.nn.softmax(scores, axis=-1)
        return jnp.einsum('hqk,khd->qhd', low(attention_weights_soft), value_rows, precision=lax.Precision.HIGHEST)
    starts = jnp.arange(seq_len // rows_block, dtype=jnp.int32) * rows_block
    blocks = lax.map(jax.checkpoint(one_block), starts)
    return blocks.reshape(seq_len, queries.shape[1], queries.shape[2])

def swiglu_down(rows_in, gate_w, up_w, down_w):
    gate_act = low_back(matmul(rows_in, gate_w))
    up_act = low_back(matmul(rows_in, up_w))
    hidden_act = low_back(low(jax.nn.silu(gate_act) * up_act))
    return matmul(hidden_act, down_w)

def expert_mix(normed_ffn, router_probs, route_rows, length, expert_gate, expert_up, expert_down):
    seq_len = normed_ffn.shape[0]
    flat_expert = route_rows.reshape(-1)
    flat_token = jnp.arange(2 * seq_len, dtype=jnp.int32) // 2
    flat_live = flat_token < length
    flat_gate = jnp.take_along_axis(router_probs, route_rows, axis=1).reshape(-1)
    half_width = FFE // 2
    capacity = N_FSDP * CAP

    def one_expert(running, expert):
        chosen = (flat_expert == expert) & flat_live
        picked = jnp.nonzero(chosen, size=capacity, fill_value=0)[0].astype(jnp.int32)
        filled = jnp.arange(capacity, dtype=jnp.int32) < jnp.sum(chosen.astype(jnp.int32))
        token_idx = flat_token[picked]
        rows_in = normed_ffn[token_idx]
        result = jnp.zeros((capacity, normed_ffn.shape[1]), jnp.float32)
        for half_idx in range(2):
            column = ((expert * 2 + half_idx) * half_width).astype(jnp.int32)
            gate_w = lax.dynamic_slice_in_dim(expert_gate, column, half_width, 1)
            up_w = lax.dynamic_slice_in_dim(expert_up, column, half_width, 1)
            down_w = lax.dynamic_slice_in_dim(expert_down, column, half_width, 0)
            result = result + low(swiglu_down(low_back(rows_in), gate_w, up_w, down_w))
        result = low_back(result)
        gate_scale = jnp.where(filled, flat_gate[picked], 0.0)
        return (running.at[token_idx].add(gate_scale[:, None] * result), None)
    mixture, _ = lax.scan(jax.checkpoint(one_expert), jnp.zeros_like(normed_ffn), jnp.arange(EXPERTS, dtype=jnp.int32))
    return mixture

def slot_forward(weights, slot_tokens, length, route_rows):
    gain_attn, gain_ffn, w_query, w_key, w_value, w_out, w_router, shared_gate, shared_up, shared_down, expert_gate, expert_up, expert_down = weights
    seq_len = slot_tokens.shape[0]
    positions = jnp.arange(seq_len, dtype=jnp.int32)
    live_col = (positions < length).astype(jnp.float32)[:, None]
    normed = low(rms_norm(slot_tokens, gain_attn))
    queries = low(rotate(low_back(matmul(normed, w_query)).reshape(seq_len, HEADS, HEAD_DIM), positions, 1.0))
    key_rows = low(rotate(low_back(matmul(normed, w_key)).reshape(seq_len, HEADS, HEAD_DIM), positions, 1.0))
    value_rows = low(low_back(matmul(normed, w_value))).reshape(seq_len, HEADS, HEAD_DIM)
    mixed_rows = low_back(low(attend(queries, key_rows, value_rows, length))).reshape(seq_len, D)
    hidden = slot_tokens + low_back(matmul(mixed_rows, w_out))
    normed_ffn = low(rms_norm(hidden, gain_ffn))
    router_probs = jax.nn.softmax(low_back(matmul(normed_ffn, w_router)), axis=-1)
    shared_out = swiglu_down(normed_ffn, shared_gate, shared_up, shared_down)
    moe_out = expert_mix(normed_ffn, router_probs, route_rows, length, expert_gate, expert_up, expert_down)
    return low(live_col * (hidden + shared_out + moe_out))

def reference(tokens, cotangent, lengths, routes, gain_attn, gain_ffn, w_query, w_key, w_value, w_out, w_router, shared_gate, shared_up, shared_down, expert_gate, expert_up, expert_down):
    weights = jax.tree.map(lambda arr_in: arr_in.astype(jnp.float32), (gain_attn, gain_ffn, w_query, w_key, w_value, w_out, w_router, shared_gate, shared_up, shared_down, expert_gate, expert_up, expert_down))

    def forward(weight_set, token_set):

        def one_slot(carry, inputs):
            slot_tokens, length, route_rows = inputs
            output = jax.checkpoint(slot_forward)(weight_set, slot_tokens, length, route_rows)
            return (carry, output)
        _, outputs = lax.scan(one_slot, jnp.zeros((), jnp.float32), (token_set, lengths, routes))
        return outputs
    outputs, pullback = jax.vjp(forward, weights, tokens.astype(jnp.float32))
    weight_grads, input_grad = pullback(cotangent.astype(jnp.float32))
    return (outputs.astype(jnp.bfloat16), input_grad, weight_grads[0], weight_grads[1], weight_grads[2], weight_grads[3], weight_grads[4], weight_grads[5], weight_grads[6], weight_grads[7], weight_grads[8], weight_grads[9], weight_grads[10], weight_grads[11], weight_grads[12])
```

```python
import functools

import jax
import jax.numpy as jnp
from jax import lax
from jax.experimental import pallas as pl
from jax.experimental.pallas import tpu as pltpu
from jax.sharding import PartitionSpec as P

HEADS = 12
HEAD_DIM = 64

EPSILON = 1e-06
ROPE_BASE = 10000.0
NEG_FILL = -1e30
F32 = jnp.float32
BF16 = jnp.bfloat16


def contract(first_op, second_op, first_dim, second_dim):
    return lax.dot_general(
        first_op,
        second_op,
        (((first_dim,), (second_dim,)), ((), ())),
        preferred_element_type=F32,
    )


def matmul(first_op, second_op):
    return contract(first_op, second_op, 1, 0)


def matmul_tn(first_op, second_op):
    return contract(first_op, second_op, 0, 0)


def matmul_nt(first_op, second_op):
    return contract(first_op, second_op, 1, 1)


def inv_rms(values):
    return lax.rsqrt(jnp.mean(values * values, axis=-1, keepdims=True) + EPSILON)


def rms_back(values, scale, grad_scaled):
    return scale * grad_scaled - values * (
        scale * scale * scale * jnp.mean(grad_scaled * values, axis=-1, keepdims=True)
    )


def swiglu(gate_act, up_act):
    return (jax.nn.silu(gate_act) * up_act).astype(BF16)


def swiglu_grad(grad_inner, gate_act, up_act):
    grad_inner = grad_inner.astype(F32)
    sig = jax.nn.sigmoid(gate_act)
    grad_gate = grad_inner * up_act * (sig * (1.0 + gate_act * (1.0 - sig)))
    grad_up = grad_inner * (gate_act * sig)
    return (grad_gate.astype(BF16), grad_up.astype(BF16))


def rope_tables(seq_len):
    half_dim = HEAD_DIM // 2
    frequency = ROPE_BASE ** (-jnp.arange(half_dim, dtype=F32) / half_dim)
    angles = frequency[:, None] * jnp.arange(seq_len, dtype=F32)[None, :]
    return (jnp.cos(angles), jnp.sin(angles))


def rotate_cols(values, cosine, sine):
    rows, seq_len = values.shape
    split = values.reshape(rows // HEAD_DIM, 2, HEAD_DIM // 2, seq_len)
    first, second = (split[:, 0], split[:, 1])
    turned = jnp.stack(
        [first * cosine - second * sine, second * cosine + first * sine], axis=1
    )
    return turned.reshape(rows, seq_len)


def attn_forward_kernel(len_ref, q_ref, k_ref, v_ref, o_ref, l_ref, *, heads, blk):
    row = pl.program_id(0)
    length = len_ref[0]
    queries = q_ref[...]

    def step(masked, col, state):
        cols = pl.ds(pl.multiple_of(col * blk, blk), blk)
        keys, values = (k_ref[:, cols], v_ref[:, cols])
        if masked:
            key_pos = col * blk + lax.broadcasted_iota(jnp.int32, (blk, blk), 0)
            query_pos = row * blk + lax.broadcasted_iota(jnp.int32, (blk, blk), 1)
            allowed = (key_pos <= query_pos) & (key_pos < length)
        result = []
        for head in range(heads):
            top, total, acc = state[head]
            part = slice(head * HEAD_DIM, (head + 1) * HEAD_DIM)
            scores = matmul_tn(keys[part], queries[part])
            if masked:
                scores = jnp.where(allowed, scores, NEG_FILL)
            new_top = jnp.maximum(top, jnp.max(scores, axis=0, keepdims=True))
            probs = jnp.exp(scores - new_top)
            shrink = jnp.exp(top - new_top)
            total = total * shrink + jnp.sum(probs, axis=0, keepdims=True)
            acc = acc * shrink + matmul(values[part], probs.astype(BF16))
            result.append((new_top, total, acc))
        return tuple(result)

    start = tuple(
        (
            jnp.full((1, blk), NEG_FILL, F32),
            jnp.zeros((1, blk), F32),
            jnp.zeros((HEAD_DIM, blk), F32),
        )
        for _ in range(heads)
    )
    whole = jnp.minimum(row, length // blk)
    end = jnp.minimum(row + 1, (length + blk - 1) // blk)
    state = lax.fori_loop(0, whole, functools.partial(step, False), start)
    state = lax.fori_loop(whole, end, functools.partial(step, True), state)
    for head in range(heads):
        top, total, acc = state[head]
        o_ref[head * HEAD_DIM : (head + 1) * HEAD_DIM, :] = acc * (1.0 / total)
        l_ref[head : head + 1, :] = top + jnp.log(total)


def attn_backward_kernel(
    len_ref, q_ref, k_ref, v_ref, o_ref, l_ref, do_ref, dq_ref, dk_ref, dv_ref, *, heads, blk
):
    row = pl.program_id(0)
    length = len_ref[0]

    @pl.when(row == 0)
    def _():
        dk_ref[...] = jnp.zeros_like(dk_ref)
        dv_ref[...] = jnp.zeros_like(dv_ref)

    parts = [slice(head * HEAD_DIM, (head + 1) * HEAD_DIM) for head in range(heads)]
    queries, grad_out = (q_ref[...], do_ref[...])
    deltas = [
        jnp.sum(grad_out[part].astype(F32) * o_ref[part, :], axis=0, keepdims=True)
        for part in parts
    ]
    log_norms = [l_ref[head : head + 1, :] for head in range(heads)]

    def step(masked, col, state):
        cols = pl.ds(pl.multiple_of(col * blk, blk), blk)
        keys, values = (k_ref[:, cols], v_ref[:, cols])
        if masked:
            key_pos = col * blk + lax.broadcasted_iota(jnp.int32, (blk, blk), 0)
            query_pos = row * blk + lax.broadcasted_iota(jnp.int32, (blk, blk), 1)
            allowed = (key_pos <= query_pos) & (key_pos < length)
        result = []
        for head, part in enumerate(parts):
            scores = matmul_tn(keys[part], queries[part])
            grad_probs = matmul_tn(values[part], grad_out[part])
            probs = jnp.exp(scores - log_norms[head])
            if masked:
                probs = jnp.where(allowed, probs, 0.0)
            grad_scores = (probs * (grad_probs - deltas[head])).astype(BF16)
            dv_ref[part, cols] += matmul_nt(grad_out[part], probs.astype(BF16))
            dk_ref[part, cols] += matmul_nt(queries[part], grad_scores)
            result.append(state[head] + matmul(keys[part], grad_scores))
        return tuple(result)

    start = tuple(jnp.zeros((HEAD_DIM, blk), F32) for _ in range(heads))
    whole = jnp.minimum(row, length // blk)
    end = jnp.minimum(row + 1, (length + blk - 1) // blk)
    state = lax.fori_loop(0, whole, functools.partial(step, False), start)
    state = lax.fori_loop(whole, end, functools.partial(step, True), state)
    for head, part in enumerate(parts):
        dq_ref[part, :] = state[head]


def attn_specs(rows, seq_len, heads, blk):
    block = pl.BlockSpec((rows, blk), lambda i, _: (0, i))
    whole = pl.BlockSpec((rows, seq_len), lambda i, _: (0, 0))
    stats = pl.BlockSpec((heads, blk), lambda i, _: (0, i))
    return (block, whole, stats)


def attn_cost(rows, seq_len, heads, products):
    pairs = heads * seq_len * seq_len // 2
    return pl.CostEstimate(
        flops=2 * products * pairs * 256, bytes_accessed=16 * rows * seq_len, transcendentals=pairs
    )


def attn_forward(length, queries, keys, values):
    rows, seq_len = queries.shape
    heads, blk = (rows // HEAD_DIM, min(512, seq_len))
    block, whole, stats = attn_specs(rows, seq_len, heads, blk)
    return pl.pallas_call(
        functools.partial(attn_forward_kernel, heads=heads, blk=blk),
        out_shape=(
            jax.ShapeDtypeStruct((rows, seq_len), F32),
            jax.ShapeDtypeStruct((heads, seq_len), F32),
        ),
        grid_spec=pltpu.PrefetchScalarGridSpec(
            num_scalar_prefetch=1,
            grid=(seq_len // blk,),
            in_specs=[block, whole, whole],
            out_specs=(block, stats),
        ),
        compiler_params=pltpu.CompilerParams(vmem_limit_bytes=40 << 20),
        cost_estimate=attn_cost(rows, seq_len, heads, 2),
        name="attn_forward",
    )(length, queries, keys, values)


def attn_backward(length, queries, keys, values, mixed, log_norm, grad_mixed):
    rows, seq_len = queries.shape
    heads, blk = (rows // HEAD_DIM, min(512, seq_len))
    block, whole, stats = attn_specs(rows, seq_len, heads, blk)
    return pl.pallas_call(
        functools.partial(attn_backward_kernel, heads=heads, blk=blk),
        out_shape=(jax.ShapeDtypeStruct((rows, seq_len), F32),) * 3,
        grid_spec=pltpu.PrefetchScalarGridSpec(
            num_scalar_prefetch=1,
            grid=(seq_len // blk,),
            in_specs=[block, whole, whole, block, stats, block],
            out_specs=(block, whole, whole),
        ),
        compiler_params=pltpu.CompilerParams(vmem_limit_bytes=40 << 20),
        cost_estimate=attn_cost(rows, seq_len, heads, 5),
        name="attn_backward",
    )(length, queries, keys, values, mixed, log_norm, grad_mixed)


def gather_rows(values):
    return lax.all_gather(values, "fsdp", axis=0, tiled=True)


def exchange(chunks):
    return lax.all_to_all(chunks, "fsdp", split_axis=0, concat_axis=0, tiled=True)


def scatter_sum(values):
    return lax.psum_scatter(values, "fsdp", scatter_dimension=0, tiled=True)


def on_device(
    tokens,
    cotangent,
    lengths,
    routes,
    gain_attn,
    gain_ffn,
    w_query,
    w_key,
    w_value,
    w_out,
    w_router,
    shared_gate,
    shared_up,
    shared_down,
    expert_gate,
    expert_up,
    expert_down,
):
    rows_dev, width = tokens.shape[1:]
    groups = lax.axis_size("fsdp")
    me = lax.axis_index("fsdp")
    seq_len = groups * rows_dev
    experts = w_router.shape[1]
    capacity = min(rows_dev, 5 * rows_dev // (2 * experts))
    length = lengths[0]
    my_rows = me * rows_dev
    live_all = jnp.arange(seq_len, dtype=jnp.int32) < length
    live_col = lax.dynamic_slice_in_dim(live_all, my_rows, rows_dev, 0).astype(F32)[:, None]

    cols_dev = width // groups
    first_heads = [d * cols_dev // HEAD_DIM for d in range(groups)]
    span = max(-(-(d + 1) * cols_dev // HEAD_DIM) - first_heads[d] for d in range(groups))
    first_heads = [min(head, HEADS - span) for head in first_heads]
    window = span * HEAD_DIM
    window_starts = [head * HEAD_DIM for head in first_heads]
    offsets = [d * cols_dev - window_starts[d] for d in range(groups)]
    my_offset = jnp.asarray(offsets, jnp.int32)[me]

    tokens_all = gather_rows(tokens[0])
    gain_attn_col = gain_attn.astype(F32)[:, None]
    qkv_rows = [
        (weight.astype(F32) * gain_attn_col).astype(BF16) for weight in (w_query, w_key, w_value)
    ]
    qkv_chunks = jnp.stack(
        [
            jnp.concatenate([weight[:, at : at + window] for weight in qkv_rows], axis=1)
            for at in window_starts
        ]
    )
    qkv_cols = exchange(qkv_chunks).reshape(width, 3 * window)
    shared_cols_dev = shared_gate.shape[1] // groups
    gate_up_chunks = jnp.concatenate(
        [
            weight.reshape(-1, groups, shared_cols_dev).transpose(1, 0, 2)
            for weight in (shared_gate, shared_up)
        ],
        axis=2,
    )
    packed_rows = jnp.concatenate([w_out, w_router, gain_ffn[:, None]], axis=1)
    packed_all = gather_rows(packed_rows)
    out_full = packed_all[:, :width]
    router_full = packed_all[:, width : width + experts]
    gain_two = packed_all[:, width + experts].astype(F32)[None, :]
    cosine, sine = rope_tables(seq_len)

    inputs_all = tokens_all.astype(F32)
    unit = (inputs_all * inv_rms(inputs_all)).astype(BF16)
    qkv = contract(qkv_cols, unit, 0, 1)
    queries = (rotate_cols(qkv[:window], cosine, sine).astype(BF16).astype(F32) * 0.125).astype(
        BF16
    )
    keys = rotate_cols(qkv[window : 2 * window], cosine, sine).astype(BF16)
    values = qkv[2 * window :].astype(BF16)
    mixed_heads, log_norm = attn_forward(lengths, queries, keys, values)
    mixed_own = lax.dynamic_slice_in_dim(mixed_heads, my_offset, cols_dev, 0).astype(BF16)
    mixed_all = gather_rows(mixed_own)

    gate_up_cols = exchange(gate_up_chunks).reshape(width, 2 * shared_cols_dev)
    cotangent_all = gather_rows(cotangent[0])
    routes_all = lax.all_gather(routes[0], "fsdp", axis=0, tiled=True)

    hidden_all = inputs_all + matmul_tn(mixed_all, out_full)
    normed = (hidden_all * inv_rms(hidden_all) * gain_two).astype(BF16)
    router_probs = jax.nn.softmax(matmul(normed, router_full), axis=-1)

    shared_act = matmul(normed, gate_up_cols)
    shared_gate_act = shared_act[:, :shared_cols_dev]
    shared_up_act = shared_act[:, shared_cols_dev:]
    shared_inner = swiglu(shared_gate_act, shared_up_act)
    shared_result = matmul(shared_inner, shared_down)

    my_expert = me // 2
    routed = jnp.any(routes_all == my_expert, axis=1) & live_all
    routed = routed.reshape(groups, rows_dev)
    rank = jnp.cumsum(routed.astype(jnp.int32), axis=1) - 1
    pick = (
        (rank[:, None, :] == jnp.arange(capacity, dtype=jnp.int32)[None, :, None])
        & routed[:, None, :]
    ).astype(BF16)

    def pick_rows(full_rows):
        picked = jnp.einsum(
            "bct,btd->bcd",
            pick,
            full_rows.reshape(groups, rows_dev, -1),
            preferred_element_type=F32,
        )
        return picked.astype(BF16).reshape(groups * capacity, -1)

    def place_rows(picked_rows):
        placed = jnp.einsum(
            "bct,bcd->btd",
            pick,
            picked_rows.reshape(groups, capacity, -1),
            preferred_element_type=F32,
        )
        return placed.reshape(seq_len, -1)

    my_prob = lax.dynamic_slice_in_dim(router_probs, my_expert, 1, 1).reshape(groups, 1, rows_dev)
    row_prob = jnp.sum(jnp.where(pick > 0, my_prob, 0.0), axis=2).reshape(-1, 1)
    rows_in = pick_rows(normed)
    expert_gate_act = matmul(rows_in, expert_gate)
    expert_up_act = matmul(rows_in, expert_up)
    expert_inner = swiglu(expert_gate_act, expert_up_act)
    expert_half = matmul(expert_inner, expert_down).astype(BF16).astype(F32)
    branch_part = shared_result + place_rows((row_prob * expert_half).astype(BF16))

    grad_out_all = jnp.where(live_all[:, None], cotangent_all, jnp.zeros((), BF16))
    shared_gate_grad, shared_up_grad = swiglu_grad(
        matmul_nt(grad_out_all, shared_down).astype(BF16), shared_gate_act, shared_up_act
    )
    shared_act_grad = jnp.concatenate([shared_gate_grad, shared_up_grad], axis=1)
    grad_rows_out = pick_rows(grad_out_all)
    grad_rows_f32 = grad_rows_out.astype(F32)
    route_dots = jnp.sum(grad_rows_f32 * expert_half, axis=1, keepdims=True)
    grad_half = (row_prob * grad_rows_f32).astype(BF16)
    expert_gate_grad, expert_up_grad = swiglu_grad(
        matmul_nt(grad_half, expert_down).astype(BF16), expert_gate_act, expert_up_act
    )
    rows_grad = (
        matmul_nt(expert_gate_grad, expert_gate) + matmul_nt(expert_up_grad, expert_up)
    ).astype(BF16)
    dots_high = route_dots.astype(BF16)
    dots_low = (route_dots - dots_high.astype(F32)).astype(BF16)
    lane = jnp.arange(128, dtype=jnp.int32)[None, :]
    zero = jnp.zeros((), BF16)
    dots_cols = jnp.where(lane == me, dots_high, zero) + jnp.where(
        lane == me + groups, dots_low, zero
    )
    grad_part = place_rows(jnp.concatenate([rows_grad, dots_cols], axis=1))
    grad_part = grad_part + jnp.pad(
        matmul_nt(shared_act_grad, gate_up_cols), ((0, 0), (0, 128))
    )
    grad_own = scatter_sum(grad_part.astype(BF16)).astype(F32)
    branch_own = scatter_sum(branch_part.astype(BF16)).astype(F32)

    grad_expert_gate = matmul_tn(rows_in, expert_gate_grad).astype(BF16)
    grad_expert_up = matmul_tn(rows_in, expert_up_grad).astype(BF16)
    grad_expert_down = matmul_tn(expert_inner, grad_half).astype(BF16)
    sum_expert = lax.psum((grad_expert_gate, grad_expert_up, grad_expert_down), "rep")
    grad_shared_down = matmul_tn(shared_inner, grad_out_all).astype(BF16)
    grad_gate_up_cols = matmul_tn(normed, shared_act_grad).astype(BF16)

    hidden = lax.dynamic_slice_in_dim(hidden_all, my_rows, rows_dev, 0)
    normed_own = lax.dynamic_slice_in_dim(normed, my_rows, rows_dev, 0)
    probs_own = lax.dynamic_slice_in_dim(router_probs, my_rows, rows_dev, 0)
    mixed_rows = lax.dynamic_slice_in_dim(mixed_all, my_rows, rows_dev, 1)
    output = (live_col * (hidden + branch_own)).astype(BF16)
    dots_own = grad_own[:, width : width + groups] + grad_own[:, width + groups : width + 2 * groups]
    grad_rprobs = jnp.sum(dots_own.reshape(rows_dev, experts, 2), axis=2)
    grad_logits = (
        probs_own * (grad_rprobs - jnp.sum(probs_own * grad_rprobs, axis=1, keepdims=True))
    ).astype(BF16)
    grad_normed = grad_own[:, :width] + matmul_nt(grad_logits, router_full)
    scale_two = inv_rms(hidden)
    grad_gain_ffn = jnp.sum(grad_normed * hidden * scale_two, axis=0)
    grad_out = live_col * cotangent[0].astype(F32)
    grad_hidden = grad_out + rms_back(hidden, scale_two, grad_normed * gain_two)
    grad_hidden_b = grad_hidden.astype(BF16)
    grad_mixed = matmul_nt(out_full, grad_hidden_b).astype(BF16)
    mixed_chunks = jnp.stack([grad_mixed[at : at + window] for at in window_starts])
    grad_mixed_cols = exchange(mixed_chunks).transpose(1, 0, 2).reshape(window, seq_len)
    packed_grad = jnp.concatenate(
        [
            matmul(mixed_rows, grad_hidden_b),
            matmul_tn(normed_own, grad_logits),
            grad_gain_ffn[:, None],
        ],
        axis=1,
    )
    packed_own = scatter_sum(packed_grad.astype(BF16))
    gate_up_back = exchange(
        grad_gate_up_cols.reshape(groups, width // groups, 2 * shared_cols_dev)
    )
    gate_up_own = jnp.concatenate(
        [
            gate_up_back[:, :, :shared_cols_dev].transpose(1, 0, 2).reshape(width // groups, -1),
            gate_up_back[:, :, shared_cols_dev:].transpose(1, 0, 2).reshape(width // groups, -1),
        ],
        axis=1,
    )
    sum_dense = lax.psum((grad_shared_down, gate_up_own, packed_own), "rep")

    grad_q, grad_k, grad_v = attn_backward(
        lengths, queries, keys, values, mixed_heads, log_norm, grad_mixed_cols
    )
    channel = jnp.arange(window, dtype=jnp.int32)[:, None]
    owned = (channel >= my_offset) & (channel < my_offset + cols_dev)
    qkv_grad = jnp.concatenate(
        [
            jnp.where(owned, rotate_cols(grad_q * 0.125, cosine, -sine), 0.0),
            jnp.where(owned, rotate_cols(grad_k, cosine, -sine), 0.0),
            jnp.where(owned, grad_v, 0.0),
        ],
        axis=0,
    ).astype(BF16)
    grad_unit = scatter_sum(contract(qkv_grad, qkv_cols, 0, 1).astype(BF16)).astype(F32)
    qkv_weight_grad = contract(unit, qkv_grad, 0, 1).astype(BF16)
    qkv_back = exchange(qkv_weight_grad.reshape(groups, width // groups, 3 * window))
    qkv_own = jnp.concatenate(
        [
            qkv_back[d, :, part * window + offsets[d] : part * window + offsets[d] + cols_dev]
            for part in range(3)
            for d in range(groups)
        ],
        axis=1,
    )
    sum_qkv = lax.psum(qkv_own, "rep").astype(F32)
    inputs = tokens[0].astype(F32)
    input_grad = grad_hidden + rms_back(inputs, inv_rms(inputs), grad_unit)

    sum_gain_attn = sum(
        jnp.sum(sum_qkv[:, part * width : (part + 1) * width] * weight.astype(F32), axis=1)
        for part, weight in enumerate((w_query, w_key, w_value))
    )
    sum_weights = sum_qkv * gain_attn_col
    sum_down, sum_gate_up, sum_packed = [total.astype(F32) for total in sum_dense]
    sum_egate, sum_eup, sum_edown = [total.astype(F32) for total in sum_expert]
    half = sum_gate_up.shape[1] // 2
    return (
        output[None],
        input_grad[None],
        sum_gain_attn,
        sum_packed[:, width + experts],
        sum_weights[:, :width],
        sum_weights[:, width : 2 * width],
        sum_weights[:, 2 * width :],
        sum_packed[:, :width],
        sum_packed[:, width : width + experts],
        sum_gate_up[:, :half],
        sum_gate_up[:, half:],
        sum_down,
        sum_egate,
        sum_eup,
        sum_edown,
    )


def solution(mesh):
    in_specs = (
        P("rep", "fsdp", None),
        P("rep", "fsdp", None),
        P("rep"),
        P("rep", "fsdp", None),
        P("fsdp"),
        P("fsdp"),
        P("fsdp", None),
        P("fsdp", None),
        P("fsdp", None),
        P("fsdp", None),
        P("fsdp", None),
        P("fsdp", None),
        P("fsdp", None),
        P("fsdp", None),
        P(None, "fsdp"),
        P(None, "fsdp"),
        P("fsdp", None),
    )
    out_specs = (
        P("rep", "fsdp", None),
        P("rep", "fsdp", None),
        P("fsdp"),
        P("fsdp"),
        P("fsdp", None),
        P("fsdp", None),
        P("fsdp", None),
        P("fsdp", None),
        P("fsdp", None),
        P("fsdp", None),
        P("fsdp", None),
        P("fsdp", None),
        P(None, "fsdp"),
        P(None, "fsdp"),
        P("fsdp", None),
    )
    return jax.shard_map(
        on_device, mesh=mesh, in_specs=in_specs, out_specs=out_specs, check_vma=False
    )
```

```python
import functools

import jax
import jax.numpy as jnp
from jax import lax
from jax.experimental import pallas as pl
from jax.experimental.pallas import tpu as pltpu
from jax.sharding import PartitionSpec as P

HEADS = 12
HEAD_DIM = 64

EPSILON = 1e-06
ROPE_BASE = 10000.0
NEG_FILL = -1e30
MARK = (8, 128)
F32 = jnp.float32
BF16 = jnp.bfloat16


def contract(first_op, second_op, first_dim, second_dim):
    return lax.dot_general(
        first_op,
        second_op,
        (((first_dim,), (second_dim,)), ((), ())),
        preferred_element_type=F32,
    )


def matmul(first_op, second_op):
    return contract(first_op, second_op, 1, 0)


def matmul_tn(first_op, second_op):
    return contract(first_op, second_op, 0, 0)


def matmul_nt(first_op, second_op):
    return contract(first_op, second_op, 1, 1)


def inv_rms(values):
    return lax.rsqrt(jnp.mean(values * values, axis=-1, keepdims=True) + EPSILON)


def rms_back(values, scale, grad_scaled):
    return scale * grad_scaled - values * (
        scale * scale * scale * jnp.mean(grad_scaled * values, axis=-1, keepdims=True)
    )


def swiglu(gate_act, up_act):
    return (jax.nn.silu(gate_act) * up_act).astype(BF16)


def swiglu_grad(grad_inner, gate_act, up_act):
    grad_inner = grad_inner.astype(F32)
    sig = jax.nn.sigmoid(gate_act)
    grad_gate = grad_inner * up_act * (sig * (1.0 + gate_act * (1.0 - sig)))
    grad_up = grad_inner * (gate_act * sig)
    return (grad_gate.astype(BF16), grad_up.astype(BF16))


def rope_tables(seq_len):
    half_dim = HEAD_DIM // 2
    frequency = ROPE_BASE ** (-jnp.arange(half_dim, dtype=F32) / half_dim)
    angles = frequency[:, None] * jnp.arange(seq_len, dtype=F32)[None, :]
    return (jnp.cos(angles), jnp.sin(angles))


def rotate_cols(values, cosine, sine):
    rows, seq_len = values.shape
    split = values.reshape(rows // HEAD_DIM, 2, HEAD_DIM // 2, seq_len)
    first, second = (split[:, 0], split[:, 1])
    turned = jnp.stack(
        [first * cosine - second * sine, second * cosine + first * sine], axis=1
    )
    return turned.reshape(rows, seq_len)


def attn_forward_kernel(len_ref, q_ref, k_ref, v_ref, o_ref, l_ref, *, heads, blk):
    row = pl.program_id(0)
    length = len_ref[0]
    queries = q_ref[...]

    def step(masked, col, state):
        cols = pl.ds(pl.multiple_of(col * blk, blk), blk)
        keys, values = (k_ref[:, cols], v_ref[:, cols])
        if masked:
            key_pos = col * blk + lax.broadcasted_iota(jnp.int32, (blk, blk), 0)
            query_pos = row * blk + lax.broadcasted_iota(jnp.int32, (blk, blk), 1)
            allowed = (key_pos <= query_pos) & (key_pos < length)
        result = []
        for head in range(heads):
            top, total, acc = state[head]
            part = slice(head * HEAD_DIM, (head + 1) * HEAD_DIM)
            scores = matmul_tn(keys[part], queries[part])
            if masked:
                scores = jnp.where(allowed, scores, NEG_FILL)
            new_top = jnp.maximum(top, jnp.max(scores, axis=0, keepdims=True))
            probs = jnp.exp(scores - new_top)
            shrink = jnp.exp(top - new_top)
            total = total * shrink + jnp.sum(probs, axis=0, keepdims=True)
            acc = acc * shrink + matmul(values[part], probs.astype(BF16))
            result.append((new_top, total, acc))
        return tuple(result)

    start = tuple(
        (
            jnp.full((1, blk), NEG_FILL, F32),
            jnp.zeros((1, blk), F32),
            jnp.zeros((HEAD_DIM, blk), F32),
        )
        for _ in range(heads)
    )
    whole = jnp.minimum(row, length // blk)
    end = jnp.minimum(row + 1, (length + blk - 1) // blk)
    state = lax.fori_loop(0, whole, functools.partial(step, False), start)
    state = lax.fori_loop(whole, end, functools.partial(step, True), state)
    for head in range(heads):
        top, total, acc = state[head]
        o_ref[head * HEAD_DIM : (head + 1) * HEAD_DIM, :] = acc * (1.0 / total)
        l_ref[head : head + 1, :] = top + jnp.log(total)


def attn_backward_kernel(
    len_ref, q_ref, k_ref, v_ref, o_ref, l_ref, do_ref, *refs, heads, blk
):
    dq_ref, dk_ref, dv_ref, mark_ref = refs[-4:]
    mark_ref[...] = jnp.zeros_like(mark_ref)
    row = pl.program_id(0)
    length = len_ref[0]

    @pl.when(row == 0)
    def _():
        dk_ref[...] = jnp.zeros_like(dk_ref)
        dv_ref[...] = jnp.zeros_like(dv_ref)

    parts = [slice(head * HEAD_DIM, (head + 1) * HEAD_DIM) for head in range(heads)]
    queries = q_ref[...]
    grad_out = jnp.concatenate([do_ref[src] for src in range(do_ref.shape[0])], axis=1)
    deltas = [
        jnp.sum(grad_out[part].astype(F32) * o_ref[part, :], axis=0, keepdims=True)
        for part in parts
    ]
    log_norms = [l_ref[head : head + 1, :] for head in range(heads)]

    def step(masked, col, state):
        cols = pl.ds(pl.multiple_of(col * blk, blk), blk)
        keys, values = (k_ref[:, cols], v_ref[:, cols])
        if masked:
            key_pos = col * blk + lax.broadcasted_iota(jnp.int32, (blk, blk), 0)
            query_pos = row * blk + lax.broadcasted_iota(jnp.int32, (blk, blk), 1)
            allowed = (key_pos <= query_pos) & (key_pos < length)
        result = []
        for head, part in enumerate(parts):
            scores = matmul_tn(keys[part], queries[part])
            grad_probs = matmul_tn(values[part], grad_out[part])
            probs = jnp.exp(scores - log_norms[head])
            if masked:
                probs = jnp.where(allowed, probs, 0.0)
            grad_scores = (probs * (grad_probs - deltas[head])).astype(BF16)
            dv_ref[part, cols] += matmul_nt(grad_out[part], probs.astype(BF16))
            dk_ref[part, cols] += matmul_nt(queries[part], grad_scores)
            result.append(state[head] + matmul(keys[part], grad_scores))
        return tuple(result)

    start = tuple(jnp.zeros((HEAD_DIM, blk), F32) for _ in range(heads))
    whole = jnp.minimum(row, length // blk)
    end = jnp.minimum(row + 1, (length + blk - 1) // blk)
    state = lax.fori_loop(0, whole, functools.partial(step, False), start)
    state = lax.fori_loop(whole, end, functools.partial(step, True), state)
    for head, part in enumerate(parts):
        dq_ref[part, :] = state[head]


def attn_specs(rows, seq_len, heads, blk):
    block = pl.BlockSpec((rows, blk), lambda i, _: (0, i))
    whole = pl.BlockSpec((rows, seq_len), lambda i, _: (0, 0))
    stats = pl.BlockSpec((heads, blk), lambda i, _: (0, i))
    return (block, whole, stats)


def attn_cost(rows, seq_len, heads, products):
    pairs = heads * seq_len * seq_len // 2
    return pl.CostEstimate(
        flops=2 * products * pairs * 256, bytes_accessed=16 * rows * seq_len, transcendentals=pairs
    )


def attn_forward(length, queries, keys, values):
    rows, seq_len = queries.shape
    heads, blk = (rows // HEAD_DIM, min(512, seq_len))
    block, whole, stats = attn_specs(rows, seq_len, heads, blk)
    return pl.pallas_call(
        functools.partial(attn_forward_kernel, heads=heads, blk=blk),
        out_shape=(
            jax.ShapeDtypeStruct((rows, seq_len), F32),
            jax.ShapeDtypeStruct((heads, seq_len), F32),
        ),
        grid_spec=pltpu.PrefetchScalarGridSpec(
            num_scalar_prefetch=1,
            grid=(seq_len // blk,),
            in_specs=[block, whole, whole],
            out_specs=(block, stats),
        ),
        compiler_params=pltpu.CompilerParams(vmem_limit_bytes=40 << 20),
        cost_estimate=attn_cost(rows, seq_len, heads, 2),
        name="attn_forward",
    )(length, queries, keys, values)


def attn_backward(length, queries, keys, values, mixed, log_norm, grad_mixed, earlier):
    rows, seq_len = queries.shape
    heads, blk = (rows // HEAD_DIM, min(512, seq_len))
    block, whole, stats = attn_specs(rows, seq_len, heads, blk)
    rows_dev = grad_mixed.shape[2]
    sources = pl.BlockSpec((blk // rows_dev, rows, rows_dev), lambda i, _: (i, 0, 0))
    return pl.pallas_call(
        functools.partial(attn_backward_kernel, heads=heads, blk=blk),
        out_shape=(
            *(jax.ShapeDtypeStruct((rows, seq_len), F32),) * 3,
            jax.ShapeDtypeStruct(MARK, F32),
        ),
        grid_spec=pltpu.PrefetchScalarGridSpec(
            num_scalar_prefetch=1,
            grid=(seq_len // blk,),
            in_specs=[block, whole, whole, block, stats, sources]
            + [pl.BlockSpec(memory_space=pl.ANY)] * len(earlier),
            out_specs=(block, whole, whole, pl.BlockSpec(MARK, lambda i, _: (0, 0))),
        ),
        compiler_params=pltpu.CompilerParams(vmem_limit_bytes=40 << 20),
        cost_estimate=attn_cost(rows, seq_len, heads, 5),
        name="attn_backward",
    )(length, queries, keys, values, mixed, log_norm, grad_mixed, *earlier)


def branch_kernel(
    info_ref,
    mixed_ref,
    tokens_ref,
    cotangent_ref,
    rank_ref,
    out_w_ref,
    gate_ref,
    up_ref,
    small_ref,
    down_ref,
    egate_ref,
    eup_ref,
    edown_ref,
    branch_ref,
    grad_ref,
    normed_ref,
    inner_ref,
    act_grad_ref,
    rows_ref,
    einner_ref,
    egate_grad_ref,
    eup_grad_ref,
    half_grad_ref,
    *,
    experts,
    groups,
    capacity,
):
    rows = tokens_ref.shape[0]
    blocks, _, rows_dev = rank_ref.shape
    length, me = (info_ref[0], info_ref[1])
    first_pos = info_ref[2] + pl.program_id(0) * rows

    hidden = tokens_ref[...].astype(F32) + matmul_tn(mixed_ref[...], out_w_ref[...])
    small = small_ref[...].astype(F32).T
    gain = small[experts : experts + 1]
    normed = (hidden * inv_rms(hidden) * gain).astype(BF16)
    normed_ref[...] = normed
    logits = matmul_nt(small[:16].astype(BF16), normed)
    expert_row = lax.broadcasted_iota(jnp.int32, logits.shape, 0)
    logits = jnp.where(expert_row < experts, logits, NEG_FILL)
    weights = jnp.exp(logits - jnp.max(logits, axis=0, keepdims=True))
    probs = weights / jnp.sum(weights, axis=0, keepdims=True)
    prob_row = jnp.sum(jnp.where(expert_row == me // 2, probs, 0.0), axis=0, keepdims=True)

    position = first_pos + lax.broadcasted_iota(jnp.int32, (rows, 1), 0)
    live = (position < length).astype(F32)
    grad_out = (cotangent_ref[...].astype(F32) * live).astype(BF16)

    gate_act, up_act = (matmul(normed, gate_ref[...]), matmul(normed, up_ref[...]))
    inner = swiglu(gate_act, up_act)
    inner_ref[...] = (inner.astype(F32) * live).astype(BF16)
    branch = matmul(inner, down_ref[...])
    gate_grad, up_grad = swiglu_grad(
        matmul_nt(grad_out, down_ref[...]).astype(BF16), gate_act, up_act
    )
    act_grad = jnp.concatenate([gate_grad, up_grad], axis=1)
    act_grad_ref[...] = act_grad
    grad = matmul_nt(gate_grad, gate_ref[...]) + matmul_nt(up_grad, up_ref[...])

    picks, picked, picked_grad, picked_prob = ([], [], [], [])
    slot = lax.broadcasted_iota(jnp.int32, (capacity, rows_dev), 0)
    for blk in range(blocks):
        part = slice(blk * rows_dev, (blk + 1) * rows_dev)
        hot = (slot == rank_ref[blk]).astype(F32)
        picked_prob.append(jnp.sum(hot * prob_row[:, part], axis=1, keepdims=True))
        pick = hot.astype(BF16)
        picks.append(pick)
        picked.append(matmul(pick, normed[part]).astype(BF16))
        picked_grad.append(matmul(pick, grad_out[part]).astype(BF16))
    rows_in = jnp.concatenate(picked, axis=0)
    grad_rows = jnp.concatenate(picked_grad, axis=0).astype(F32)
    row_prob = jnp.concatenate(picked_prob, axis=0)
    rows_ref[...] = rows_in
    egate_act = matmul(rows_in, egate_ref[...])
    eup_act = matmul(rows_in, eup_ref[...])
    einner = swiglu(egate_act, eup_act)
    einner_ref[...] = einner
    half = matmul(einner, edown_ref[...]).astype(BF16).astype(F32)
    dots = jnp.sum(grad_rows * half, axis=1, keepdims=True)
    half_grad = (row_prob * grad_rows).astype(BF16)
    half_grad_ref[...] = half_grad
    egate_grad, eup_grad = swiglu_grad(
        matmul_nt(half_grad, edown_ref[...]).astype(BF16), egate_act, eup_act
    )
    egate_grad_ref[...] = egate_grad
    eup_grad_ref[...] = eup_grad
    rows_grad = (
        matmul_nt(egate_grad, egate_ref[...]) + matmul_nt(eup_grad, eup_ref[...])
    ).astype(BF16)
    gated = (row_prob * half).astype(BF16)

    dots_high = dots.astype(BF16).astype(F32)
    lane = lax.broadcasted_iota(jnp.int32, (1, 128), 1)
    dots_cols = jnp.where(lane == me, dots_high, 0.0) + jnp.where(
        lane == me + groups, dots - dots_high, 0.0
    )
    dots_cols = dots_cols.astype(BF16)
    width = normed.shape[1]
    for blk in range(blocks):
        part = slice(blk * rows_dev, (blk + 1) * rows_dev)
        from_part = slice(blk * capacity, (blk + 1) * capacity)
        pick = picks[blk]
        branch_ref[part, :] = (branch[part] + matmul_tn(pick, gated[from_part])).astype(BF16)
        grad_ref[part, :width] = (grad[part] + matmul_tn(pick, rows_grad[from_part])).astype(BF16)
        grad_ref[part, width:] = matmul_tn(pick, dots_cols[from_part]).astype(BF16)


def run_branches(
    info, mixed, tokens, cotangent, rank, packed, down, egate, eup, edown, experts, capacity
):
    seq_len, width = tokens.shape
    groups, _, rows_dev = rank.shape
    blocks = 2 if groups % 2 == 0 else 1
    rows, picked = (blocks * rows_dev, blocks * capacity)
    hidden, ehidden = (down.shape[0], egate.shape[1])
    act_cols = 2 * hidden

    def step_rows(count, cols):
        return pl.BlockSpec((count, cols), lambda i, _: (i, 0))

    def whole(shape):
        return pl.BlockSpec(shape, lambda i, _: (0, 0), pipeline_mode=pl.Buffered(1))

    def packed_part(cols, at):
        return pl.BlockSpec(
            (width, cols), lambda i, _: (0, at // cols), pipeline_mode=pl.Buffered(1)
        )

    def result(count, cols):
        return jax.ShapeDtypeStruct((count, cols), BF16)

    all_picked = groups * capacity
    flops = 2 * seq_len * width * (width + 6 * act_cols // 2) + 2 * all_picked * width * (
        6 * ehidden + 4 * rows_dev
    )
    return pl.pallas_call(
        functools.partial(branch_kernel, experts=experts, groups=groups, capacity=capacity),
        out_shape=(
            result(seq_len, width),
            result(seq_len, width + 128),
            result(seq_len, width),
            result(seq_len, hidden),
            result(seq_len, act_cols),
            result(all_picked, width),
            result(all_picked, ehidden),
            result(all_picked, ehidden),
            result(all_picked, ehidden),
            result(all_picked, width),
        ),
        grid_spec=pltpu.PrefetchScalarGridSpec(
            num_scalar_prefetch=1,
            grid=(groups // blocks,),
            in_specs=[
                pl.BlockSpec((width, rows), lambda i, _: (0, i)),
                step_rows(rows, width),
                step_rows(rows, width),
                pl.BlockSpec((blocks, 1, rows_dev), lambda i, _: (i, 0, 0)),
                packed_part(width, 0),
                packed_part(hidden, width),
                packed_part(hidden, width + hidden),
                packed_part(128, width + act_cols),
                whole(down.shape),
                whole(egate.shape),
                whole(eup.shape),
                whole(edown.shape),
            ],
            out_specs=(
                step_rows(rows, width),
                step_rows(rows, width + 128),
                step_rows(rows, width),
                step_rows(rows, hidden),
                step_rows(rows, act_cols),
                step_rows(picked, width),
                step_rows(picked, ehidden),
                step_rows(picked, ehidden),
                step_rows(picked, ehidden),
                step_rows(picked, width),
            ),
        ),
        compiler_params=pltpu.CompilerParams(vmem_limit_bytes=56 << 20),
        cost_estimate=pl.CostEstimate(
            flops=flops, bytes_accessed=40 << 20, transcendentals=2 * all_picked * ehidden
        ),
        name="branches",
    )(info, mixed, tokens, cotangent, rank, packed, packed, packed, packed, down, egate, eup, edown)


def own_rows_kernel(
    info_ref,
    grad_ref,
    mixed_ref,
    tokens_ref,
    cotangent_ref,
    out_w_ref,
    small_ref,
    *refs,
    experts,
    groups,
    window_starts,
):
    hidden_ref, grad_hidden_ref, grad_mixed_ref, normed_ref, logits_ref, back_ref, mark_ref = refs[
        -8:-1
    ]
    mark_ref[...] = jnp.zeros_like(mark_ref)
    rows, width = tokens_ref.shape
    length, me = (info_ref[0], info_ref[1])
    small = small_ref[...].astype(F32)
    gain = small.T[experts : experts + 1]
    hidden = tokens_ref[...].astype(F32) + matmul_tn(mixed_ref[...], out_w_ref[...])
    scale = inv_rms(hidden)
    unit = hidden * scale
    normed = (unit * gain).astype(BF16)
    lane = lax.broadcasted_iota(jnp.int32, (rows, 128), 1)
    is_expert = lane < experts
    logits = jnp.where(is_expert, matmul(normed, small.astype(BF16)), NEG_FILL)
    weights = jnp.exp(logits - jnp.max(logits, axis=1, keepdims=True))
    probs = weights / jnp.sum(weights, axis=1, keepdims=True)
    dots = grad_ref[:, width:].astype(F32)
    grad_probs = jnp.zeros((rows, 128), F32)
    for expert in range(experts):
        source = lane % groups // 2
        part = jnp.where((lane < 2 * groups) & (source == expert), dots, 0.0)
        grad_probs = jnp.where(
            lane == expert, jnp.sum(part, axis=1, keepdims=True), grad_probs
        )
    mean = jnp.sum(probs * grad_probs, axis=1, keepdims=True)
    grad_logits = jnp.where(is_expert, probs * (grad_probs - mean), 0.0).astype(BF16)
    router = jnp.where(
        lax.broadcasted_iota(jnp.int32, small.shape, 1) < experts, small, 0.0
    ).astype(BF16)
    grad_normed = grad_ref[:, :width].astype(F32) + matmul_nt(grad_logits, router)
    position = me * rows + lax.broadcasted_iota(jnp.int32, (rows, 1), 0)
    live = (position < length).astype(F32)
    grad_hidden = cotangent_ref[...].astype(F32) * live + rms_back(
        hidden, scale, grad_normed * gain
    )
    hidden_ref[...] = hidden * live
    grad_hidden_ref[...] = grad_hidden
    grad_mixed = matmul_nt(out_w_ref[...], grad_hidden.astype(BF16)).astype(BF16)
    for dest, at in enumerate(window_starts):
        grad_mixed_ref[dest] = grad_mixed[at : at + grad_mixed_ref.shape[1]]
    normed_ref[...] = normed
    logits_ref[...] = jnp.where(lane == experts, jnp.ones((), BF16), grad_logits)
    back_ref[...] = (grad_normed * unit).astype(BF16)


def own_rows(
    info, grad_own, mixed, tokens, cotangent, packed, branch, earlier, experts, groups,
    window, window_starts,
):
    rows, width = tokens.shape
    small_at = packed.shape[1] // 128 - 1

    def whole(shape):
        return pl.BlockSpec(shape, lambda i, _: (0,) * len(shape))

    anywhere = pl.BlockSpec(memory_space=pl.ANY)
    shapes = (
        ((rows, width), F32),
        ((rows, width), F32),
        ((groups, window, rows), BF16),
        ((rows, width), BF16),
        ((rows, 128), BF16),
        ((rows, width), BF16),
        (MARK, F32),
    )
    return pl.pallas_call(
        functools.partial(
            own_rows_kernel, experts=experts, groups=groups, window_starts=tuple(window_starts)
        ),
        out_shape=(
            *(jax.ShapeDtypeStruct(shape, dtype) for shape, dtype in shapes),
            jax.ShapeDtypeStruct(branch.shape, branch.dtype),
        ),
        grid_spec=pltpu.PrefetchScalarGridSpec(
            num_scalar_prefetch=1,
            grid=(1,),
            in_specs=[
                whole(grad_own.shape),
                pl.BlockSpec((width, rows), lambda i, info: (0, info[1])),
                whole(tokens.shape),
                whole(cotangent.shape),
                whole((width, width)),
                pl.BlockSpec((width, 128), lambda i, _: (0, small_at)),
                anywhere,
            ]
            + [anywhere] * len(earlier),
            out_specs=(*(whole(shape) for shape, _ in shapes), anywhere),
        ),
        input_output_aliases={7: len(shapes)},
        compiler_params=pltpu.CompilerParams(vmem_limit_bytes=40 << 20),
        cost_estimate=pl.CostEstimate(
            flops=6 * rows * width * width, bytes_accessed=6 << 20, transcendentals=rows * 128
        ),
        name="own_rows",
    )(info, grad_own, mixed, tokens, cotangent, packed, packed, branch, *earlier)


def gather_rows(values):
    return lax.all_gather(values, "fsdp", axis=0, tiled=True)


def exchange(chunks):
    return lax.all_to_all(chunks, "fsdp", split_axis=0, concat_axis=0, tiled=True)


def scatter_sum(values):
    return lax.psum_scatter(values, "fsdp", scatter_dimension=0, tiled=True)


def after(values, mark):
    mark = mark[(slice(0, 1),) * mark.ndim].reshape(()).astype(F32)
    return jnp.where(mark < jnp.inf, values, jnp.zeros((), values.dtype))


def swap_rep(values, bit):
    count = lax.axis_size("rep")
    return lax.ppermute(values, "rep", [(i, i ^ (1 << bit)) for i in range(count)])


def rep_bits():
    count = lax.axis_size("rep")
    bits = count.bit_length() - 1
    assert count == 1 << bits
    return range(bits)


def rep_scatter_sum(values, axis, bits=None, marks=()):
    index = lax.axis_index("rep")
    for step, bit in enumerate(rep_bits() if bits is None else bits):
        half = values.shape[axis] // 2
        mine = (index >> bit) & 1
        keep = lax.dynamic_slice_in_dim(values, mine * half, half, axis)
        send = lax.dynamic_slice_in_dim(values, (1 - mine) * half, half, axis)
        if step < len(marks):
            keep = after(keep, marks[step])
        values = (keep.astype(F32) + swap_rep(send, bit).astype(F32)).astype(values.dtype)
    return values


def rep_join(values, axis, bits=None):
    index = lax.axis_index("rep")
    for bit in reversed(rep_bits() if bits is None else bits):
        other = swap_rep(values, bit)
        mine = (index >> bit) & 1
        values = jnp.where(
            mine == 0,
            jnp.concatenate([values, other], axis=axis),
            jnp.concatenate([other, values], axis=axis),
        )
    return values


def on_device(
    tokens,
    cotangent,
    lengths,
    routes,
    gain_attn,
    gain_ffn,
    w_query,
    w_key,
    w_value,
    w_out,
    w_router,
    shared_gate,
    shared_up,
    shared_down,
    expert_gate,
    expert_up,
    expert_down,
):
    rows_dev, width = tokens.shape[1:]
    groups = lax.axis_size("fsdp")
    reps = lax.axis_size("rep")
    me = lax.axis_index("fsdp")
    seq_len = groups * rows_dev
    experts = w_router.shape[1]
    capacity = min(rows_dev, 5 * rows_dev // (2 * experts))
    length = lengths[0]
    my_rows = me * rows_dev
    live_all = jnp.arange(seq_len, dtype=jnp.int32) < length
    live_col = lax.dynamic_slice_in_dim(live_all, my_rows, rows_dev, 0).astype(F32)[:, None]

    cols_dev = width // groups
    first_heads = [d * cols_dev // HEAD_DIM for d in range(groups)]
    span = max(-(-(d + 1) * cols_dev // HEAD_DIM) - first_heads[d] for d in range(groups))
    first_heads = [min(head, HEADS - span) for head in first_heads]
    window = span * HEAD_DIM
    window_starts = [head * HEAD_DIM for head in first_heads]
    offsets = [d * cols_dev - window_starts[d] for d in range(groups)]
    my_offset = jnp.asarray(offsets, jnp.int32)[me]

    tokens_all = gather_rows(tokens[0])
    rep_rows = cols_dev // reps
    rep_at = lax.axis_index("rep") * rep_rows

    def rep_part(weight):
        return lax.dynamic_slice_in_dim(weight, rep_at, rep_rows, 0)

    gain_part = rep_part(gain_attn).astype(F32)[:, None]
    qkv_rows = [
        (rep_part(weight).astype(F32) * gain_part).astype(BF16)
        for weight in (w_query, w_key, w_value)
    ]
    qkv_chunks = jnp.stack(
        [
            jnp.concatenate([weight[:, at : at + window] for weight in qkv_rows], axis=1)
            for at in window_starts
        ]
    )
    qkv_part = exchange(qkv_chunks)
    qkv_cols = lax.all_gather(qkv_part, "rep", axis=0)
    qkv_cols = qkv_cols.transpose(1, 0, 2, 3).reshape(width, 3 * window)
    cosine, sine = rope_tables(seq_len)

    cotangent_all = gather_rows(after(cotangent[0], qkv_cols))
    shared_cols_dev = shared_gate.shape[1] // groups
    gate_chunks, up_chunks = [
        rep_part(weight).reshape(rep_rows, groups, shared_cols_dev).transpose(1, 0, 2)
        for weight in (shared_gate, shared_up)
    ]
    route_cols = -(-2 * rows_dev // rep_rows)
    route_chunk = jnp.pad(
        routes[0].astype(BF16).reshape(-1), (0, route_cols * rep_rows - 2 * rows_dev)
    ).reshape(rep_rows, route_cols)
    small_cols = experts + 1 + route_cols
    small = jnp.concatenate(
        [
            rep_part(w_router),
            rep_part(gain_ffn)[:, None],
            route_chunk,
            jnp.zeros((rep_rows, -small_cols % 128), BF16),
        ],
        axis=1,
    )
    packed_part = exchange(
        after(
            jnp.concatenate(
                [
                    jnp.broadcast_to(rep_part(w_out), (groups, rep_rows, width)),
                    gate_chunks,
                    up_chunks,
                    jnp.broadcast_to(small, (groups, *small.shape)),
                ],
                axis=2,
            ),
            qkv_cols,
        )
    )
    small_at = width + 2 * shared_cols_dev
    routes_all = (
        packed_part[:, :, small_at + experts + 1 : small_at + small_cols]
        .reshape(groups, rep_rows * route_cols)[:, : 2 * rows_dev]
        .reshape(groups, rows_dev, 2)
        .astype(jnp.int32)
    )
    packed_all = lax.psum(
        lax.dynamic_update_slice_in_dim(
            jnp.zeros((groups, cols_dev, small_at + 128), BF16),
            packed_part[:, :, : small_at + 128],
            rep_at,
            1,
        ),
        "rep",
    ).reshape(width, -1)
    routed = jnp.any(routes_all == me // 2, axis=2) & live_all.reshape(groups, rows_dev)
    rank = jnp.cumsum(routed.astype(jnp.int32), axis=1) - 1
    rank = jnp.where(routed, rank, -1)[:, None, :]

    inputs_all = tokens_all.astype(F32)
    unit = (inputs_all * inv_rms(inputs_all)).astype(BF16)
    qkv = contract(qkv_cols, unit, 0, 1)
    queries = (rotate_cols(qkv[:window], cosine, sine).astype(BF16).astype(F32) * 0.125).astype(
        BF16
    )
    keys = rotate_cols(qkv[window : 2 * window], cosine, sine).astype(BF16)
    values = qkv[2 * window :].astype(BF16)
    mixed_heads, log_norm = attn_forward(lengths, queries, keys, values)
    mixed_own = lax.dynamic_slice_in_dim(mixed_heads, my_offset, cols_dev, 0).astype(BF16)
    mixed_own = after(mixed_own, cotangent_all)
    mixed_all = gather_rows(mixed_own)

    info = jnp.stack([length, me, jnp.zeros((), jnp.int32)])
    (
        branch_part,
        grad_part,
        normed,
        shared_inner,
        shared_act_grad,
        rows_in,
        expert_inner,
        expert_gate_grad,
        expert_up_grad,
        grad_half,
    ) = run_branches(
        info,
        mixed_all,
        tokens_all,
        cotangent_all,
        rank,
        packed_all,
        shared_down,
        expert_gate,
        expert_up,
        expert_down,
        experts,
        capacity,
    )
    grad_own = scatter_sum(grad_part)

    expert_grads = jnp.concatenate(
        [
            matmul_tn(rows_in, expert_gate_grad).astype(BF16),
            matmul_tn(rows_in, expert_up_grad).astype(BF16),
            matmul_tn(grad_half, expert_inner).astype(BF16),
        ],
        axis=0,
    )
    grad_down = matmul_tn(shared_inner, cotangent_all).astype(BF16)
    grad_gate_up = matmul_tn(normed, shared_act_grad).astype(BF16)

    hidden, grad_hidden, grad_mixed, normed_own, logits_own, back_own, mark_own, branch_part = (
        own_rows(
            info,
            grad_own,
            mixed_all,
            tokens[0],
            cotangent[0],
            packed_all,
            branch_part,
            (expert_grads, grad_down, grad_gate_up),
            experts,
            groups,
            window,
            window_starts,
        )
    )
    grad_mixed_cols = exchange(grad_mixed)
    branch_own = scatter_sum(branch_part).astype(F32)
    orders = (list(rep_bits()), list(rep_bits())[::-1])
    half_rows = expert_grads.shape[0] // 2
    expert_parts = [
        rep_scatter_sum(expert_grads[at : at + half_rows], 0, order, (mark_own,))
        for at, order in zip((0, half_rows), orders)
    ]
    packed_grad = jnp.concatenate(
        [
            matmul(
                lax.dynamic_slice_in_dim(mixed_all, my_rows, rows_dev, 1),
                grad_hidden.astype(BF16),
            ),
            matmul_tn(normed_own, logits_own[:, :experts]),
            matmul_tn(back_own, logits_own[:, experts : experts + 1]),
        ],
        axis=1,
    ).astype(BF16)

    grad_q, grad_k, grad_v, mark_attn = attn_backward(
        lengths,
        queries,
        keys,
        values,
        mixed_heads,
        log_norm,
        grad_mixed_cols,
        tuple(expert_parts),
    )
    grad_down = rep_scatter_sum(grad_down, 0, orders[1], (mark_attn,))
    grad_gate_up = rep_scatter_sum(
        grad_gate_up.reshape(groups, cols_dev, -1), 1, orders[1], (mark_attn,)
    )
    gate_up_back = exchange(grad_gate_up)
    gate_up_part = jnp.concatenate(
        [
            gate_up_back[:, :, at : at + shared_cols_dev]
            .transpose(1, 0, 2)
            .reshape(rep_rows, -1)
            for at in (0, shared_cols_dev)
        ],
        axis=1,
    )
    packed_part = rep_scatter_sum(
        packed_grad.reshape(groups, cols_dev, -1), 1, orders[0], (mark_attn,)
    )
    packed_part = jnp.sum(exchange(packed_part).astype(F32), axis=0).astype(BF16)
    channel = jnp.arange(window, dtype=jnp.int32)[:, None]
    owned = (channel >= my_offset) & (channel < my_offset + cols_dev)
    qkv_grad = jnp.concatenate(
        [
            jnp.where(owned, rotate_cols(grad_q * 0.125, cosine, -sine), 0.0),
            jnp.where(owned, rotate_cols(grad_k, cosine, -sine), 0.0),
            jnp.where(owned, grad_v, 0.0),
        ],
        axis=0,
    ).astype(BF16)
    grad_unit = scatter_sum(contract(qkv_grad, qkv_cols, 0, 1).astype(BF16)).astype(F32)
    expert_sum = jnp.concatenate(
        [rep_join(part, 0, order) for part, order in zip(expert_parts, orders)], axis=0
    )
    expert_sum = expert_sum.astype(F32)
    sum_egate, sum_eup, sum_edown = (
        expert_sum[:width],
        expert_sum[width : 2 * width],
        expert_sum[2 * width :].T,
    )
    sum_down = rep_join(grad_down, 0, orders[1]).astype(F32)
    inputs = tokens[0].astype(F32)
    output = (hidden + live_col * branch_own).astype(BF16)
    input_grad = grad_hidden + rms_back(inputs, inv_rms(inputs), grad_unit)

    qkv_weight_grad = contract(unit, qkv_grad, 0, 1).astype(BF16)
    qkv_part = rep_scatter_sum(qkv_weight_grad.reshape(groups, cols_dev, 3 * window), 1)
    qkv_back = exchange(qkv_part)
    qkv_part = jnp.concatenate(
        [
            qkv_back[d, :, part * window + offsets[d] : part * window + offsets[d] + cols_dev]
            for part in range(3)
            for d in range(groups)
        ],
        axis=1,
    )
    sum_qkv = rep_join(qkv_part, 0).astype(F32)
    sum_gate_up = rep_join(gate_up_part, 0, orders[1]).astype(F32)
    sum_packed = rep_join(packed_part, 0).astype(F32)

    sum_gain_attn = sum(
        jnp.sum(sum_qkv[:, part * width : (part + 1) * width] * weight.astype(F32), axis=1)
        for part, weight in enumerate((w_query, w_key, w_value))
    )
    sum_weights = sum_qkv * gain_attn.astype(F32)[:, None]
    half = sum_gate_up.shape[1] // 2
    return (
        output[None],
        input_grad[None],
        sum_gain_attn,
        sum_packed[:, width + experts],
        sum_weights[:, :width],
        sum_weights[:, width : 2 * width],
        sum_weights[:, 2 * width :],
        sum_packed[:, :width],
        sum_packed[:, width : width + experts],
        sum_gate_up[:, :half],
        sum_gate_up[:, half:],
        sum_down,
        sum_egate,
        sum_eup,
        sum_edown,
    )


def solution(mesh):
    in_specs = (
        P("rep", "fsdp", None),
        P("rep", "fsdp", None),
        P("rep"),
        P("rep", "fsdp", None),
        P("fsdp"),
        P("fsdp"),
        P("fsdp", None),
        P("fsdp", None),
        P("fsdp", None),
        P("fsdp", None),
        P("fsdp", None),
        P("fsdp", None),
        P("fsdp", None),
        P("fsdp", None),
        P(None, "fsdp"),
        P(None, "fsdp"),
        P("fsdp", None),
    )
    out_specs = (
        P("rep", "fsdp", None),
        P("rep", "fsdp", None),
        P("fsdp"),
        P("fsdp"),
        P("fsdp", None),
        P("fsdp", None),
        P("fsdp", None),
        P("fsdp", None),
        P("fsdp", None),
        P("fsdp", None),
        P("fsdp", None),
        P("fsdp", None),
        P(None, "fsdp"),
        P(None, "fsdp"),
        P("fsdp", None),
    )
    return jax.shard_map(
        on_device, mesh=mesh, in_specs=in_specs, out_specs=out_specs, check_vma=False
    )
```

```python
import functools

import jax
import jax.numpy as jnp
from jax import lax
from jax.experimental import pallas as pl
from jax.experimental.pallas import tpu as pltpu
from jax.sharding import PartitionSpec as P

HEADS = 12
HEAD_DIM = 64

EPSILON = 1e-06
ROPE_BASE = 10000.0
NEG_FILL = -1e30
MARK = (8, 128)
ALL_VMEM = 60 << 20
IN_HBM = pl.BlockSpec(memory_space=pltpu.HBM)
F32 = jnp.float32
BF16 = jnp.bfloat16


def contract(first_op, second_op, first_dim, second_dim):
    return lax.dot_general(
        first_op,
        second_op,
        (((first_dim,), (second_dim,)), ((), ())),
        preferred_element_type=F32,
    )


def matmul(first_op, second_op):
    return contract(first_op, second_op, 1, 0)


def matmul_tn(first_op, second_op):
    return contract(first_op, second_op, 0, 0)


def matmul_nt(first_op, second_op):
    return contract(first_op, second_op, 1, 1)


def inv_rms(values):
    return lax.rsqrt(jnp.mean(values * values, axis=-1, keepdims=True) + EPSILON)


def rms_back(values, scale, grad_scaled):
    return scale * grad_scaled - values * (
        scale * scale * scale * jnp.mean(grad_scaled * values, axis=-1, keepdims=True)
    )


def swiglu(gate_act, up_act):
    return (jax.nn.silu(gate_act) * up_act).astype(BF16)


def swiglu_grad(grad_inner, gate_act, up_act):
    grad_inner = grad_inner.astype(F32)
    sig = jax.nn.sigmoid(gate_act)
    grad_gate = grad_inner * up_act * (sig * (1.0 + gate_act * (1.0 - sig)))
    grad_up = grad_inner * (gate_act * sig)
    return (grad_gate.astype(BF16), grad_up.astype(BF16))


def rope_tables(seq_len):
    half_dim = HEAD_DIM // 2
    frequency = ROPE_BASE ** (-jnp.arange(half_dim, dtype=F32) / half_dim)
    angles = frequency[:, None] * jnp.arange(seq_len, dtype=F32)[None, :]
    return (jnp.cos(angles), jnp.sin(angles))


def rotate_cols(values, cosine, sine):
    rows, seq_len = values.shape
    split = values.reshape(rows // HEAD_DIM, 2, HEAD_DIM // 2, seq_len)
    first, second = (split[:, 0], split[:, 1])
    turned = jnp.stack(
        [first * cosine - second * sine, second * cosine + first * sine], axis=1
    )
    return turned.reshape(rows, seq_len)


def put_halves(values, mine, keep_ref, send_ref, at=0):
    groups, rows, _ = keep_ref.shape
    cols = slice(at, at + values.shape[1])
    for dest in range(groups):
        first = values[2 * dest * rows : (2 * dest + 1) * rows]
        last = values[(2 * dest + 1) * rows : (2 * dest + 2) * rows]
        keep_ref[dest, :, cols] = jnp.where(mine == 0, first, last).astype(BF16)
        send_ref[dest, :, cols] = jnp.where(mine == 0, last, first).astype(BF16)


def attn_forward_kernel(len_ref, q_ref, k_ref, v_ref, o_ref, l_ref, *, heads, blk):
    row = pl.program_id(0)
    length = len_ref[0]
    queries = q_ref[...]

    def step(masked, col, state):
        cols = pl.ds(pl.multiple_of(col * blk, blk), blk)
        keys, values = (k_ref[:, cols], v_ref[:, cols])
        if masked:
            key_pos = col * blk + lax.broadcasted_iota(jnp.int32, (blk, blk), 0)
            query_pos = row * blk + lax.broadcasted_iota(jnp.int32, (blk, blk), 1)
            allowed = (key_pos <= query_pos) & (key_pos < length)
        result = []
        for head in range(heads):
            top, total, acc = state[head]
            part = slice(head * HEAD_DIM, (head + 1) * HEAD_DIM)
            scores = matmul_tn(keys[part], queries[part])
            if masked:
                scores = jnp.where(allowed, scores, NEG_FILL)
            new_top = jnp.maximum(top, jnp.max(scores, axis=0, keepdims=True))
            probs = jnp.exp(scores - new_top)
            shrink = jnp.exp(top - new_top)
            total = total * shrink + jnp.sum(probs, axis=0, keepdims=True)
            acc = acc * shrink + matmul(values[part], probs.astype(BF16))
            result.append((new_top, total, acc))
        return tuple(result)

    start = tuple(
        (
            jnp.full((1, blk), NEG_FILL, F32),
            jnp.zeros((1, blk), F32),
            jnp.zeros((HEAD_DIM, blk), F32),
        )
        for _ in range(heads)
    )
    whole = jnp.minimum(row, length // blk)
    end = jnp.minimum(row + 1, (length + blk - 1) // blk)
    state = lax.fori_loop(0, whole, functools.partial(step, False), start)
    state = lax.fori_loop(whole, end, functools.partial(step, True), state)
    for head in range(heads):
        top, total, acc = state[head]
        o_ref[head * HEAD_DIM : (head + 1) * HEAD_DIM, :] = acc * (1.0 / total)
        l_ref[head : head + 1, :] = top + jnp.log(total)


def attn_backward_kernel(
    len_ref, q_ref, k_ref, v_ref, o_ref, l_ref, do_ref, *refs, heads, blk
):
    dq_ref, dk_ref, dv_ref, mark_ref = refs[-4:]
    mark_ref[...] = jnp.zeros_like(mark_ref)
    row = pl.program_id(0)
    length = len_ref[0]

    @pl.when(row == 0)
    def _():
        dk_ref[...] = jnp.zeros_like(dk_ref)
        dv_ref[...] = jnp.zeros_like(dv_ref)

    parts = [slice(head * HEAD_DIM, (head + 1) * HEAD_DIM) for head in range(heads)]
    queries = q_ref[...]
    grad_out = jnp.concatenate([do_ref[src] for src in range(do_ref.shape[0])], axis=1)
    deltas = [
        jnp.sum(grad_out[part].astype(F32) * o_ref[part, :], axis=0, keepdims=True)
        for part in parts
    ]
    log_norms = [l_ref[head : head + 1, :] for head in range(heads)]

    def step(masked, col, state):
        cols = pl.ds(pl.multiple_of(col * blk, blk), blk)
        keys, values = (k_ref[:, cols], v_ref[:, cols])
        if masked:
            key_pos = col * blk + lax.broadcasted_iota(jnp.int32, (blk, blk), 0)
            query_pos = row * blk + lax.broadcasted_iota(jnp.int32, (blk, blk), 1)
            allowed = (key_pos <= query_pos) & (key_pos < length)
        result = []
        for head, part in enumerate(parts):
            scores = matmul_tn(keys[part], queries[part])
            grad_probs = matmul_tn(values[part], grad_out[part])
            probs = jnp.exp(scores - log_norms[head])
            if masked:
                probs = jnp.where(allowed, probs, 0.0)
            grad_scores = (probs * (grad_probs - deltas[head])).astype(BF16)
            dv_ref[part, cols] += matmul_nt(grad_out[part], probs.astype(BF16))
            dk_ref[part, cols] += matmul_nt(queries[part], grad_scores)
            result.append(state[head] + matmul(keys[part], grad_scores))
        return tuple(result)

    start = tuple(jnp.zeros((HEAD_DIM, blk), F32) for _ in range(heads))
    whole = jnp.minimum(row, length // blk)
    end = jnp.minimum(row + 1, (length + blk - 1) // blk)
    state = lax.fori_loop(0, whole, functools.partial(step, False), start)
    state = lax.fori_loop(whole, end, functools.partial(step, True), state)
    for head, part in enumerate(parts):
        dq_ref[part, :] = state[head]


def attn_specs(rows, seq_len, heads, blk):
    block = pl.BlockSpec((rows, blk), lambda i, _: (0, i))
    whole = pl.BlockSpec((rows, seq_len), lambda i, _: (0, 0))
    stats = pl.BlockSpec((heads, blk), lambda i, _: (0, i))
    return (block, whole, stats)


def attn_cost(rows, seq_len, heads, products):
    pairs = heads * seq_len * seq_len // 2
    return pl.CostEstimate(
        flops=2 * products * pairs * 256, bytes_accessed=16 * rows * seq_len, transcendentals=pairs
    )


def attn_forward(length, queries, keys, values):
    rows, seq_len = queries.shape
    heads, blk = (rows // HEAD_DIM, min(512, seq_len))
    block, whole, stats = attn_specs(rows, seq_len, heads, blk)
    return pl.pallas_call(
        functools.partial(attn_forward_kernel, heads=heads, blk=blk),
        out_shape=(
            jax.ShapeDtypeStruct((rows, seq_len), F32),
            jax.ShapeDtypeStruct((heads, seq_len), F32),
        ),
        grid_spec=pltpu.PrefetchScalarGridSpec(
            num_scalar_prefetch=1,
            grid=(seq_len // blk,),
            in_specs=[block, whole, whole],
            out_specs=(block, stats),
        ),
        compiler_params=pltpu.CompilerParams(vmem_limit_bytes=40 << 20),
        cost_estimate=attn_cost(rows, seq_len, heads, 2),
        name="attn_forward",
    )(length, queries, keys, values)


def attn_backward(length, queries, keys, values, mixed, log_norm, grad_mixed, earlier):
    rows, seq_len = queries.shape
    heads, blk = (rows // HEAD_DIM, min(512, seq_len))
    block, whole, stats = attn_specs(rows, seq_len, heads, blk)
    rows_dev = grad_mixed.shape[2]
    sources = pl.BlockSpec((blk // rows_dev, rows, rows_dev), lambda i, _: (i, 0, 0))
    return pl.pallas_call(
        functools.partial(attn_backward_kernel, heads=heads, blk=blk),
        out_shape=(
            *(jax.ShapeDtypeStruct((rows, seq_len), F32),) * 3,
            jax.ShapeDtypeStruct(MARK, F32),
        ),
        grid_spec=pltpu.PrefetchScalarGridSpec(
            num_scalar_prefetch=1,
            grid=(seq_len // blk,),
            in_specs=[block, whole, whole, block, stats, sources]
            + [IN_HBM] * len(earlier),
            out_specs=(block, whole, whole, pl.BlockSpec(MARK, lambda i, _: (0, 0))),
        ),
        compiler_params=pltpu.CompilerParams(vmem_limit_bytes=ALL_VMEM),
        cost_estimate=pl.CostEstimate(flops=0, bytes_accessed=0, transcendentals=0),
        name="attn_backward",
    )(length, queries, keys, values, mixed, log_norm, grad_mixed, *earlier)


def projections_kernel(
    info_ref, dq_ref, dk_ref, dv_ref, cos_ref, sin_ref, unit_ref, w_ref, *refs, cols_dev
):
    grad_ref, keep_ref, send_ref, total_ref = refs[-4:]
    rows = dq_ref.shape[0]
    cosine, sine = (cos_ref[...], sin_ref[...])
    channel = lax.broadcasted_iota(jnp.int32, (rows, 1), 0)
    owned = ((channel >= info_ref[3]) & (channel < info_ref[3] + cols_dev)).astype(F32)

    def turn_back(values):
        parts = []
        for at in range(0, rows, HEAD_DIM):
            first = values[at : at + HEAD_DIM // 2]
            second = values[at + HEAD_DIM // 2 : at + HEAD_DIM]
            parts += [first * cosine + second * sine, second * cosine - first * sine]
        return jnp.concatenate(parts, axis=0)

    grads = jnp.concatenate(
        [
            (owned * turn_back(dq_ref[...] * 0.125)).astype(BF16),
            (owned * turn_back(dk_ref[...])).astype(BF16),
            (owned * dv_ref[...]).astype(BF16),
        ],
        axis=0,
    )
    grad_ref[...] = contract(grads, w_ref[...], 0, 1).astype(BF16)
    part = matmul(grads, unit_ref[...])

    @pl.when(pl.program_id(0) == 0)
    def _():
        total_ref[...] = part

    @pl.when(pl.program_id(0) > 0)
    def _():
        total_ref[...] += part

    @pl.when(pl.program_id(0) == pl.num_programs(0) - 1)
    def _():
        put_halves(total_ref[...].T, info_ref[4], keep_ref, send_ref)


def projections_backward(
    info, grad_q, grad_k, grad_v, cosine, sine, unit, weight, cols_dev, earlier
):
    rows, seq_len = grad_q.shape
    width = unit.shape[1]
    blk = min(512, seq_len)

    def part(count):
        return pl.BlockSpec((count, blk), lambda i, _: (0, i))

    by_row = pl.BlockSpec((blk, width), lambda i, _: (i, 0))
    whole = pl.BlockSpec(weight.shape, lambda i, _: (0, 0))
    half_shape = (width // cols_dev, cols_dev // 2, 3 * rows)
    return pl.pallas_call(
        functools.partial(projections_kernel, cols_dev=cols_dev),
        out_shape=(
            pltpu.HBM((seq_len, width), BF16),
            *(jax.ShapeDtypeStruct(half_shape, BF16),) * 2,
        ),
        grid_spec=pltpu.PrefetchScalarGridSpec(
            num_scalar_prefetch=1,
            grid=(seq_len // blk,),
            in_specs=[part(rows)] * 3
            + [part(HEAD_DIM // 2)] * 2
            + [by_row, whole]
            + [IN_HBM] * len(earlier),
            out_specs=(by_row, *(pl.BlockSpec(half_shape, lambda i, _: (0, 0, 0)),) * 2),
            scratch_shapes=[pltpu.VMEM((3 * rows, width), F32)],
        ),
        compiler_params=pltpu.CompilerParams(vmem_limit_bytes=40 << 20),
        cost_estimate=pl.CostEstimate(flops=0, bytes_accessed=0, transcendentals=0),
        name="projections_backward",
    )(info, grad_q, grad_k, grad_v, cosine, sine, unit, weight, *earlier)


def branch_kernel(
    info_ref,
    mixed_ref,
    tokens_ref,
    cotangent_ref,
    rank_ref,
    out_w_ref,
    gate_ref,
    up_ref,
    small_ref,
    down_ref,
    egate_ref,
    eup_ref,
    edown_ref,
    branch_ref,
    grad_ref,
    normed_ref,
    inner_ref,
    act_grad_ref,
    rows_ref,
    einner_ref,
    egate_grad_ref,
    eup_grad_ref,
    half_grad_ref,
    *,
    experts,
    groups,
    capacity,
):
    rows = tokens_ref.shape[0]
    blocks, _, rows_dev = rank_ref.shape
    length, me = (info_ref[0], info_ref[1])
    first_pos = info_ref[2] + pl.program_id(0) * rows

    hidden = tokens_ref[...].astype(F32) + matmul_tn(mixed_ref[...], out_w_ref[...])
    small = small_ref[...].astype(F32).T
    gain = small[experts : experts + 1]
    normed = (hidden * inv_rms(hidden) * gain).astype(BF16)
    normed_ref[...] = normed
    logits = matmul_nt(small[:16].astype(BF16), normed)
    expert_row = lax.broadcasted_iota(jnp.int32, logits.shape, 0)
    logits = jnp.where(expert_row < experts, logits, NEG_FILL)
    weights = jnp.exp(logits - jnp.max(logits, axis=0, keepdims=True))
    probs = weights / jnp.sum(weights, axis=0, keepdims=True)
    prob_row = jnp.sum(jnp.where(expert_row == me // 2, probs, 0.0), axis=0, keepdims=True)

    position = first_pos + lax.broadcasted_iota(jnp.int32, (rows, 1), 0)
    live = (position < length).astype(F32)
    grad_out = (cotangent_ref[...].astype(F32) * live).astype(BF16)

    gate_act, up_act = (matmul(normed, gate_ref[...]), matmul(normed, up_ref[...]))
    inner = swiglu(gate_act, up_act)
    inner_ref[...] = (inner.astype(F32) * live).astype(BF16)
    branch = matmul(inner, down_ref[...])
    gate_grad, up_grad = swiglu_grad(
        matmul_nt(grad_out, down_ref[...]).astype(BF16), gate_act, up_act
    )
    act_grad = jnp.concatenate([gate_grad, up_grad], axis=1)
    act_grad_ref[...] = act_grad
    grad = matmul_nt(gate_grad, gate_ref[...]) + matmul_nt(up_grad, up_ref[...])

    picks, picked, picked_grad, picked_prob = ([], [], [], [])
    slot = lax.broadcasted_iota(jnp.int32, (capacity, rows_dev), 0)
    for blk in range(blocks):
        part = slice(blk * rows_dev, (blk + 1) * rows_dev)
        hot = (slot == rank_ref[blk]).astype(F32)
        picked_prob.append(jnp.sum(hot * prob_row[:, part], axis=1, keepdims=True))
        pick = hot.astype(BF16)
        picks.append(pick)
        picked.append(matmul(pick, normed[part]).astype(BF16))
        picked_grad.append(matmul(pick, grad_out[part]).astype(BF16))
    rows_in = jnp.concatenate(picked, axis=0)
    grad_rows = jnp.concatenate(picked_grad, axis=0).astype(F32)
    row_prob = jnp.concatenate(picked_prob, axis=0)
    rows_ref[...] = rows_in
    egate_act = matmul(rows_in, egate_ref[...])
    eup_act = matmul(rows_in, eup_ref[...])
    einner = swiglu(egate_act, eup_act)
    einner_ref[...] = einner
    half = matmul(einner, edown_ref[...]).astype(BF16).astype(F32)
    dots = jnp.sum(grad_rows * half, axis=1, keepdims=True)
    half_grad = (row_prob * grad_rows).astype(BF16)
    half_grad_ref[...] = half_grad
    egate_grad, eup_grad = swiglu_grad(
        matmul_nt(half_grad, edown_ref[...]).astype(BF16), egate_act, eup_act
    )
    egate_grad_ref[...] = egate_grad
    eup_grad_ref[...] = eup_grad
    rows_grad = (
        matmul_nt(egate_grad, egate_ref[...]) + matmul_nt(eup_grad, eup_ref[...])
    ).astype(BF16)
    gated = (row_prob * half).astype(BF16)

    dots_high = dots.astype(BF16).astype(F32)
    lane = lax.broadcasted_iota(jnp.int32, (1, 128), 1)
    dots_cols = jnp.where(lane == me, dots_high, 0.0) + jnp.where(
        lane == me + groups, dots - dots_high, 0.0
    )
    dots_cols = dots_cols.astype(BF16)
    width = normed.shape[1]
    for blk in range(blocks):
        part = slice(blk * rows_dev, (blk + 1) * rows_dev)
        from_part = slice(blk * capacity, (blk + 1) * capacity)
        pick = picks[blk]
        branch_ref[part, :] = (branch[part] + matmul_tn(pick, gated[from_part])).astype(BF16)
        grad_ref[part, :width] = (grad[part] + matmul_tn(pick, rows_grad[from_part])).astype(BF16)
        grad_ref[part, width:] = matmul_tn(pick, dots_cols[from_part]).astype(BF16)


def run_branches(
    info, mixed, tokens, cotangent, rank, packed, down, egate, eup, edown, experts, capacity
):
    seq_len, width = tokens.shape
    groups, _, rows_dev = rank.shape
    blocks = 2 if groups % 2 == 0 else 1
    rows, picked = (blocks * rows_dev, blocks * capacity)
    hidden, ehidden = (down.shape[0], egate.shape[1])
    act_cols = 2 * hidden

    def step_rows(count, cols):
        return pl.BlockSpec((count, cols), lambda i, _: (i, 0))

    def whole(shape):
        return pl.BlockSpec(shape, lambda i, _: (0, 0), pipeline_mode=pl.Buffered(1))

    def packed_part(cols, at):
        return pl.BlockSpec(
            (width, cols), lambda i, _: (0, at // cols), pipeline_mode=pl.Buffered(1)
        )

    def result(count, cols):
        return jax.ShapeDtypeStruct((count, cols), BF16)

    all_picked = groups * capacity
    flops = 2 * seq_len * width * (width + 6 * act_cols // 2) + 2 * all_picked * width * (
        6 * ehidden + 4 * rows_dev
    )
    return pl.pallas_call(
        functools.partial(branch_kernel, experts=experts, groups=groups, capacity=capacity),
        out_shape=(
            result(seq_len, width),
            result(seq_len, width + 128),
            result(seq_len, width),
            result(seq_len, hidden),
            result(seq_len, act_cols),
            result(all_picked, width),
            result(all_picked, ehidden),
            result(all_picked, ehidden),
            result(all_picked, ehidden),
            result(all_picked, width),
        ),
        grid_spec=pltpu.PrefetchScalarGridSpec(
            num_scalar_prefetch=1,
            grid=(groups // blocks,),
            in_specs=[
                pl.BlockSpec((width, rows), lambda i, _: (0, i)),
                step_rows(rows, width),
                step_rows(rows, width),
                pl.BlockSpec((blocks, 1, rows_dev), lambda i, _: (i, 0, 0)),
                packed_part(width, 0),
                packed_part(hidden, width),
                packed_part(hidden, width + hidden),
                packed_part(128, width + act_cols),
                whole(down.shape),
                whole(egate.shape),
                whole(eup.shape),
                whole(edown.shape),
            ],
            out_specs=(
                step_rows(rows, width),
                step_rows(rows, width + 128),
                step_rows(rows, width),
                step_rows(rows, hidden),
                step_rows(rows, act_cols),
                step_rows(picked, width),
                step_rows(picked, ehidden),
                step_rows(picked, ehidden),
                step_rows(picked, ehidden),
                step_rows(picked, width),
            ),
        ),
        compiler_params=pltpu.CompilerParams(vmem_limit_bytes=ALL_VMEM),
        cost_estimate=pl.CostEstimate(
            flops=flops, bytes_accessed=40 << 20, transcendentals=2 * all_picked * ehidden
        ),
        name="branches",
    )(info, mixed, tokens, cotangent, rank, packed, packed, packed, packed, down, egate, eup, edown)


def own_rows_kernel(
    info_ref,
    grad_ref,
    mixed_ref,
    tokens_ref,
    cotangent_ref,
    out_w_ref,
    small_ref,
    shared_ref,
    *refs,
    experts,
    groups,
    window_starts,
):
    hidden_ref, grad_hidden_ref, grad_mixed_ref, *first_refs, last_keep_ref, last_send_ref = refs[
        -7:
    ]
    rows, width = tokens_ref.shape
    length, me = (info_ref[0], info_ref[1])
    small = small_ref[...].astype(F32)
    gain = small.T[experts : experts + 1]
    hidden = tokens_ref[...].astype(F32) + matmul_tn(mixed_ref[...], out_w_ref[...])
    scale = inv_rms(hidden)
    unit = hidden * scale
    normed = (unit * gain).astype(BF16)
    lane = lax.broadcasted_iota(jnp.int32, (rows, 128), 1)
    is_expert = lane < experts
    logits = jnp.where(is_expert, matmul(normed, small.astype(BF16)), NEG_FILL)
    weights = jnp.exp(logits - jnp.max(logits, axis=1, keepdims=True))
    probs = weights / jnp.sum(weights, axis=1, keepdims=True)
    dots = grad_ref[:, width:].astype(F32)
    grad_probs = jnp.zeros((rows, 128), F32)
    for expert in range(experts):
        source = lane % groups // 2
        part = jnp.where((lane < 2 * groups) & (source == expert), dots, 0.0)
        grad_probs = jnp.where(
            lane == expert, jnp.sum(part, axis=1, keepdims=True), grad_probs
        )
    mean = jnp.sum(probs * grad_probs, axis=1, keepdims=True)
    grad_logits = jnp.where(is_expert, probs * (grad_probs - mean), 0.0).astype(BF16)
    router = jnp.where(
        lax.broadcasted_iota(jnp.int32, small.shape, 1) < experts, small, 0.0
    ).astype(BF16)
    grad_normed = grad_ref[:, :width].astype(F32) + matmul_nt(grad_logits, router)
    position = me * rows + lax.broadcasted_iota(jnp.int32, (rows, 1), 0)
    live = (position < length).astype(F32)
    grad_hidden = cotangent_ref[...].astype(F32) * live + rms_back(
        hidden, scale, grad_normed * gain
    )
    hidden_ref[...] = hidden * live
    grad_hidden_ref[...] = grad_hidden
    grad_hidden_b = grad_hidden.astype(BF16)
    grad_mixed = matmul_nt(out_w_ref[...], grad_hidden_b).astype(BF16)
    for dest, at in enumerate(window_starts):
        grad_mixed_ref[dest] = grad_mixed[at : at + grad_mixed_ref.shape[1]]
    cut = first_refs[0].shape[2]
    grad_out_w = matmul(mixed_ref[...], grad_hidden_b)
    put_halves(grad_out_w[:, :cut], info_ref[4], *first_refs)
    ones = jnp.where(lane == experts, 1.0, 0.0).astype(BF16)
    small_grad = matmul_tn(normed, grad_logits) + matmul_tn((grad_normed * unit).astype(BF16), ones)
    last = jnp.concatenate([grad_out_w[:, cut:], small_grad, shared_ref[...].astype(F32)], axis=1)
    put_halves(last, info_ref[5], last_keep_ref, last_send_ref)


def own_rows(
    info, grad_own, mixed, tokens, cotangent, packed, grad_shared, earlier, experts, groups, window,
    window_starts,
):
    rows, width = tokens.shape
    small_at = packed.shape[1] // 128 - 1

    def whole(shape):
        return pl.BlockSpec(shape, lambda i, _: (0,) * len(shape))

    shapes = (
        ((rows, width), F32),
        ((rows, width), F32),
        ((groups, window, rows), BF16),
        *(((groups, width // groups // 2, width - 128), BF16),) * 2,
        *(((groups, width // groups // 2, 256 + grad_shared.shape[1]), BF16),) * 2,
    )
    return pl.pallas_call(
        functools.partial(
            own_rows_kernel, experts=experts, groups=groups, window_starts=tuple(window_starts)
        ),
        out_shape=tuple(jax.ShapeDtypeStruct(shape, dtype) for shape, dtype in shapes),
        grid_spec=pltpu.PrefetchScalarGridSpec(
            num_scalar_prefetch=1,
            grid=(1,),
            in_specs=[
                whole(grad_own.shape),
                whole(mixed.shape),
                whole(tokens.shape),
                whole(cotangent.shape),
                whole((width, width)),
                pl.BlockSpec((width, 128), lambda i, _: (0, small_at)),
                whole(grad_shared.shape),
            ]
            + [IN_HBM] * len(earlier),
            out_specs=tuple(whole(shape) for shape, _ in shapes),
        ),
        compiler_params=pltpu.CompilerParams(vmem_limit_bytes=ALL_VMEM),
        cost_estimate=pl.CostEstimate(
            flops=6 * rows * width * width, bytes_accessed=6 << 20, transcendentals=rows * 128
        ),
        name="own_rows",
    )(info, grad_own, mixed, tokens, cotangent, packed, packed, grad_shared, *earlier)


def passed_after(values, mark):
    return pl.pallas_call(
        lambda *_: None,
        out_shape=jax.ShapeDtypeStruct(values.shape, values.dtype),
        in_specs=[IN_HBM, IN_HBM],
        out_specs=IN_HBM,
        input_output_aliases={0: 0},
        name="passed_after",
    )(values, mark)


def finish_expert_kernel(mine_ref, *refs):
    half = pl.program_id(0)
    refs[4][...] = jnp.concatenate(
        [
            jnp.where(
                mine_ref[part] == half, refs[part][...].astype(F32), refs[2 + part][...].astype(F32)
            )
            for part in range(2)
        ],
        axis=1,
    )


def finish_expert(mine, own, other):
    rows, cols = own[0].shape
    taken = pl.BlockSpec((rows, cols), lambda i, _: (0, 0))
    return pl.pallas_call(
        finish_expert_kernel,
        out_shape=jax.ShapeDtypeStruct((2 * rows, 2 * cols), F32),
        grid_spec=pltpu.PrefetchScalarGridSpec(
            num_scalar_prefetch=1,
            grid=(2,),
            in_specs=[taken] * 4,
            out_specs=pl.BlockSpec((rows, 2 * cols), lambda i, _: (i, 0)),
        ),
        compiler_params=pltpu.CompilerParams(vmem_limit_bytes=32 << 20),
        cost_estimate=pl.CostEstimate(flops=0, bytes_accessed=5 << 20, transcendentals=0),
        name="finish_expert",
    )(mine, *own, *other)


def finish_dense_kernel(
    mine_ref, first_ref, first_other_ref, last_ref, last_other_ref, gain_ref, wq_ref, wk_ref, wv_ref,
    *refs
):
    *weight_refs, out_ref, gate_ref, up_ref, gain_one_ref, gain_two_ref, router_ref = refs[-9:]

    def pieces(own_ref, other_ref, mine, widths):
        own, other = (own_ref[...].astype(F32), other_ref[...].astype(F32))
        whole = jnp.concatenate(
            [jnp.where(mine == 0, own, other), jnp.where(mine == 0, other, own)], axis=0
        )
        at = 0
        for cols in widths:
            yield whole[:, at : at + cols]
            at += cols

    width = out_ref.shape[1]
    *weights, out = pieces(first_ref, first_other_ref, mine_ref[0], [width] * 3 + [width - 128])
    out_end, small, gate, up = pieces(
        last_ref, last_other_ref, mine_ref[1], [128] * 2 + [gate_ref.shape[1]] * 2
    )
    gain_grad = jnp.zeros(gain_ref.shape, F32)
    for total, w_ref, weight_ref in zip(weights, (wq_ref, wk_ref, wv_ref), weight_refs):
        weight_ref[...] = total * gain_ref[...]
        gain_grad += jnp.sum(total * w_ref[...].astype(F32), axis=1, keepdims=True)
    out_ref[...] = jnp.concatenate([out, out_end], axis=1)
    gate_ref[...], up_ref[...] = (gate, up)
    lane = lax.broadcasted_iota(jnp.int32, small.shape, 1)
    experts = router_ref.shape[0]
    rows = jnp.where(lane == experts + 1, gain_grad, small).T
    router_ref[...] = rows[:experts]
    gain_two_ref[...] = rows[experts : experts + 1]
    gain_one_ref[...] = rows[experts + 1 : experts + 2]


def finish_dense(mine, first, first_other, last, last_other, gain, weights, earlier, experts):
    rows, width = weights[0].shape
    half = (last.shape[1] - 256) // 2
    shapes = [(rows, width)] * 4 + [(rows, half)] * 2 + [(1, rows)] * 2 + [(experts, rows)]
    vmem = pl.BlockSpec(memory_space=pltpu.VMEM)
    return pl.pallas_call(
        finish_dense_kernel,
        out_shape=tuple(jax.ShapeDtypeStruct(shape, F32) for shape in shapes),
        in_specs=[pl.BlockSpec(memory_space=pltpu.SMEM)] + [vmem] * 8 + [IN_HBM] * len(earlier),
        out_specs=(vmem,) * len(shapes),
        compiler_params=pltpu.CompilerParams(vmem_limit_bytes=ALL_VMEM),
        name="finish_dense",
    )(mine, first, first_other, last, last_other, gain, *weights, *earlier)


def assemble_kernel(back_ref, *refs, offsets, width, window):
    first_ref, last_ref = refs[-2:]
    groups = back_ref.shape[0]
    back = [back_ref[d].astype(F32) for d in range(groups)]
    cols_dev, first_at = (width // groups, 3 * window)
    last_at = first_at + width - 128
    act_at = last_at + 256
    hidden = (back_ref.shape[2] - act_at) // 2
    columns = [
        back[d][:, part * window + offsets[d] : part * window + offsets[d] + cols_dev]
        for part in range(3)
        for d in range(groups)
    ]
    summed = back[0][:, first_at:act_at]
    for d in range(1, groups):
        summed += back[d][:, first_at:act_at]
    first_ref[...] = jnp.concatenate(columns + [summed[:, : last_at - first_at]], axis=1).astype(
        BF16
    )
    last_ref[...] = jnp.concatenate(
        [summed[:, last_at - first_at :]]
        + [
            back[d][:, act_at + part * hidden : act_at + (part + 1) * hidden]
            for part in range(2)
            for d in range(groups)
        ],
        axis=1,
    ).astype(BF16)


def assemble(back, offsets, width, hidden, window, earlier):
    groups, rows, cols = back.shape
    vmem = pl.BlockSpec(memory_space=pltpu.VMEM)
    return pl.pallas_call(
        functools.partial(
            assemble_kernel, offsets=tuple(offsets), width=width, window=window
        ),
        out_shape=(
            jax.ShapeDtypeStruct((rows, 4 * width - 128), BF16),
            jax.ShapeDtypeStruct((rows, 256 + 2 * groups * hidden), BF16),
        ),
        in_specs=[vmem] + [IN_HBM] * len(earlier),
        out_specs=(vmem, vmem),
        compiler_params=pltpu.CompilerParams(vmem_limit_bytes=ALL_VMEM),
        name="assemble",
    )(back, *earlier)


def finish_rows_kernel(
    info_ref, hidden_ref, branch_ref, grad_hidden_ref, grad_unit_ref, tokens_ref, out_ref, grad_ref
):
    rows = hidden_ref.shape[0]
    position = info_ref[1] * rows + lax.broadcasted_iota(jnp.int32, (rows, 1), 0)
    live = (position < info_ref[0]).astype(F32)
    out_ref[...] = (hidden_ref[...] + live * branch_ref[...].astype(F32)).astype(BF16)
    inputs = tokens_ref[...].astype(F32)
    grad_ref[...] = grad_hidden_ref[...] + rms_back(
        inputs, inv_rms(inputs), grad_unit_ref[...].astype(F32)
    )


def finish_rows(info, hidden, branch, grad_hidden, grad_unit, tokens):
    vmem = pl.BlockSpec(memory_space=pltpu.VMEM)
    return pl.pallas_call(
        finish_rows_kernel,
        out_shape=(
            jax.ShapeDtypeStruct(hidden.shape, BF16),
            jax.ShapeDtypeStruct(hidden.shape, F32),
        ),
        in_specs=[pl.BlockSpec(memory_space=pltpu.SMEM)] + [vmem] * 5,
        out_specs=(vmem, vmem),
        compiler_params=pltpu.CompilerParams(vmem_limit_bytes=ALL_VMEM),
        name="finish_rows",
    )(info, hidden, branch, grad_hidden, grad_unit, tokens)


def gather_rows(values):
    return lax.all_gather(values, "fsdp", axis=0, tiled=True)


def exchange(chunks):
    return lax.all_to_all(chunks, "fsdp", split_axis=0, concat_axis=0, tiled=True)


def scatter_sum(values):
    return lax.psum_scatter(values, "fsdp", scatter_dimension=0, tiled=True)


def after(values, mark):
    mark = mark[(slice(-1, None),) * mark.ndim].reshape(()).astype(F32)
    return jnp.where(mark < jnp.inf, values, jnp.zeros((), values.dtype))


def swap_rep(values, bit):
    count = lax.axis_size("rep")
    return lax.ppermute(values, "rep", [(i, i ^ (1 << bit)) for i in range(count)])


def rep_bits():
    count = lax.axis_size("rep")
    bits = count.bit_length() - 1
    assert count == 1 << bits
    return range(bits)


def rep_add(keep, send, bit, mark=None):
    if mark is not None:
        keep = after(keep, mark)
    return (keep.astype(F32) + swap_rep(send, bit).astype(F32)).astype(keep.dtype)


def rep_step(values, axis, bit, ready=None):
    half = values.shape[axis] // 2
    mine = (lax.axis_index("rep") >> bit) & 1
    keep = lax.dynamic_slice_in_dim(values, mine * half, half, axis)
    send = lax.dynamic_slice_in_dim(values, (1 - mine) * half, half, axis)
    if ready is not None:
        send = after(send, ready)
    return rep_add(keep, send, bit)


def rep_scatter_sum(values, axis, bits):
    for bit in bits:
        values = rep_step(values, axis, bit)
    return values


def rep_join(values, axis, bits=None):
    index = lax.axis_index("rep")
    for bit in reversed(rep_bits() if bits is None else bits):
        values = joined(values, swap_rep(values, bit), (index >> bit) & 1, axis)
    return values


def joined(own, other, mine, axis):
    return jnp.where(
        mine == 0,
        jnp.concatenate([own, other], axis=axis),
        jnp.concatenate([other, own], axis=axis),
    )


def on_device(
    tokens,
    cotangent,
    lengths,
    routes,
    gain_attn,
    gain_ffn,
    w_query,
    w_key,
    w_value,
    w_out,
    w_router,
    shared_gate,
    shared_up,
    shared_down,
    expert_gate,
    expert_up,
    expert_down,
):
    rows_dev, width = tokens.shape[1:]
    groups = lax.axis_size("fsdp")
    reps = lax.axis_size("rep")
    me = lax.axis_index("fsdp")
    seq_len = groups * rows_dev
    experts = w_router.shape[1]
    capacity = min(rows_dev, 5 * rows_dev // (2 * experts))
    length = lengths[0]
    my_rows = me * rows_dev
    live_all = jnp.arange(seq_len, dtype=jnp.int32) < length
    live_col = lax.dynamic_slice_in_dim(live_all, my_rows, rows_dev, 0).astype(F32)[:, None]

    cols_dev = width // groups
    first_heads = [d * cols_dev // HEAD_DIM for d in range(groups)]
    span = max(-(-(d + 1) * cols_dev // HEAD_DIM) - first_heads[d] for d in range(groups))
    first_heads = [min(head, HEADS - span) for head in first_heads]
    window = span * HEAD_DIM
    window_starts = [head * HEAD_DIM for head in first_heads]
    offsets = [d * cols_dev - window_starts[d] for d in range(groups)]
    my_offset = jnp.asarray(offsets, jnp.int32)[me]

    tokens_all = gather_rows(tokens[0])
    rep_rows = cols_dev // reps
    rep_at = lax.axis_index("rep") * rep_rows

    def rep_part(weight):
        return lax.dynamic_slice_in_dim(weight, rep_at, rep_rows, 0)

    gain_part = rep_part(gain_attn).astype(F32)[:, None]
    qkv_rows = [
        (rep_part(weight).astype(F32) * gain_part).astype(BF16)
        for weight in (w_query, w_key, w_value)
    ]
    qkv_chunks = jnp.stack(
        [
            jnp.concatenate([weight[:, at : at + window] for weight in qkv_rows], axis=1)
            for at in window_starts
        ]
    )
    qkv_part = exchange(qkv_chunks)
    qkv_cols = lax.all_gather(qkv_part, "rep", axis=0)
    qkv_cols = qkv_cols.transpose(1, 0, 2, 3).reshape(width, 3 * window)
    cosine, sine = rope_tables(seq_len)

    cotangent_all = gather_rows(after(cotangent[0], qkv_cols))
    shared_cols_dev = shared_gate.shape[1] // groups
    gate_chunks, up_chunks = [
        rep_part(weight).reshape(rep_rows, groups, shared_cols_dev).transpose(1, 0, 2)
        for weight in (shared_gate, shared_up)
    ]
    route_cols = -(-2 * rows_dev // rep_rows)
    route_chunk = jnp.pad(
        routes[0].astype(BF16).reshape(-1), (0, route_cols * rep_rows - 2 * rows_dev)
    ).reshape(rep_rows, route_cols)
    small_cols = experts + 1 + route_cols
    small = jnp.concatenate(
        [
            rep_part(w_router),
            rep_part(gain_ffn)[:, None],
            route_chunk,
            jnp.zeros((rep_rows, -small_cols % 128), BF16),
        ],
        axis=1,
    )
    packed_part = exchange(
        after(
            jnp.concatenate(
                [
                    jnp.broadcast_to(rep_part(w_out), (groups, rep_rows, width)),
                    gate_chunks,
                    up_chunks,
                    jnp.broadcast_to(small, (groups, *small.shape)),
                ],
                axis=2,
            ),
            qkv_cols,
        )
    )
    small_at = width + 2 * shared_cols_dev
    routes_all = (
        packed_part[:, :, small_at + experts + 1 : small_at + small_cols]
        .reshape(groups, rep_rows * route_cols)[:, : 2 * rows_dev]
        .reshape(groups, rows_dev, 2)
        .astype(jnp.int32)
    )
    packed_all = lax.psum(
        lax.dynamic_update_slice_in_dim(
            jnp.zeros((groups, cols_dev, small_at + 128), BF16),
            packed_part[:, :, : small_at + 128],
            rep_at,
            1,
        ),
        "rep",
    ).reshape(width, -1)
    routed = jnp.any(routes_all == me // 2, axis=2) & live_all.reshape(groups, rows_dev)
    rank = jnp.cumsum(routed.astype(jnp.int32), axis=1) - 1
    rank = jnp.where(routed, rank, -1)[:, None, :]

    inputs_all = tokens_all.astype(F32)
    unit = (inputs_all * inv_rms(inputs_all)).astype(BF16)
    qkv = contract(qkv_cols, unit, 0, 1)
    queries = (rotate_cols(qkv[:window], cosine, sine).astype(BF16).astype(F32) * 0.125).astype(
        BF16
    )
    keys = rotate_cols(qkv[window : 2 * window], cosine, sine).astype(BF16)
    values = qkv[2 * window :].astype(BF16)
    mixed_heads, log_norm = attn_forward(lengths, queries, keys, values)
    mixed_own = lax.dynamic_slice_in_dim(mixed_heads, my_offset, cols_dev, 0).astype(BF16)
    mixed_own = after(mixed_own, cotangent_all)
    mixed_all = gather_rows(mixed_own)

    orders = (list(rep_bits()), list(rep_bits())[::-1])
    mine = [(lax.axis_index("rep") >> order[0]) & 1 for order in orders]
    info = jnp.stack([length, me, jnp.zeros((), jnp.int32), my_offset, *mine])
    (
        branch_part,
        grad_part,
        normed,
        shared_inner,
        shared_act_grad,
        rows_in,
        expert_inner,
        expert_gate_grad,
        expert_up_grad,
        grad_half,
    ) = run_branches(
        info,
        mixed_all,
        tokens_all,
        cotangent_all,
        rank,
        packed_all,
        shared_down,
        expert_gate,
        expert_up,
        expert_down,
        experts,
        capacity,
    )
    grad_own = scatter_sum(grad_part)

    half_rows, half_cols = (expert_inner.shape[1] // 2, width // 2)

    def half_grad(part, half):
        rows_half = lax.dynamic_slice_in_dim(expert_inner, half * half_rows, half_rows, 1)
        cols_half = grad_half[:, part * half_cols : (part + 1) * half_cols]
        return matmul_tn(rows_half, cols_half).astype(BF16)

    received = [
        swap_rep(half_grad(part, 1 - mine[part]), order[0]) for part, order in enumerate(orders)
    ]
    expert_parts = [
        (half_grad(part, mine[part]).astype(F32) + received[part].astype(F32)).astype(BF16)
        for part in range(2)
    ]
    whole_sums = lax.psum(
        (
            matmul_tn(rows_in, expert_gate_grad).astype(BF16),
            matmul_tn(rows_in, expert_up_grad).astype(BF16),
            matmul_tn(shared_inner, cotangent_all).astype(BF16),
        ),
        "rep",
    )
    grad_shared = matmul_tn(normed, shared_act_grad).astype(BF16)
    mixed_rows = lax.dynamic_slice_in_dim(mixed_all, my_rows, rows_dev, 1)

    hidden, grad_hidden, grad_mixed, first_keep, first_send, last_keep, last_send = (
        own_rows(
            info,
            grad_own,
            mixed_rows,
            tokens[0],
            cotangent[0],
            packed_all,
            grad_shared,
            tuple(expert_parts),
            experts,
            groups,
            window,
            window_starts,
        )
    )
    grad_mixed_cols = exchange(grad_mixed)
    branch_own = scatter_sum(passed_after(branch_part, grad_mixed_cols))
    expert_parts = [
        rep_scatter_sum(
            rep_step(part, 0, order[1], ready=grad_mixed_cols), 0, order[2:]
        )
        for part, order in zip(expert_parts, orders)
    ]
    grad_q, grad_k, grad_v, mark_attn = attn_backward(
        lengths,
        queries,
        keys,
        values,
        mixed_heads,
        log_norm,
        grad_mixed_cols,
        (),
    )
    dense_first = rep_add(first_keep, first_send, orders[0][0], mark_attn)
    dense_last = rep_add(last_keep, last_send, orders[1][0], mark_attn)
    grad_unit_part, qkv_keep, qkv_send = projections_backward(
        info,
        grad_q,
        grad_k,
        grad_v,
        cosine,
        sine,
        unit,
        qkv_cols,
        cols_dev,
        (dense_first, dense_last),
    )
    qkv_part = rep_add(qkv_keep, qkv_send, orders[0][0], expert_parts[1])
    dense_first = rep_scatter_sum(dense_first, 1, orders[0][1:])
    dense_last = rep_scatter_sum(dense_last, 1, orders[1][1:])
    grad_unit = scatter_sum(grad_unit_part)
    output, input_grad = finish_rows(info, hidden, branch_own, grad_hidden, grad_unit, tokens[0])

    expert_own = [
        rep_join(after(part, qkv_part), 0, order[1:]) for part, order in zip(expert_parts, orders)
    ]
    expert_other = [swap_rep(part, order[0]) for part, order in zip(expert_own, orders)]
    sum_edown = finish_expert(jnp.stack(mine), expert_own, expert_other)
    qkv_part = rep_scatter_sum(qkv_part, 1, orders[0][1:])
    back = exchange(jnp.concatenate([qkv_part, dense_first, dense_last], axis=2))
    sum_egate, sum_eup, sum_down = [after(total, back).astype(F32) for total in whole_sums]
    first_part, last_part = assemble(back, offsets, width, shared_cols_dev, window, (sum_edown,))
    first_part = rep_join(first_part, 0, orders[0][1:])
    last_part = rep_join(last_part, 0, orders[1][1:])
    first_other = swap_rep(first_part, orders[0][0])
    last_other = swap_rep(last_part, orders[1][0])
    *sums_qkv, sum_out, sum_gate, sum_up, sum_gain_attn, sum_gain_ffn, sum_router = finish_dense(
        jnp.stack(mine),
        first_part,
        first_other,
        last_part,
        last_other,
        gain_attn.astype(F32)[:, None],
        (w_query, w_key, w_value),
        (sum_egate, sum_edown),
        experts,
    )
    return (
        output[None],
        input_grad[None],
        sum_gain_attn[0],
        sum_gain_ffn[0],
        *sums_qkv,
        sum_out,
        sum_router.T,
        sum_gate,
        sum_up,
        sum_down,
        sum_egate,
        sum_eup,
        sum_edown,
    )


def solution(mesh):
    in_specs = (
        P("rep", "fsdp", None),
        P("rep", "fsdp", None),
        P("rep"),
        P("rep", "fsdp", None),
        P("fsdp"),
        P("fsdp"),
        P("fsdp", None),
        P("fsdp", None),
        P("fsdp", None),
        P("fsdp", None),
        P("fsdp", None),
        P("fsdp", None),
        P("fsdp", None),
        P("fsdp", None),
        P(None, "fsdp"),
        P(None, "fsdp"),
        P("fsdp", None),
    )
    out_specs = (
        P("rep", "fsdp", None),
        P("rep", "fsdp", None),
        P("fsdp"),
        P("fsdp"),
        P("fsdp", None),
        P("fsdp", None),
        P("fsdp", None),
        P("fsdp", None),
        P("fsdp", None),
        P("fsdp", None),
        P("fsdp", None),
        P("fsdp", None),
        P(None, "fsdp"),
        P(None, "fsdp"),
        P("fsdp", None),
    )
    return jax.shard_map(
        on_device, mesh=mesh, in_specs=in_specs, out_specs=out_specs, check_vma=False
    )
```

```python
import functools

import jax
import jax.numpy as jnp
from jax import lax
from jax.experimental import pallas as pl
from jax.experimental.pallas import tpu as pltpu
from jax.sharding import PartitionSpec as P

HEADS = 12
HEAD_DIM = 64

EPSILON = 1e-06
ROPE_BASE = 10000.0
NEG_FILL = -1e30
ALL_VMEM = 60 << 20
IN_HBM = pl.BlockSpec(memory_space=pltpu.HBM)
F32 = jnp.float32
BF16 = jnp.bfloat16


def contract(first_op, second_op, first_dim, second_dim):
    return lax.dot_general(
        first_op,
        second_op,
        (((first_dim,), (second_dim,)), ((), ())),
        preferred_element_type=F32,
    )


def matmul(first_op, second_op):
    return contract(first_op, second_op, 1, 0)


def matmul_tn(first_op, second_op):
    return contract(first_op, second_op, 0, 0)


def matmul_nt(first_op, second_op):
    return contract(first_op, second_op, 1, 1)


def inv_rms(values):
    return lax.rsqrt(jnp.mean(values * values, axis=-1, keepdims=True) + EPSILON)


def rms_back(values, scale, grad_scaled):
    return scale * grad_scaled - values * (
        scale * scale * scale * jnp.mean(grad_scaled * values, axis=-1, keepdims=True)
    )


def swiglu(gate_act, up_act):
    return (jax.nn.silu(gate_act) * up_act).astype(BF16)


def swiglu_grad(grad_inner, gate_act, up_act):
    grad_inner = grad_inner.astype(F32)
    sig = jax.nn.sigmoid(gate_act)
    grad_gate = grad_inner * up_act * (sig * (1.0 + gate_act * (1.0 - sig)))
    grad_up = grad_inner * (gate_act * sig)
    return (grad_gate.astype(BF16), grad_up.astype(BF16))


def rope_tables(seq_len):
    half_dim = HEAD_DIM // 2
    frequency = ROPE_BASE ** (-jnp.arange(half_dim, dtype=F32) / half_dim)
    angles = frequency[:, None] * jnp.arange(seq_len, dtype=F32)[None, :]
    return (jnp.cos(angles), jnp.sin(angles))


def rotate_cols(values, cosine, sine):
    rows, seq_len = values.shape
    split = values.reshape(rows // HEAD_DIM, 2, HEAD_DIM // 2, seq_len)
    first, second = (split[:, 0], split[:, 1])
    turned = jnp.stack(
        [first * cosine - second * sine, second * cosine + first * sine], axis=1
    )
    return turned.reshape(rows, seq_len)


def put_halves(values, mine, keep_ref, send_ref, at=0):
    groups, rows, _ = keep_ref.shape
    cols = slice(at, at + values.shape[1])
    for dest in range(groups):
        first = values[2 * dest * rows : (2 * dest + 1) * rows]
        last = values[(2 * dest + 1) * rows : (2 * dest + 2) * rows]
        keep_ref[dest, :, cols] = jnp.where(mine == 0, first, last).astype(BF16)
        send_ref[dest, :, cols] = jnp.where(mine == 0, last, first).astype(BF16)


def attn_forward_kernel(len_ref, q_ref, k_ref, v_ref, o_ref, l_ref, *, heads, blk):
    row = pl.program_id(0)
    length = len_ref[0]
    queries = q_ref[...]

    def step(masked, col, state):
        cols = pl.ds(pl.multiple_of(col * blk, blk), blk)
        keys, values = (k_ref[:, cols], v_ref[:, cols])
        if masked:
            key_pos = col * blk + lax.broadcasted_iota(jnp.int32, (blk, blk), 0)
            query_pos = row * blk + lax.broadcasted_iota(jnp.int32, (blk, blk), 1)
            allowed = (key_pos <= query_pos) & (key_pos < length)
        result = []
        for head in range(heads):
            top, total, acc = state[head]
            part = slice(head * HEAD_DIM, (head + 1) * HEAD_DIM)
            scores = matmul_tn(keys[part], queries[part])
            if masked:
                scores = jnp.where(allowed, scores, NEG_FILL)
            new_top = jnp.maximum(top, jnp.max(scores, axis=0, keepdims=True))
            probs = jnp.exp(scores - new_top)
            shrink = jnp.exp(top - new_top)
            total = total * shrink + jnp.sum(probs, axis=0, keepdims=True)
            acc = acc * shrink + matmul(values[part], probs.astype(BF16))
            result.append((new_top, total, acc))
        return tuple(result)

    start = tuple(
        (
            jnp.full((1, blk), NEG_FILL, F32),
            jnp.zeros((1, blk), F32),
            jnp.zeros((HEAD_DIM, blk), F32),
        )
        for _ in range(heads)
    )
    whole = jnp.minimum(row, length // blk)
    end = jnp.minimum(row + 1, (length + blk - 1) // blk)
    state = lax.fori_loop(0, whole, functools.partial(step, False), start)
    state = lax.fori_loop(whole, end, functools.partial(step, True), state)
    for head in range(heads):
        top, total, acc = state[head]
        o_ref[head * HEAD_DIM : (head + 1) * HEAD_DIM, :] = acc * (1.0 / total)
        l_ref[head : head + 1, :] = top + jnp.log(total)


def attn_backward_kernel(
    len_ref, q_ref, k_ref, v_ref, o_ref, l_ref, do_ref, *refs, heads, blk
):
    dq_ref, dk_ref, dv_ref = refs[-3:]
    row = pl.program_id(0)
    length = len_ref[0]

    @pl.when(row == 0)
    def _():
        dk_ref[...] = jnp.zeros_like(dk_ref)
        dv_ref[...] = jnp.zeros_like(dv_ref)

    parts = [slice(head * HEAD_DIM, (head + 1) * HEAD_DIM) for head in range(heads)]
    queries = q_ref[...]
    grad_out = jnp.concatenate([do_ref[src] for src in range(do_ref.shape[0])], axis=1)
    deltas = [
        jnp.sum(grad_out[part].astype(F32) * o_ref[part, :], axis=0, keepdims=True)
        for part in parts
    ]
    log_norms = [l_ref[head : head + 1, :] for head in range(heads)]

    def step(masked, col, state):
        cols = pl.ds(pl.multiple_of(col * blk, blk), blk)
        keys, values = (k_ref[:, cols], v_ref[:, cols])
        if masked:
            key_pos = col * blk + lax.broadcasted_iota(jnp.int32, (blk, blk), 0)
            query_pos = row * blk + lax.broadcasted_iota(jnp.int32, (blk, blk), 1)
            allowed = (key_pos <= query_pos) & (key_pos < length)
        result = []
        for head, part in enumerate(parts):
            scores = matmul_tn(keys[part], queries[part])
            grad_probs = matmul_tn(values[part], grad_out[part])
            probs = jnp.exp(scores - log_norms[head])
            if masked:
                probs = jnp.where(allowed, probs, 0.0)
            grad_scores = (probs * (grad_probs - deltas[head])).astype(BF16)
            dv_ref[part, cols] += matmul_nt(grad_out[part], probs.astype(BF16))
            dk_ref[part, cols] += matmul_nt(queries[part], grad_scores)
            result.append(state[head] + matmul(keys[part], grad_scores))
        return tuple(result)

    start = tuple(jnp.zeros((HEAD_DIM, blk), F32) for _ in range(heads))
    whole = jnp.minimum(row, length // blk)
    end = jnp.minimum(row + 1, (length + blk - 1) // blk)
    state = lax.fori_loop(0, whole, functools.partial(step, False), start)
    state = lax.fori_loop(whole, end, functools.partial(step, True), state)
    for head, part in enumerate(parts):
        dq_ref[part, :] = state[head]


def attn_specs(rows, seq_len, heads, blk):
    block = pl.BlockSpec((rows, blk), lambda i, _: (0, i))
    whole = pl.BlockSpec((rows, seq_len), lambda i, _: (0, 0))
    stats = pl.BlockSpec((heads, blk), lambda i, _: (0, i))
    return (block, whole, stats)


def attn_cost(rows, seq_len, heads, products):
    pairs = heads * seq_len * seq_len // 2
    return pl.CostEstimate(
        flops=2 * products * pairs * 256, bytes_accessed=16 * rows * seq_len, transcendentals=pairs
    )


def attn_forward(length, queries, keys, values):
    rows, seq_len = queries.shape
    heads, blk = (rows // HEAD_DIM, min(512, seq_len))
    block, whole, stats = attn_specs(rows, seq_len, heads, blk)
    return pl.pallas_call(
        functools.partial(attn_forward_kernel, heads=heads, blk=blk),
        out_shape=(
            jax.ShapeDtypeStruct((rows, seq_len), F32),
            jax.ShapeDtypeStruct((heads, seq_len), F32),
        ),
        grid_spec=pltpu.PrefetchScalarGridSpec(
            num_scalar_prefetch=1,
            grid=(seq_len // blk,),
            in_specs=[block, whole, whole],
            out_specs=(block, stats),
        ),
        compiler_params=pltpu.CompilerParams(vmem_limit_bytes=40 << 20),
        cost_estimate=attn_cost(rows, seq_len, heads, 2),
        name="attn_forward",
    )(length, queries, keys, values)


def attn_backward(length, queries, keys, values, mixed, log_norm, grad_mixed, earlier):
    rows, seq_len = queries.shape
    heads, blk = (rows // HEAD_DIM, min(512, seq_len))
    block, whole, stats = attn_specs(rows, seq_len, heads, blk)
    rows_dev = grad_mixed.shape[2]
    sources = pl.BlockSpec((blk // rows_dev, rows, rows_dev), lambda i, _: (i, 0, 0))
    return pl.pallas_call(
        functools.partial(attn_backward_kernel, heads=heads, blk=blk),
        out_shape=(jax.ShapeDtypeStruct((rows, seq_len), F32),) * 3,
        grid_spec=pltpu.PrefetchScalarGridSpec(
            num_scalar_prefetch=1,
            grid=(seq_len // blk,),
            in_specs=[block, whole, whole, block, stats, sources]
            + [IN_HBM] * len(earlier),
            out_specs=(block, whole, whole),
        ),
        compiler_params=pltpu.CompilerParams(vmem_limit_bytes=ALL_VMEM),
        cost_estimate=pl.CostEstimate(flops=0, bytes_accessed=0, transcendentals=0),
        name="attn_backward",
    )(length, queries, keys, values, mixed, log_norm, grad_mixed, *earlier)


def projections_kernel(
    info_ref, dq_ref, dk_ref, dv_ref, cos_ref, sin_ref, unit_ref, w_ref, first_ref, first_got_ref,
    last_ref, last_got_ref, grad_ref, keep_ref, send_ref, first_keep_ref, first_send_ref,
    last_keep_ref, last_send_ref, total_ref, *, cols_dev
):
    rows = dq_ref.shape[0]
    cosine, sine = (cos_ref[...], sin_ref[...])
    channel = lax.broadcasted_iota(jnp.int32, (rows, 1), 0)
    owned = ((channel >= info_ref[3]) & (channel < info_ref[3] + cols_dev)).astype(F32)

    def turn_back(values):
        parts = []
        for at in range(0, rows, HEAD_DIM):
            first = values[at : at + HEAD_DIM // 2]
            second = values[at + HEAD_DIM // 2 : at + HEAD_DIM]
            parts += [first * cosine + second * sine, second * cosine - first * sine]
        return jnp.concatenate(parts, axis=0)

    grads = jnp.concatenate(
        [
            (owned * turn_back(dq_ref[...] * 0.125)).astype(BF16),
            (owned * turn_back(dk_ref[...])).astype(BF16),
            (owned * dv_ref[...]).astype(BF16),
        ],
        axis=0,
    )
    grad_ref[...] = contract(grads, w_ref[...], 0, 1).astype(BF16)
    part = matmul(grads, unit_ref[...])

    @pl.when(pl.program_id(0) == 0)
    def _():
        total_ref[...] = part
        for mine, own, got, kept, sent in (
            (info_ref[6], first_ref, first_got_ref, first_keep_ref, first_send_ref),
            (info_ref[7], last_ref, last_got_ref, last_keep_ref, last_send_ref),
        ):
            half = own.shape[1] // 2
            for dest in range(own.shape[0]):
                summed = own[dest].astype(F32) + got[dest].astype(F32)
                first, last = (summed[:half], summed[half:])
                kept[dest] = jnp.where(mine == 0, first, last).astype(BF16)
                sent[dest] = jnp.where(mine == 0, last, first).astype(BF16)

    @pl.when(pl.program_id(0) > 0)
    def _():
        total_ref[...] += part

    @pl.when(pl.program_id(0) == pl.num_programs(0) - 1)
    def _():
        put_halves(total_ref[...].T, info_ref[4], keep_ref, send_ref)


def projections_backward(
    info, grad_q, grad_k, grad_v, cosine, sine, unit, weight, cols_dev, dense
):
    rows, seq_len = grad_q.shape
    width = unit.shape[1]
    blk = min(512, seq_len)

    def part(count):
        return pl.BlockSpec((count, blk), lambda i, _: (0, i))

    by_row = pl.BlockSpec((blk, width), lambda i, _: (i, 0))
    whole = pl.BlockSpec(weight.shape, lambda i, _: (0, 0))
    half_shape = (width // cols_dev, cols_dev // 2, 3 * rows)
    quarters = [(part.shape[0], part.shape[1] // 2, part.shape[2]) for part in dense[::2]]
    quarters = [shape for shape in quarters for _ in range(2)]

    def all_of(shape):
        return pl.BlockSpec(shape, lambda i, _: (0, 0, 0))

    return pl.pallas_call(
        functools.partial(projections_kernel, cols_dev=cols_dev),
        out_shape=(
            pltpu.HBM((seq_len, width), BF16),
            *(jax.ShapeDtypeStruct(half_shape, BF16),) * 2,
            *(jax.ShapeDtypeStruct(shape, BF16) for shape in quarters),
        ),
        grid_spec=pltpu.PrefetchScalarGridSpec(
            num_scalar_prefetch=1,
            grid=(seq_len // blk,),
            in_specs=[part(rows)] * 3
            + [part(HEAD_DIM // 2)] * 2
            + [by_row, whole]
            + [all_of(part.shape) for part in dense],
            out_specs=(by_row, *(all_of(shape) for shape in [half_shape] * 2 + quarters)),
            scratch_shapes=[pltpu.VMEM((3 * rows, width), F32)],
        ),
        compiler_params=pltpu.CompilerParams(vmem_limit_bytes=ALL_VMEM),
        cost_estimate=pl.CostEstimate(flops=0, bytes_accessed=0, transcendentals=0),
        name="projections_backward",
    )(info, grad_q, grad_k, grad_v, cosine, sine, unit, weight, *dense)


def branch_kernel(
    info_ref,
    mixed_ref,
    tokens_ref,
    cotangent_ref,
    rank_ref,
    out_w_ref,
    gate_ref,
    up_ref,
    small_ref,
    down_ref,
    egate_ref,
    eup_ref,
    edown_ref,
    branch_ref,
    grad_ref,
    normed_ref,
    inner_ref,
    act_grad_ref,
    rows_ref,
    einner_ref,
    egate_grad_ref,
    eup_grad_ref,
    half_grad_ref,
    *,
    experts,
    groups,
    capacity,
):
    rows = tokens_ref.shape[0]
    blocks, _, rows_dev = rank_ref.shape
    length, me = (info_ref[0], info_ref[1])
    first_pos = info_ref[2] + pl.program_id(0) * rows

    hidden = tokens_ref[...].astype(F32) + matmul_tn(mixed_ref[...], out_w_ref[...])
    small = small_ref[...].astype(F32).T
    gain = small[experts : experts + 1]
    normed = (hidden * inv_rms(hidden) * gain).astype(BF16)
    normed_ref[...] = normed
    logits = matmul_nt(small[:16].astype(BF16), normed)
    expert_row = lax.broadcasted_iota(jnp.int32, logits.shape, 0)
    logits = jnp.where(expert_row < experts, logits, NEG_FILL)
    weights = jnp.exp(logits - jnp.max(logits, axis=0, keepdims=True))
    probs = weights / jnp.sum(weights, axis=0, keepdims=True)
    prob_row = jnp.sum(jnp.where(expert_row == me // 2, probs, 0.0), axis=0, keepdims=True)

    position = first_pos + lax.broadcasted_iota(jnp.int32, (rows, 1), 0)
    live = (position < length).astype(F32)
    grad_out = (cotangent_ref[...].astype(F32) * live).astype(BF16)

    gate_act, up_act = (matmul(normed, gate_ref[...]), matmul(normed, up_ref[...]))
    inner = swiglu(gate_act, up_act)
    inner_ref[...] = (inner.astype(F32) * live).astype(BF16)
    branch = matmul(inner, down_ref[...])
    gate_grad, up_grad = swiglu_grad(
        matmul_nt(grad_out, down_ref[...]).astype(BF16), gate_act, up_act
    )
    act_grad = jnp.concatenate([gate_grad, up_grad], axis=1)
    act_grad_ref[...] = act_grad
    grad = matmul_nt(gate_grad, gate_ref[...]) + matmul_nt(up_grad, up_ref[...])

    picks, picked, picked_grad, picked_prob = ([], [], [], [])
    slot = lax.broadcasted_iota(jnp.int32, (capacity, rows_dev), 0)
    for blk in range(blocks):
        part = slice(blk * rows_dev, (blk + 1) * rows_dev)
        hot = (slot == rank_ref[blk]).astype(F32)
        picked_prob.append(jnp.sum(hot * prob_row[:, part], axis=1, keepdims=True))
        pick = hot.astype(BF16)
        picks.append(pick)
        picked.append(matmul(pick, normed[part]).astype(BF16))
        picked_grad.append(matmul(pick, grad_out[part]).astype(BF16))
    rows_in = jnp.concatenate(picked, axis=0)
    grad_rows = jnp.concatenate(picked_grad, axis=0).astype(F32)
    row_prob = jnp.concatenate(picked_prob, axis=0)
    rows_ref[...] = rows_in
    egate_act = matmul(rows_in, egate_ref[...])
    eup_act = matmul(rows_in, eup_ref[...])
    einner = swiglu(egate_act, eup_act)
    einner_ref[...] = einner
    half = matmul(einner, edown_ref[...]).astype(BF16).astype(F32)
    dots = jnp.sum(grad_rows * half, axis=1, keepdims=True)
    half_grad = (row_prob * grad_rows).astype(BF16)
    half_grad_ref[...] = half_grad
    egate_grad, eup_grad = swiglu_grad(
        matmul_nt(half_grad, edown_ref[...]).astype(BF16), egate_act, eup_act
    )
    egate_grad_ref[...] = egate_grad
    eup_grad_ref[...] = eup_grad
    rows_grad = (
        matmul_nt(egate_grad, egate_ref[...]) + matmul_nt(eup_grad, eup_ref[...])
    ).astype(BF16)
    gated = (row_prob * half).astype(BF16)

    dots_high = dots.astype(BF16).astype(F32)
    lane = lax.broadcasted_iota(jnp.int32, (1, 128), 1)
    dots_cols = jnp.where(lane == me, dots_high, 0.0) + jnp.where(
        lane == me + groups, dots - dots_high, 0.0
    )
    dots_cols = dots_cols.astype(BF16)
    width = normed.shape[1]
    for blk in range(blocks):
        part = slice(blk * rows_dev, (blk + 1) * rows_dev)
        from_part = slice(blk * capacity, (blk + 1) * capacity)
        pick = picks[blk]
        branch_ref[part, :] = (branch[part] + matmul_tn(pick, gated[from_part])).astype(BF16)
        grad_ref[part, :width] = (grad[part] + matmul_tn(pick, rows_grad[from_part])).astype(BF16)
        grad_ref[part, width:] = matmul_tn(pick, dots_cols[from_part]).astype(BF16)


def run_branches(
    info, mixed, tokens, cotangent, rank, packed, down, egate, eup, edown, experts, capacity
):
    seq_len, width = tokens.shape
    groups, _, rows_dev = rank.shape
    blocks = 2 if groups % 2 == 0 else 1
    rows, picked = (blocks * rows_dev, blocks * capacity)
    hidden, ehidden = (down.shape[0], egate.shape[1])
    act_cols = 2 * hidden

    def step_rows(count, cols):
        return pl.BlockSpec((count, cols), lambda i, _: (i, 0))

    def whole(shape):
        return pl.BlockSpec(shape, lambda i, _: (0, 0), pipeline_mode=pl.Buffered(1))

    def packed_part(cols, at):
        return pl.BlockSpec(
            (width, cols), lambda i, _: (0, at // cols), pipeline_mode=pl.Buffered(1)
        )

    def result(count, cols):
        return jax.ShapeDtypeStruct((count, cols), BF16)

    all_picked = groups * capacity
    flops = 2 * seq_len * width * (width + 6 * act_cols // 2) + 2 * all_picked * width * (
        6 * ehidden + 4 * rows_dev
    )
    return pl.pallas_call(
        functools.partial(branch_kernel, experts=experts, groups=groups, capacity=capacity),
        out_shape=(
            result(seq_len, width),
            result(seq_len, width + 128),
            result(seq_len, width),
            result(seq_len, hidden),
            result(seq_len, act_cols),
            result(all_picked, width),
            result(all_picked, ehidden),
            result(all_picked, ehidden),
            result(all_picked, ehidden),
            result(all_picked, width),
        ),
        grid_spec=pltpu.PrefetchScalarGridSpec(
            num_scalar_prefetch=1,
            grid=(groups // blocks,),
            in_specs=[
                pl.BlockSpec((width, rows), lambda i, _: (0, i)),
                step_rows(rows, width),
                step_rows(rows, width),
                pl.BlockSpec((blocks, 1, rows_dev), lambda i, _: (i, 0, 0)),
                packed_part(width, 0),
                packed_part(hidden, width),
                packed_part(hidden, width + hidden),
                packed_part(128, width + act_cols),
                whole(down.shape),
                whole(egate.shape),
                whole(eup.shape),
                whole(edown.shape),
            ],
            out_specs=(
                step_rows(rows, width),
                step_rows(rows, width + 128),
                step_rows(rows, width),
                step_rows(rows, hidden),
                step_rows(rows, act_cols),
                step_rows(picked, width),
                step_rows(picked, ehidden),
                step_rows(picked, ehidden),
                step_rows(picked, ehidden),
                step_rows(picked, width),
            ),
        ),
        compiler_params=pltpu.CompilerParams(vmem_limit_bytes=ALL_VMEM),
        cost_estimate=pl.CostEstimate(
            flops=flops, bytes_accessed=40 << 20, transcendentals=2 * all_picked * ehidden
        ),
        name="branches",
    )(info, mixed, tokens, cotangent, rank, packed, packed, packed, packed, down, egate, eup, edown)


def own_rows_kernel(
    info_ref,
    grad_ref,
    mixed_ref,
    tokens_ref,
    cotangent_ref,
    out_w_ref,
    small_ref,
    shared_ref,
    *refs,
    experts,
    groups,
    window_starts,
):
    hidden_ref, grad_hidden_ref, grad_mixed_ref, *first_refs, last_keep_ref, last_send_ref = refs[
        -7:
    ]
    rows, width = tokens_ref.shape
    length, me = (info_ref[0], info_ref[1])
    small = small_ref[...].astype(F32)
    gain = small.T[experts : experts + 1]
    hidden = tokens_ref[...].astype(F32) + matmul_tn(mixed_ref[...], out_w_ref[...])
    scale = inv_rms(hidden)
    unit = hidden * scale
    normed = (unit * gain).astype(BF16)
    lane = lax.broadcasted_iota(jnp.int32, (rows, 128), 1)
    is_expert = lane < experts
    logits = jnp.where(is_expert, matmul(normed, small.astype(BF16)), NEG_FILL)
    weights = jnp.exp(logits - jnp.max(logits, axis=1, keepdims=True))
    probs = weights / jnp.sum(weights, axis=1, keepdims=True)
    dots = grad_ref[:, width:].astype(F32)
    grad_probs = jnp.zeros((rows, 128), F32)
    for expert in range(experts):
        source = lane % groups // 2
        part = jnp.where((lane < 2 * groups) & (source == expert), dots, 0.0)
        grad_probs = jnp.where(
            lane == expert, jnp.sum(part, axis=1, keepdims=True), grad_probs
        )
    mean = jnp.sum(probs * grad_probs, axis=1, keepdims=True)
    grad_logits = jnp.where(is_expert, probs * (grad_probs - mean), 0.0).astype(BF16)
    router = jnp.where(
        lax.broadcasted_iota(jnp.int32, small.shape, 1) < experts, small, 0.0
    ).astype(BF16)
    grad_normed = grad_ref[:, :width].astype(F32) + matmul_nt(grad_logits, router)
    position = me * rows + lax.broadcasted_iota(jnp.int32, (rows, 1), 0)
    live = (position < length).astype(F32)
    grad_hidden = cotangent_ref[...].astype(F32) * live + rms_back(
        hidden, scale, grad_normed * gain
    )
    hidden_ref[...] = hidden * live
    grad_hidden_ref[...] = grad_hidden
    grad_hidden_b = grad_hidden.astype(BF16)
    grad_mixed = matmul_nt(out_w_ref[...], grad_hidden_b).astype(BF16)
    for dest, at in enumerate(window_starts):
        grad_mixed_ref[dest] = grad_mixed[at : at + grad_mixed_ref.shape[1]]
    cut = first_refs[0].shape[2]
    grad_out_w = matmul(mixed_ref[...], grad_hidden_b)
    put_halves(grad_out_w[:, :cut], info_ref[4], *first_refs)
    ones = jnp.where(lane == experts, 1.0, 0.0).astype(BF16)
    small_grad = matmul_tn(normed, grad_logits) + matmul_tn((grad_normed * unit).astype(BF16), ones)
    last = jnp.concatenate([grad_out_w[:, cut:], small_grad, shared_ref[...].astype(F32)], axis=1)
    put_halves(last, info_ref[5], last_keep_ref, last_send_ref)


def own_rows(
    info, grad_own, mixed, tokens, cotangent, packed, grad_shared, earlier, experts, groups, window,
    window_starts,
):
    rows, width = tokens.shape
    small_at = packed.shape[1] // 128 - 1

    def whole(shape):
        return pl.BlockSpec(shape, lambda i, _: (0,) * len(shape))

    shapes = (
        ((rows, width), F32),
        ((rows, width), F32),
        ((groups, window, rows), BF16),
        *(((groups, width // groups // 2, width - 128), BF16),) * 2,
        *(((groups, width // groups // 2, 256 + grad_shared.shape[1]), BF16),) * 2,
    )
    return pl.pallas_call(
        functools.partial(
            own_rows_kernel, experts=experts, groups=groups, window_starts=tuple(window_starts)
        ),
        out_shape=tuple(jax.ShapeDtypeStruct(shape, dtype) for shape, dtype in shapes),
        grid_spec=pltpu.PrefetchScalarGridSpec(
            num_scalar_prefetch=1,
            grid=(1,),
            in_specs=[
                whole(grad_own.shape),
                whole(mixed.shape),
                whole(tokens.shape),
                whole(cotangent.shape),
                whole((width, width)),
                pl.BlockSpec((width, 128), lambda i, _: (0, small_at)),
                whole(grad_shared.shape),
            ]
            + [IN_HBM] * len(earlier),
            out_specs=tuple(whole(shape) for shape, _ in shapes),
        ),
        compiler_params=pltpu.CompilerParams(vmem_limit_bytes=ALL_VMEM),
        cost_estimate=pl.CostEstimate(
            flops=6 * rows * width * width, bytes_accessed=6 << 20, transcendentals=rows * 128
        ),
        name="own_rows",
    )(info, grad_own, mixed, tokens, cotangent, packed, packed, grad_shared, *earlier)


def passed_after(values, mark):
    return pl.pallas_call(
        lambda *_: None,
        out_shape=jax.ShapeDtypeStruct(values.shape, values.dtype),
        in_specs=[IN_HBM, IN_HBM],
        out_specs=IN_HBM,
        input_output_aliases={0: 0},
        name="passed_after",
    )(values, mark)


def finish_down_kernel(mine_ref, *refs):
    half = pl.program_id(0)
    whole = jnp.concatenate(
        [
            jnp.where(
                mine_ref[part] == half, refs[part][...].astype(F32), refs[2 + part][...].astype(F32)
            )
            for part in range(2)
        ],
        axis=1,
    )
    rows = refs[4].shape[0]
    refs[4][...] = whole[:rows]
    refs[5][...] = whole[rows:]


def finish_down(mine, own, other, expert_rows):
    rows, cols = own[0].shape
    shapes = ((expert_rows, 2 * cols), (2 * rows - expert_rows, 2 * cols))
    return pl.pallas_call(
        finish_down_kernel,
        out_shape=tuple(jax.ShapeDtypeStruct(shape, F32) for shape in shapes),
        grid_spec=pltpu.PrefetchScalarGridSpec(
            num_scalar_prefetch=1,
            grid=(2,),
            in_specs=[pl.BlockSpec((rows, cols), lambda i, _: (0, 0))] * 4,
            out_specs=tuple(
                pl.BlockSpec((shape[0] // 2, shape[1]), lambda i, _: (i, 0)) for shape in shapes
            ),
        ),
        compiler_params=pltpu.CompilerParams(vmem_limit_bytes=32 << 20),
        cost_estimate=pl.CostEstimate(flops=0, bytes_accessed=6 << 20, transcendentals=0),
        name="finish_down",
    )(mine, *own, *other)


def finish_dense_kernel(
    mine_ref, first_ref, first_other_ref, last_ref, last_other_ref, gain_ref, wq_ref, wk_ref, wv_ref,
    *refs
):
    *weight_refs, out_ref, gate_ref, up_ref, gain_one_ref, gain_two_ref, router_ref = refs[-9:]

    def pieces(own_ref, other_ref, mine, widths):
        own, other = (own_ref[...].astype(F32), other_ref[...].astype(F32))
        whole = jnp.concatenate(
            [jnp.where(mine == 0, own, other), jnp.where(mine == 0, other, own)], axis=0
        )
        at = 0
        for cols in widths:
            yield whole[:, at : at + cols]
            at += cols

    width = out_ref.shape[1]
    *weights, out = pieces(first_ref, first_other_ref, mine_ref[0], [width] * 3 + [width - 128])
    out_end, small, gate, up = pieces(
        last_ref, last_other_ref, mine_ref[1], [128] * 2 + [gate_ref.shape[1]] * 2
    )
    gain_grad = jnp.zeros(gain_ref.shape, F32)
    for total, w_ref, weight_ref in zip(weights, (wq_ref, wk_ref, wv_ref), weight_refs):
        weight_ref[...] = total * gain_ref[...]
        gain_grad += jnp.sum(total * w_ref[...].astype(F32), axis=1, keepdims=True)
    out_ref[...] = jnp.concatenate([out, out_end], axis=1)
    gate_ref[...], up_ref[...] = (gate, up)
    lane = lax.broadcasted_iota(jnp.int32, small.shape, 1)
    experts = router_ref.shape[0]
    rows = jnp.where(lane == experts + 1, gain_grad, small).T
    router_ref[...] = rows[:experts]
    gain_two_ref[...] = rows[experts : experts + 1]
    gain_one_ref[...] = rows[experts + 1 : experts + 2]


def finish_dense(mine, first, first_other, last, last_other, gain, weights, earlier, experts):
    rows, width = weights[0].shape
    half = (last.shape[1] - 256) // 2
    shapes = [(rows, width)] * 4 + [(rows, half)] * 2 + [(1, rows)] * 2 + [(experts, rows)]
    vmem = pl.BlockSpec(memory_space=pltpu.VMEM)
    return pl.pallas_call(
        finish_dense_kernel,
        out_shape=tuple(jax.ShapeDtypeStruct(shape, F32) for shape in shapes),
        in_specs=[pl.BlockSpec(memory_space=pltpu.SMEM)] + [vmem] * 8 + [IN_HBM] * len(earlier),
        out_specs=(vmem,) * len(shapes),
        compiler_params=pltpu.CompilerParams(vmem_limit_bytes=ALL_VMEM),
        name="finish_dense",
    )(mine, first, first_other, last, last_other, gain, *weights, *earlier)


def assemble_kernel(back_ref, *refs, offsets, width, window):
    first_ref, last_ref = refs[-2:]
    groups = back_ref.shape[0]
    back = [back_ref[d].astype(F32) for d in range(groups)]
    cols_dev, first_at = (width // groups, 3 * window)
    last_at = first_at + width - 128
    act_at = last_at + 256
    hidden = (back_ref.shape[2] - act_at) // 2
    columns = [
        back[d][:, part * window + offsets[d] : part * window + offsets[d] + cols_dev]
        for part in range(3)
        for d in range(groups)
    ]
    summed = back[0][:, first_at:act_at]
    for d in range(1, groups):
        summed += back[d][:, first_at:act_at]
    first_ref[...] = jnp.concatenate(columns + [summed[:, : last_at - first_at]], axis=1).astype(
        BF16
    )
    last_ref[...] = jnp.concatenate(
        [summed[:, last_at - first_at :]]
        + [
            back[d][:, act_at + part * hidden : act_at + (part + 1) * hidden]
            for part in range(2)
            for d in range(groups)
        ],
        axis=1,
    ).astype(BF16)


def assemble(back, offsets, width, hidden, window, earlier):
    groups, rows, cols = back.shape
    vmem = pl.BlockSpec(memory_space=pltpu.VMEM)
    return pl.pallas_call(
        functools.partial(
            assemble_kernel, offsets=tuple(offsets), width=width, window=window
        ),
        out_shape=(
            jax.ShapeDtypeStruct((rows, 4 * width - 128), BF16),
            jax.ShapeDtypeStruct((rows, 256 + 2 * groups * hidden), BF16),
        ),
        in_specs=[vmem] + [IN_HBM] * len(earlier),
        out_specs=(vmem, vmem),
        compiler_params=pltpu.CompilerParams(vmem_limit_bytes=ALL_VMEM),
        name="assemble",
    )(back, *earlier)


def finish_rows_kernel(
    info_ref, hidden_ref, branch_ref, grad_hidden_ref, grad_unit_ref, tokens_ref, out_ref, grad_ref
):
    rows = hidden_ref.shape[0]
    position = info_ref[1] * rows + lax.broadcasted_iota(jnp.int32, (rows, 1), 0)
    live = (position < info_ref[0]).astype(F32)
    out_ref[...] = (hidden_ref[...] + live * branch_ref[...].astype(F32)).astype(BF16)
    inputs = tokens_ref[...].astype(F32)
    grad_ref[...] = grad_hidden_ref[...] + rms_back(
        inputs, inv_rms(inputs), grad_unit_ref[...].astype(F32)
    )


def finish_rows(info, hidden, branch, grad_hidden, grad_unit, tokens):
    vmem = pl.BlockSpec(memory_space=pltpu.VMEM)
    return pl.pallas_call(
        finish_rows_kernel,
        out_shape=(
            jax.ShapeDtypeStruct(hidden.shape, BF16),
            jax.ShapeDtypeStruct(hidden.shape, F32),
        ),
        in_specs=[pl.BlockSpec(memory_space=pltpu.SMEM)] + [vmem] * 5,
        out_specs=(vmem, vmem),
        compiler_params=pltpu.CompilerParams(vmem_limit_bytes=ALL_VMEM),
        name="finish_rows",
    )(info, hidden, branch, grad_hidden, grad_unit, tokens)


def gather_rows(values):
    return lax.all_gather(values, "fsdp", axis=0, tiled=True)


def exchange(chunks):
    return lax.all_to_all(chunks, "fsdp", split_axis=0, concat_axis=0, tiled=True)


def scatter_sum(values):
    return lax.psum_scatter(values, "fsdp", scatter_dimension=0, tiled=True)


def after(values, mark):
    mark = mark[(slice(-1, None),) * mark.ndim].reshape(()).astype(F32)
    return jnp.where(mark < jnp.inf, values, jnp.zeros((), values.dtype))


def swap_rep(values, bit):
    count = lax.axis_size("rep")
    return lax.ppermute(values, "rep", [(i, i ^ (1 << bit)) for i in range(count)])


def rep_bits():
    count = lax.axis_size("rep")
    bits = count.bit_length() - 1
    assert count == 1 << bits
    return range(bits)


def rep_add(keep, send, bit, mark=None):
    if mark is not None:
        keep = after(keep, mark)
    return (keep.astype(F32) + swap_rep(send, bit).astype(F32)).astype(keep.dtype)


def rep_step(values, axis, bit, ready=None):
    half = values.shape[axis] // 2
    mine = (lax.axis_index("rep") >> bit) & 1
    keep = lax.dynamic_slice_in_dim(values, mine * half, half, axis)
    send = lax.dynamic_slice_in_dim(values, (1 - mine) * half, half, axis)
    if ready is not None:
        send = after(send, ready)
    return rep_add(keep, send, bit)


def rep_scatter_sum(values, axis, bits):
    for bit in bits:
        values = rep_step(values, axis, bit)
    return values


def rep_join(values, axis, bits=None):
    index = lax.axis_index("rep")
    for bit in reversed(rep_bits() if bits is None else bits):
        values = joined(values, swap_rep(values, bit), (index >> bit) & 1, axis)
    return values


def joined(own, other, mine, axis):
    return jnp.where(
        mine == 0,
        jnp.concatenate([own, other], axis=axis),
        jnp.concatenate([other, own], axis=axis),
    )


def on_device(
    tokens,
    cotangent,
    lengths,
    routes,
    gain_attn,
    gain_ffn,
    w_query,
    w_key,
    w_value,
    w_out,
    w_router,
    shared_gate,
    shared_up,
    shared_down,
    expert_gate,
    expert_up,
    expert_down,
):
    rows_dev, width = tokens.shape[1:]
    groups = lax.axis_size("fsdp")
    reps = lax.axis_size("rep")
    me = lax.axis_index("fsdp")
    seq_len = groups * rows_dev
    experts = w_router.shape[1]
    capacity = min(rows_dev, 5 * rows_dev // (2 * experts))
    length = lengths[0]
    my_rows = me * rows_dev
    live_all = jnp.arange(seq_len, dtype=jnp.int32) < length
    live_col = lax.dynamic_slice_in_dim(live_all, my_rows, rows_dev, 0).astype(F32)[:, None]

    cols_dev = width // groups
    first_heads = [d * cols_dev // HEAD_DIM for d in range(groups)]
    span = max(-(-(d + 1) * cols_dev // HEAD_DIM) - first_heads[d] for d in range(groups))
    first_heads = [min(head, HEADS - span) for head in first_heads]
    window = span * HEAD_DIM
    window_starts = [head * HEAD_DIM for head in first_heads]
    offsets = [d * cols_dev - window_starts[d] for d in range(groups)]
    my_offset = jnp.asarray(offsets, jnp.int32)[me]

    tokens_all = gather_rows(tokens[0])
    rep_rows = cols_dev // reps
    rep_at = lax.axis_index("rep") * rep_rows

    def rep_part(weight):
        return lax.dynamic_slice_in_dim(weight, rep_at, rep_rows, 0)

    gain_part = rep_part(gain_attn).astype(F32)[:, None]
    qkv_rows = [
        (rep_part(weight).astype(F32) * gain_part).astype(BF16)
        for weight in (w_query, w_key, w_value)
    ]
    qkv_chunks = jnp.stack(
        [
            jnp.concatenate([weight[:, at : at + window] for weight in qkv_rows], axis=1)
            for at in window_starts
        ]
    )
    qkv_part = exchange(qkv_chunks)
    qkv_cols = lax.all_gather(qkv_part, "rep", axis=0)
    qkv_cols = qkv_cols.transpose(1, 0, 2, 3).reshape(width, 3 * window)
    cosine, sine = rope_tables(seq_len)

    cotangent_all = gather_rows(after(cotangent[0], qkv_cols))
    shared_cols_dev = shared_gate.shape[1] // groups
    gate_chunks, up_chunks = [
        rep_part(weight).reshape(rep_rows, groups, shared_cols_dev).transpose(1, 0, 2)
        for weight in (shared_gate, shared_up)
    ]
    route_cols = -(-2 * rows_dev // rep_rows)
    route_chunk = jnp.pad(
        routes[0].astype(BF16).reshape(-1), (0, route_cols * rep_rows - 2 * rows_dev)
    ).reshape(rep_rows, route_cols)
    small_cols = experts + 1 + route_cols
    small = jnp.concatenate(
        [
            rep_part(w_router),
            rep_part(gain_ffn)[:, None],
            route_chunk,
            jnp.zeros((rep_rows, -small_cols % 128), BF16),
        ],
        axis=1,
    )
    packed_part = exchange(
        after(
            jnp.concatenate(
                [
                    jnp.broadcast_to(rep_part(w_out), (groups, rep_rows, width)),
                    gate_chunks,
                    up_chunks,
                    jnp.broadcast_to(small, (groups, *small.shape)),
                ],
                axis=2,
            ),
            qkv_cols,
        )
    )
    small_at = width + 2 * shared_cols_dev
    routes_all = (
        packed_part[:, :, small_at + experts + 1 : small_at + small_cols]
        .reshape(groups, rep_rows * route_cols)[:, : 2 * rows_dev]
        .reshape(groups, rows_dev, 2)
        .astype(jnp.int32)
    )
    packed_all = lax.psum(
        lax.dynamic_update_slice_in_dim(
            jnp.zeros((groups, cols_dev, small_at + 128), BF16),
            packed_part[:, :, : small_at + 128],
            rep_at,
            1,
        ),
        "rep",
    ).reshape(width, -1)
    routed = jnp.any(routes_all == me // 2, axis=2) & live_all.reshape(groups, rows_dev)
    rank = jnp.cumsum(routed.astype(jnp.int32), axis=1) - 1
    rank = jnp.where(routed, rank, -1)[:, None, :]

    inputs_all = tokens_all.astype(F32)
    unit = (inputs_all * inv_rms(inputs_all)).astype(BF16)
    qkv = contract(qkv_cols, unit, 0, 1)
    queries = (rotate_cols(qkv[:window], cosine, sine).astype(BF16).astype(F32) * 0.125).astype(
        BF16
    )
    keys = rotate_cols(qkv[window : 2 * window], cosine, sine).astype(BF16)
    values = qkv[2 * window :].astype(BF16)
    mixed_heads, log_norm = attn_forward(lengths, queries, keys, values)
    mixed_own = lax.dynamic_slice_in_dim(mixed_heads, my_offset, cols_dev, 0).astype(BF16)
    mixed_own = after(mixed_own, cotangent_all)
    mixed_all = gather_rows(mixed_own)

    orders = (list(rep_bits()), list(rep_bits())[::-1])
    mine, mine_next = [
        [(lax.axis_index("rep") >> order[step]) & 1 for order in orders] for step in range(2)
    ]
    info = jnp.stack([length, me, jnp.zeros((), jnp.int32), my_offset, *mine, *mine_next])
    (
        branch_part,
        grad_part,
        normed,
        shared_inner,
        shared_act_grad,
        rows_in,
        expert_inner,
        expert_gate_grad,
        expert_up_grad,
        grad_half,
    ) = run_branches(
        info,
        mixed_all,
        tokens_all,
        cotangent_all,
        rank,
        packed_all,
        shared_down,
        expert_gate,
        expert_up,
        expert_down,
        experts,
        capacity,
    )
    grad_own = scatter_sum(grad_part)

    half_cols = width // 2

    def half_grad(part, half):
        def of_rows(inner, grad):
            rows = inner.shape[1] // 2
            return matmul_tn(
                lax.dynamic_slice_in_dim(inner, half * rows, rows, 1),
                grad[:, part * half_cols : (part + 1) * half_cols],
            ).astype(BF16)

        return jnp.concatenate(
            [of_rows(expert_inner, grad_half), of_rows(shared_inner, cotangent_all)], axis=0
        )

    down_parts = [
        rep_scatter_sum(
            rep_add(half_grad(part, mine[part]), half_grad(part, 1 - mine[part]), order[0]),
            0,
            order[1:],
        )
        for part, order in enumerate(orders)
    ]
    whole_sums = lax.psum(
        (
            matmul_tn(rows_in, expert_gate_grad).astype(BF16),
            matmul_tn(rows_in, expert_up_grad).astype(BF16),
        ),
        "rep",
    )
    grad_shared = matmul_tn(normed, shared_act_grad).astype(BF16)
    mixed_rows = lax.dynamic_slice_in_dim(mixed_all, my_rows, rows_dev, 1)

    hidden, grad_hidden, grad_mixed, first_keep, first_send, last_keep, last_send = (
        own_rows(
            info,
            grad_own,
            mixed_rows,
            tokens[0],
            cotangent[0],
            packed_all,
            grad_shared,
            tuple(down_parts),
            experts,
            groups,
            window,
            window_starts,
        )
    )
    grad_mixed_cols = exchange(grad_mixed)
    branch_own = scatter_sum(passed_after(branch_part, grad_mixed_cols))
    grad_q, grad_k, grad_v = attn_backward(
        lengths,
        queries,
        keys,
        values,
        mixed_heads,
        log_norm,
        grad_mixed_cols,
        (),
    )
    (
        grad_unit_part,
        qkv_keep,
        qkv_send,
        first_keep,
        first_send,
        last_keep,
        last_send,
    ) = projections_backward(
        info,
        grad_q,
        grad_k,
        grad_v,
        cosine,
        sine,
        unit,
        qkv_cols,
        cols_dev,
        (
            first_keep,
            swap_rep(first_send, orders[0][0]),
            last_keep,
            swap_rep(last_send, orders[1][0]),
        ),
    )
    qkv_part = rep_add(qkv_keep, qkv_send, orders[0][0], branch_own)
    dense_first = rep_scatter_sum(
        rep_add(first_keep, first_send, orders[0][1]), 1, orders[0][2:]
    )
    dense_last = rep_scatter_sum(rep_add(last_keep, last_send, orders[1][1]), 1, orders[1][2:])
    grad_unit = scatter_sum(grad_unit_part)
    output, input_grad = finish_rows(info, hidden, branch_own, grad_hidden, grad_unit, tokens[0])

    down_own = [rep_join(part, 0, order[1:]) for part, order in zip(down_parts, orders)]
    down_other = [swap_rep(own, order[0]) for own, order in zip(down_own, orders)]
    sum_edown, sum_down = finish_down(
        jnp.stack(mine), down_own, down_other, expert_inner.shape[1]
    )
    qkv_part = rep_scatter_sum(qkv_part, 1, orders[0][1:])
    back = exchange(
        jnp.concatenate(
            [
                qkv_part,
                after(dense_first, down_own[0]),
                after(after(dense_last, down_own[1]), whole_sums[1]),
            ],
            axis=2,
        )
    )
    sum_egate, sum_eup = [after(total, back).astype(F32) for total in whole_sums]
    first_part, last_part = assemble(back, offsets, width, shared_cols_dev, window, (sum_edown,))
    first_part = rep_join(first_part, 0, orders[0][1:])
    last_part = rep_join(last_part, 0, orders[1][1:])
    first_other = swap_rep(first_part, orders[0][0])
    last_other = swap_rep(last_part, orders[1][0])
    *sums_qkv, sum_out, sum_gate, sum_up, sum_gain_attn, sum_gain_ffn, sum_router = finish_dense(
        jnp.stack(mine),
        first_part,
        first_other,
        last_part,
        last_other,
        gain_attn.astype(F32)[:, None],
        (w_query, w_key, w_value),
        (sum_egate, sum_edown),
        experts,
    )
    return (
        output[None],
        input_grad[None],
        sum_gain_attn[0],
        sum_gain_ffn[0],
        *sums_qkv,
        sum_out,
        sum_router.T,
        sum_gate,
        sum_up,
        sum_down,
        sum_egate,
        sum_eup,
        sum_edown,
    )


def solution(mesh):
    in_specs = (
        P("rep", "fsdp", None),
        P("rep", "fsdp", None),
        P("rep"),
        P("rep", "fsdp", None),
        P("fsdp"),
        P("fsdp"),
        P("fsdp", None),
        P("fsdp", None),
        P("fsdp", None),
        P("fsdp", None),
        P("fsdp", None),
        P("fsdp", None),
        P("fsdp", None),
        P("fsdp", None),
        P(None, "fsdp"),
        P(None, "fsdp"),
        P("fsdp", None),
    )
    out_specs = (
        P("rep", "fsdp", None),
        P("rep", "fsdp", None),
        P("fsdp"),
        P("fsdp"),
        P("fsdp", None),
        P("fsdp", None),
        P("fsdp", None),
        P("fsdp", None),
        P("fsdp", None),
        P("fsdp", None),
        P("fsdp", None),
        P("fsdp", None),
        P(None, "fsdp"),
        P(None, "fsdp"),
        P("fsdp", None),
    )
    return jax.shard_map(
        on_device, mesh=mesh, in_specs=in_specs, out_specs=out_specs, check_vma=False
    )
```

```python
import functools

import jax
import jax.numpy as jnp
from jax import lax
from jax.experimental import pallas as pl
from jax.experimental.pallas import tpu as pltpu
from jax.sharding import PartitionSpec as P

HEADS = 12
HEAD_DIM = 64

EPSILON = 1e-06
ROPE_BASE = 10000.0
NEG_FILL = -1e30
ALL_VMEM = 60 << 20
IN_HBM = pl.BlockSpec(memory_space=pltpu.HBM)
F32 = jnp.float32
BF16 = jnp.bfloat16


def contract(first_op, second_op, first_dim, second_dim):
    return lax.dot_general(
        first_op,
        second_op,
        (((first_dim,), (second_dim,)), ((), ())),
        preferred_element_type=F32,
    )


def matmul(first_op, second_op):
    return contract(first_op, second_op, 1, 0)


def matmul_tn(first_op, second_op):
    return contract(first_op, second_op, 0, 0)


def matmul_nt(first_op, second_op):
    return contract(first_op, second_op, 1, 1)


def inv_rms(values):
    return lax.rsqrt(jnp.mean(values * values, axis=-1, keepdims=True) + EPSILON)


def rms_back(values, scale, grad_scaled):
    return scale * grad_scaled - values * (
        scale * scale * scale * jnp.mean(grad_scaled * values, axis=-1, keepdims=True)
    )


def swiglu(gate_act, up_act):
    return (jax.nn.silu(gate_act) * up_act).astype(BF16)


def swiglu_grad(grad_inner, gate_act, up_act):
    grad_inner = grad_inner.astype(F32)
    sig = jax.nn.sigmoid(gate_act)
    grad_gate = grad_inner * up_act * (sig * (1.0 + gate_act * (1.0 - sig)))
    grad_up = grad_inner * (gate_act * sig)
    return (grad_gate.astype(BF16), grad_up.astype(BF16))


def rope_tables(seq_len):
    half_dim = HEAD_DIM // 2
    frequency = ROPE_BASE ** (-jnp.arange(half_dim, dtype=F32) / half_dim)
    angles = frequency[:, None] * jnp.arange(seq_len, dtype=F32)[None, :]
    return (jnp.cos(angles), jnp.sin(angles))


def rotate_cols(values, cosine, sine):
    rows, seq_len = values.shape
    split = values.reshape(rows // HEAD_DIM, 2, HEAD_DIM // 2, seq_len)
    first, second = (split[:, 0], split[:, 1])
    turned = jnp.stack(
        [first * cosine - second * sine, second * cosine + first * sine], axis=1
    )
    return turned.reshape(rows, seq_len)


def put_halves(values, mine, keep_ref, send_ref, at=0):
    groups, rows, _ = keep_ref.shape
    cols = slice(at, at + values.shape[1])
    for dest in range(groups):
        first = values[2 * dest * rows : (2 * dest + 1) * rows]
        last = values[(2 * dest + 1) * rows : (2 * dest + 2) * rows]
        keep_ref[dest, :, cols] = jnp.where(mine == 0, first, last).astype(BF16)
        send_ref[dest, :, cols] = jnp.where(mine == 0, last, first).astype(BF16)


def attn_forward_kernel(len_ref, q_ref, k_ref, v_ref, o_ref, l_ref, *, heads, blk):
    row = pl.program_id(0)
    length = len_ref[0]
    queries = q_ref[...]

    def step(masked, col, state):
        cols = pl.ds(pl.multiple_of(col * blk, blk), blk)
        keys, values = (k_ref[:, cols], v_ref[:, cols])
        if masked:
            key_pos = col * blk + lax.broadcasted_iota(jnp.int32, (blk, blk), 0)
            query_pos = row * blk + lax.broadcasted_iota(jnp.int32, (blk, blk), 1)
            allowed = (key_pos <= query_pos) & (key_pos < length)
        result = []
        for head in range(heads):
            top, total, acc = state[head]
            part = slice(head * HEAD_DIM, (head + 1) * HEAD_DIM)
            scores = matmul_tn(keys[part], queries[part])
            if masked:
                scores = jnp.where(allowed, scores, NEG_FILL)
            new_top = jnp.maximum(top, jnp.max(scores, axis=0, keepdims=True))
            probs = jnp.exp(scores - new_top)
            shrink = jnp.exp(top - new_top)
            total = total * shrink + jnp.sum(probs, axis=0, keepdims=True)
            acc = acc * shrink + matmul(values[part], probs.astype(BF16))
            result.append((new_top, total, acc))
        return tuple(result)

    start = tuple(
        (
            jnp.full((1, blk), NEG_FILL, F32),
            jnp.zeros((1, blk), F32),
            jnp.zeros((HEAD_DIM, blk), F32),
        )
        for _ in range(heads)
    )
    whole = jnp.minimum(row, length // blk)
    end = jnp.minimum(row + 1, (length + blk - 1) // blk)
    state = lax.fori_loop(0, whole, functools.partial(step, False), start)
    state = lax.fori_loop(whole, end, functools.partial(step, True), state)
    for head in range(heads):
        top, total, acc = state[head]
        o_ref[head * HEAD_DIM : (head + 1) * HEAD_DIM, :] = acc * (1.0 / total)
        l_ref[head : head + 1, :] = top + jnp.log(total)


def attn_backward_kernel(
    len_ref, q_ref, k_ref, v_ref, o_ref, l_ref, do_ref, *refs, heads, blk
):
    dq_ref, dk_ref, dv_ref = refs[-3:]
    row = pl.program_id(0)
    length = len_ref[0]

    @pl.when(row == 0)
    def _():
        dk_ref[...] = jnp.zeros_like(dk_ref)
        dv_ref[...] = jnp.zeros_like(dv_ref)

    parts = [slice(head * HEAD_DIM, (head + 1) * HEAD_DIM) for head in range(heads)]
    queries = q_ref[...]
    grad_out = jnp.concatenate([do_ref[src] for src in range(do_ref.shape[0])], axis=1)
    deltas = [
        jnp.sum(grad_out[part].astype(F32) * o_ref[part, :], axis=0, keepdims=True)
        for part in parts
    ]
    log_norms = [l_ref[head : head + 1, :] for head in range(heads)]

    def step(masked, col, state):
        cols = pl.ds(pl.multiple_of(col * blk, blk), blk)
        keys, values = (k_ref[:, cols], v_ref[:, cols])
        if masked:
            key_pos = col * blk + lax.broadcasted_iota(jnp.int32, (blk, blk), 0)
            query_pos = row * blk + lax.broadcasted_iota(jnp.int32, (blk, blk), 1)
            allowed = (key_pos <= query_pos) & (key_pos < length)
        result = []
        for head, part in enumerate(parts):
            scores = matmul_tn(keys[part], queries[part])
            grad_probs = matmul_tn(values[part], grad_out[part])
            probs = jnp.exp(scores - log_norms[head])
            if masked:
                probs = jnp.where(allowed, probs, 0.0)
            grad_scores = (probs * (grad_probs - deltas[head])).astype(BF16)
            dv_ref[part, cols] += matmul_nt(grad_out[part], probs.astype(BF16))
            dk_ref[part, cols] += matmul_nt(queries[part], grad_scores)
            result.append(state[head] + matmul(keys[part], grad_scores))
        return tuple(result)

    start = tuple(jnp.zeros((HEAD_DIM, blk), F32) for _ in range(heads))
    whole = jnp.minimum(row, length // blk)
    end = jnp.minimum(row + 1, (length + blk - 1) // blk)
    state = lax.fori_loop(0, whole, functools.partial(step, False), start)
    state = lax.fori_loop(whole, end, functools.partial(step, True), state)
    for head, part in enumerate(parts):
        dq_ref[part, :] = state[head]


def attn_specs(rows, seq_len, heads, blk):
    block = pl.BlockSpec((rows, blk), lambda i, _: (0, i))
    whole = pl.BlockSpec((rows, seq_len), lambda i, _: (0, 0))
    stats = pl.BlockSpec((heads, blk), lambda i, _: (0, i))
    return (block, whole, stats)


def attn_cost(rows, seq_len, heads, products):
    pairs = heads * seq_len * seq_len // 2
    return pl.CostEstimate(
        flops=2 * products * pairs * 256, bytes_accessed=16 * rows * seq_len, transcendentals=pairs
    )


def attn_forward(length, queries, keys, values):
    rows, seq_len = queries.shape
    heads, blk = (rows // HEAD_DIM, min(512, seq_len))
    block, whole, stats = attn_specs(rows, seq_len, heads, blk)
    return pl.pallas_call(
        functools.partial(attn_forward_kernel, heads=heads, blk=blk),
        out_shape=(
            jax.ShapeDtypeStruct((rows, seq_len), F32),
            jax.ShapeDtypeStruct((heads, seq_len), F32),
        ),
        grid_spec=pltpu.PrefetchScalarGridSpec(
            num_scalar_prefetch=1,
            grid=(seq_len // blk,),
            in_specs=[block, whole, whole],
            out_specs=(block, stats),
        ),
        compiler_params=pltpu.CompilerParams(vmem_limit_bytes=40 << 20),
        cost_estimate=attn_cost(rows, seq_len, heads, 2),
        name="attn_forward",
    )(length, queries, keys, values)


def attn_backward(length, queries, keys, values, mixed, log_norm, grad_mixed, earlier):
    rows, seq_len = queries.shape
    heads, blk = (rows // HEAD_DIM, min(512, seq_len))
    block, whole, stats = attn_specs(rows, seq_len, heads, blk)
    rows_dev = grad_mixed.shape[2]
    sources = pl.BlockSpec((blk // rows_dev, rows, rows_dev), lambda i, _: (i, 0, 0))
    return pl.pallas_call(
        functools.partial(attn_backward_kernel, heads=heads, blk=blk),
        out_shape=(jax.ShapeDtypeStruct((rows, seq_len), F32),) * 3,
        grid_spec=pltpu.PrefetchScalarGridSpec(
            num_scalar_prefetch=1,
            grid=(seq_len // blk,),
            in_specs=[block, whole, whole, block, stats, sources]
            + [IN_HBM] * len(earlier),
            out_specs=(block, whole, whole),
        ),
        compiler_params=pltpu.CompilerParams(vmem_limit_bytes=ALL_VMEM),
        cost_estimate=pl.CostEstimate(flops=0, bytes_accessed=0, transcendentals=0),
        name="attn_backward",
    )(length, queries, keys, values, mixed, log_norm, grad_mixed, *earlier)


def projections_kernel(
    info_ref, dq_ref, dk_ref, dv_ref, cos_ref, sin_ref, unit_ref, w_ref, first_ref, first_got_ref,
    last_ref, last_got_ref, grad_ref, keep_ref, send_ref, first_keep_ref, first_send_ref,
    last_keep_ref, last_send_ref, total_ref, *, cols_dev
):
    rows = dq_ref.shape[0]
    cosine, sine = (cos_ref[...], sin_ref[...])
    channel = lax.broadcasted_iota(jnp.int32, (rows, 1), 0)
    owned = ((channel >= info_ref[3]) & (channel < info_ref[3] + cols_dev)).astype(F32)

    def turn_back(values):
        parts = []
        for at in range(0, rows, HEAD_DIM):
            first = values[at : at + HEAD_DIM // 2]
            second = values[at + HEAD_DIM // 2 : at + HEAD_DIM]
            parts += [first * cosine + second * sine, second * cosine - first * sine]
        return jnp.concatenate(parts, axis=0)

    grads = jnp.concatenate(
        [
            (owned * turn_back(dq_ref[...] * 0.125)).astype(BF16),
            (owned * turn_back(dk_ref[...])).astype(BF16),
            (owned * dv_ref[...]).astype(BF16),
        ],
        axis=0,
    )
    grad_ref[...] = contract(grads, w_ref[...], 0, 1).astype(BF16)
    part = matmul(grads, unit_ref[...])

    @pl.when(pl.program_id(0) == 0)
    def _():
        total_ref[...] = part
        for mine, own, got, kept, sent in (
            (info_ref[6], first_ref, first_got_ref, first_keep_ref, first_send_ref),
            (info_ref[7], last_ref, last_got_ref, last_keep_ref, last_send_ref),
        ):
            half = own.shape[1] // 2
            for dest in range(own.shape[0]):
                summed = own[dest].astype(F32) + got[dest].astype(F32)
                first, last = (summed[:half], summed[half:])
                kept[dest] = jnp.where(mine == 0, first, last).astype(BF16)
                sent[dest] = jnp.where(mine == 0, last, first).astype(BF16)

    @pl.when(pl.program_id(0) > 0)
    def _():
        total_ref[...] += part

    @pl.when(pl.program_id(0) == pl.num_programs(0) - 1)
    def _():
        put_halves(total_ref[...].T, info_ref[4], keep_ref, send_ref)


def projections_backward(
    info, grad_q, grad_k, grad_v, cosine, sine, unit, weight, cols_dev, dense
):
    rows, seq_len = grad_q.shape
    width = unit.shape[1]
    blk = min(512, seq_len)

    def part(count):
        return pl.BlockSpec((count, blk), lambda i, _: (0, i))

    by_row = pl.BlockSpec((blk, width), lambda i, _: (i, 0))
    whole = pl.BlockSpec(weight.shape, lambda i, _: (0, 0))
    half_shape = (width // cols_dev, cols_dev // 2, 3 * rows)
    quarters = [(part.shape[0], part.shape[1] // 2, part.shape[2]) for part in dense[::2]]
    quarters = [shape for shape in quarters for _ in range(2)]

    def all_of(shape):
        return pl.BlockSpec(shape, lambda i, _: (0, 0, 0))

    return pl.pallas_call(
        functools.partial(projections_kernel, cols_dev=cols_dev),
        out_shape=(
            pltpu.HBM((seq_len, width), BF16),
            *(jax.ShapeDtypeStruct(half_shape, BF16),) * 2,
            *(jax.ShapeDtypeStruct(shape, BF16) for shape in quarters),
        ),
        grid_spec=pltpu.PrefetchScalarGridSpec(
            num_scalar_prefetch=1,
            grid=(seq_len // blk,),
            in_specs=[part(rows)] * 3
            + [part(HEAD_DIM // 2)] * 2
            + [by_row, whole]
            + [all_of(part.shape) for part in dense],
            out_specs=(by_row, *(all_of(shape) for shape in [half_shape] * 2 + quarters)),
            scratch_shapes=[pltpu.VMEM((3 * rows, width), F32)],
        ),
        compiler_params=pltpu.CompilerParams(vmem_limit_bytes=ALL_VMEM),
        cost_estimate=pl.CostEstimate(flops=0, bytes_accessed=0, transcendentals=0),
        name="projections_backward",
    )(info, grad_q, grad_k, grad_v, cosine, sine, unit, weight, *dense)


def branch_kernel(
    info_ref,
    mixed_ref,
    tokens_ref,
    cotangent_ref,
    rank_ref,
    out_w_ref,
    gate_ref,
    up_ref,
    small_ref,
    down_ref,
    egate_ref,
    eup_ref,
    edown_ref,
    branch_ref,
    grad_ref,
    normed_ref,
    inner_ref,
    act_grad_ref,
    rows_ref,
    einner_ref,
    egate_grad_ref,
    eup_grad_ref,
    half_grad_ref,
    *,
    experts,
    groups,
    capacity,
):
    rows = tokens_ref.shape[0]
    blocks, _, rows_dev = rank_ref.shape
    length, me = (info_ref[0], info_ref[1])
    first_pos = info_ref[2] + pl.program_id(0) * rows

    hidden = tokens_ref[...].astype(F32) + matmul_tn(mixed_ref[...], out_w_ref[...])
    small = small_ref[...].astype(F32).T
    gain = small[experts : experts + 1]
    normed = (hidden * inv_rms(hidden) * gain).astype(BF16)
    normed_ref[...] = normed
    logits = matmul_nt(small[:16].astype(BF16), normed)
    expert_row = lax.broadcasted_iota(jnp.int32, logits.shape, 0)
    logits = jnp.where(expert_row < experts, logits, NEG_FILL)
    weights = jnp.exp(logits - jnp.max(logits, axis=0, keepdims=True))
    probs = weights / jnp.sum(weights, axis=0, keepdims=True)
    prob_row = jnp.sum(jnp.where(expert_row == me // 2, probs, 0.0), axis=0, keepdims=True)

    position = first_pos + lax.broadcasted_iota(jnp.int32, (rows, 1), 0)
    live = (position < length).astype(F32)
    grad_out = (cotangent_ref[...].astype(F32) * live).astype(BF16)

    gate_act, up_act = (matmul(normed, gate_ref[...]), matmul(normed, up_ref[...]))
    inner = swiglu(gate_act, up_act)
    inner_ref[...] = (inner.astype(F32) * live).astype(BF16)
    branch = matmul(inner, down_ref[...])
    gate_grad, up_grad = swiglu_grad(
        matmul_nt(grad_out, down_ref[...]).astype(BF16), gate_act, up_act
    )
    act_grad = jnp.concatenate([gate_grad, up_grad], axis=1)
    act_grad_ref[...] = act_grad
    grad = matmul_nt(gate_grad, gate_ref[...]) + matmul_nt(up_grad, up_ref[...])

    picks, picked, picked_grad, picked_prob = ([], [], [], [])
    slot = lax.broadcasted_iota(jnp.int32, (capacity, rows_dev), 0)
    for blk in range(blocks):
        part = slice(blk * rows_dev, (blk + 1) * rows_dev)
        hot = (slot == rank_ref[blk]).astype(F32)
        picked_prob.append(jnp.sum(hot * prob_row[:, part], axis=1, keepdims=True))
        pick = hot.astype(BF16)
        picks.append(pick)
        picked.append(matmul(pick, normed[part]).astype(BF16))
        picked_grad.append(matmul(pick, grad_out[part]).astype(BF16))
    rows_in = jnp.concatenate(picked, axis=0)
    grad_rows = jnp.concatenate(picked_grad, axis=0).astype(F32)
    row_prob = jnp.concatenate(picked_prob, axis=0)
    rows_ref[...] = rows_in
    egate_act = matmul(rows_in, egate_ref[...])
    eup_act = matmul(rows_in, eup_ref[...])
    einner = swiglu(egate_act, eup_act)
    einner_ref[...] = einner
    half = matmul(einner, edown_ref[...]).astype(BF16).astype(F32)
    dots = jnp.sum(grad_rows * half, axis=1, keepdims=True)
    half_grad = (row_prob * grad_rows).astype(BF16)
    half_grad_ref[...] = half_grad
    egate_grad, eup_grad = swiglu_grad(
        matmul_nt(half_grad, edown_ref[...]).astype(BF16), egate_act, eup_act
    )
    egate_grad_ref[...] = egate_grad
    eup_grad_ref[...] = eup_grad
    rows_grad = (
        matmul_nt(egate_grad, egate_ref[...]) + matmul_nt(eup_grad, eup_ref[...])
    ).astype(BF16)
    gated = (row_prob * half).astype(BF16)

    dots_high = dots.astype(BF16).astype(F32)
    lane = lax.broadcasted_iota(jnp.int32, (1, 128), 1)
    dots_cols = jnp.where(lane == me, dots_high, 0.0) + jnp.where(
        lane == me + groups, dots - dots_high, 0.0
    )
    dots_cols = dots_cols.astype(BF16)
    width = normed.shape[1]
    for blk in range(blocks):
        part = slice(blk * rows_dev, (blk + 1) * rows_dev)
        from_part = slice(blk * capacity, (blk + 1) * capacity)
        pick = picks[blk]
        branch_ref[part, :] = (branch[part] + matmul_tn(pick, gated[from_part])).astype(BF16)
        grad_ref[part, :width] = (grad[part] + matmul_tn(pick, rows_grad[from_part])).astype(BF16)
        grad_ref[part, width:] = matmul_tn(pick, dots_cols[from_part]).astype(BF16)


def run_branches(
    info, mixed, tokens, cotangent, rank, packed, down, egate, eup, edown, experts, capacity
):
    seq_len, width = tokens.shape
    groups, _, rows_dev = rank.shape
    blocks = 2 if groups % 2 == 0 else 1
    rows, picked = (blocks * rows_dev, blocks * capacity)
    hidden, ehidden = (down.shape[0], egate.shape[1])
    act_cols = 2 * hidden

    def step_rows(count, cols):
        return pl.BlockSpec((count, cols), lambda i, _: (i, 0))

    def whole(shape):
        return pl.BlockSpec(shape, lambda i, _: (0, 0), pipeline_mode=pl.Buffered(1))

    def packed_part(cols, at):
        return pl.BlockSpec(
            (width, cols), lambda i, _: (0, at // cols), pipeline_mode=pl.Buffered(1)
        )

    def result(count, cols):
        return jax.ShapeDtypeStruct((count, cols), BF16)

    all_picked = groups * capacity
    flops = 2 * seq_len * width * (width + 6 * act_cols // 2) + 2 * all_picked * width * (
        6 * ehidden + 4 * rows_dev
    )
    return pl.pallas_call(
        functools.partial(branch_kernel, experts=experts, groups=groups, capacity=capacity),
        out_shape=(
            result(seq_len, width),
            result(seq_len, width + 128),
            result(seq_len, width),
            result(seq_len, hidden),
            result(seq_len, act_cols),
            result(all_picked, width),
            result(all_picked, ehidden),
            result(all_picked, ehidden),
            result(all_picked, ehidden),
            result(all_picked, width),
        ),
        grid_spec=pltpu.PrefetchScalarGridSpec(
            num_scalar_prefetch=1,
            grid=(groups // blocks,),
            in_specs=[
                pl.BlockSpec((width, rows), lambda i, _: (0, i)),
                step_rows(rows, width),
                step_rows(rows, width),
                pl.BlockSpec((blocks, 1, rows_dev), lambda i, _: (i, 0, 0)),
                packed_part(width, 0),
                packed_part(hidden, width),
                packed_part(hidden, width + hidden),
                packed_part(128, width + act_cols),
                whole(down.shape),
                whole(egate.shape),
                whole(eup.shape),
                whole(edown.shape),
            ],
            out_specs=(
                step_rows(rows, width),
                step_rows(rows, width + 128),
                step_rows(rows, width),
                step_rows(rows, hidden),
                step_rows(rows, act_cols),
                step_rows(picked, width),
                step_rows(picked, ehidden),
                step_rows(picked, ehidden),
                step_rows(picked, ehidden),
                step_rows(picked, width),
            ),
        ),
        compiler_params=pltpu.CompilerParams(vmem_limit_bytes=ALL_VMEM),
        cost_estimate=pl.CostEstimate(
            flops=flops, bytes_accessed=40 << 20, transcendentals=2 * all_picked * ehidden
        ),
        name="branches",
    )(info, mixed, tokens, cotangent, rank, packed, packed, packed, packed, down, egate, eup, edown)


def own_rows_kernel(
    info_ref,
    grad_ref,
    mixed_ref,
    tokens_ref,
    cotangent_ref,
    out_w_ref,
    small_ref,
    shared_ref,
    *refs,
    experts,
    groups,
    window_starts,
):
    hidden_ref, grad_hidden_ref, grad_mixed_ref, *first_refs, last_keep_ref, last_send_ref = refs[
        -7:
    ]
    rows, width = tokens_ref.shape
    length, me = (info_ref[0], info_ref[1])
    small = small_ref[...].astype(F32)
    gain = small.T[experts : experts + 1]
    hidden = tokens_ref[...].astype(F32) + matmul_tn(mixed_ref[...], out_w_ref[...])
    scale = inv_rms(hidden)
    unit = hidden * scale
    normed = (unit * gain).astype(BF16)
    lane = lax.broadcasted_iota(jnp.int32, (rows, 128), 1)
    is_expert = lane < experts
    logits = jnp.where(is_expert, matmul(normed, small.astype(BF16)), NEG_FILL)
    weights = jnp.exp(logits - jnp.max(logits, axis=1, keepdims=True))
    probs = weights / jnp.sum(weights, axis=1, keepdims=True)
    dots = grad_ref[:, width:].astype(F32)
    grad_probs = jnp.zeros((rows, 128), F32)
    for expert in range(experts):
        source = lane % groups // 2
        part = jnp.where((lane < 2 * groups) & (source == expert), dots, 0.0)
        grad_probs = jnp.where(
            lane == expert, jnp.sum(part, axis=1, keepdims=True), grad_probs
        )
    mean = jnp.sum(probs * grad_probs, axis=1, keepdims=True)
    grad_logits = jnp.where(is_expert, probs * (grad_probs - mean), 0.0).astype(BF16)
    router = jnp.where(
        lax.broadcasted_iota(jnp.int32, small.shape, 1) < experts, small, 0.0
    ).astype(BF16)
    grad_normed = grad_ref[:, :width].astype(F32) + matmul_nt(grad_logits, router)
    position = me * rows + lax.broadcasted_iota(jnp.int32, (rows, 1), 0)
    live = (position < length).astype(F32)
    grad_hidden = cotangent_ref[...].astype(F32) * live + rms_back(
        hidden, scale, grad_normed * gain
    )
    hidden_ref[...] = hidden * live
    grad_hidden_ref[...] = grad_hidden
    grad_hidden_b = grad_hidden.astype(BF16)
    grad_mixed = matmul_nt(out_w_ref[...], grad_hidden_b).astype(BF16)
    for dest, at in enumerate(window_starts):
        grad_mixed_ref[dest] = grad_mixed[at : at + grad_mixed_ref.shape[1]]
    cut = first_refs[0].shape[2]
    grad_out_w = matmul(mixed_ref[...], grad_hidden_b)
    put_halves(grad_out_w[:, :cut], info_ref[4], *first_refs)
    ones = jnp.where(lane == experts, 1.0, 0.0).astype(BF16)
    small_grad = matmul_tn(normed, grad_logits) + matmul_tn((grad_normed * unit).astype(BF16), ones)
    last = jnp.concatenate([grad_out_w[:, cut:], small_grad, shared_ref[...].astype(F32)], axis=1)
    put_halves(last, info_ref[5], last_keep_ref, last_send_ref)


def own_rows(
    info, grad_own, mixed, tokens, cotangent, packed, grad_shared, earlier, experts, groups, window,
    window_starts,
):
    rows, width = tokens.shape
    small_at = packed.shape[1] // 128 - 1

    def whole(shape):
        return pl.BlockSpec(shape, lambda i, _: (0,) * len(shape))

    shapes = (
        ((rows, width), F32),
        ((rows, width), F32),
        ((groups, window, rows), BF16),
        *(((groups, width // groups // 2, width - 128), BF16),) * 2,
        *(((groups, width // groups // 2, 256 + grad_shared.shape[1]), BF16),) * 2,
    )
    return pl.pallas_call(
        functools.partial(
            own_rows_kernel, experts=experts, groups=groups, window_starts=tuple(window_starts)
        ),
        out_shape=tuple(jax.ShapeDtypeStruct(shape, dtype) for shape, dtype in shapes),
        grid_spec=pltpu.PrefetchScalarGridSpec(
            num_scalar_prefetch=1,
            grid=(1,),
            in_specs=[
                whole(grad_own.shape),
                whole(mixed.shape),
                whole(tokens.shape),
                whole(cotangent.shape),
                whole((width, width)),
                pl.BlockSpec((width, 128), lambda i, _: (0, small_at)),
                whole(grad_shared.shape),
            ]
            + [IN_HBM] * len(earlier),
            out_specs=tuple(whole(shape) for shape, _ in shapes),
        ),
        compiler_params=pltpu.CompilerParams(vmem_limit_bytes=ALL_VMEM),
        cost_estimate=pl.CostEstimate(
            flops=6 * rows * width * width, bytes_accessed=6 << 20, transcendentals=rows * 128
        ),
        name="own_rows",
    )(info, grad_own, mixed, tokens, cotangent, packed, packed, grad_shared, *earlier)


def passed_after(values, mark):
    return pl.pallas_call(
        lambda *_: None,
        out_shape=jax.ShapeDtypeStruct(values.shape, values.dtype),
        in_specs=[IN_HBM, IN_HBM],
        out_specs=IN_HBM,
        input_output_aliases={0: 0},
        name="passed_after",
    )(values, mark)


def finish_down_kernel(mine_ref, *refs):
    half = pl.program_id(0)
    whole = jnp.concatenate(
        [
            jnp.where(
                mine_ref[part] == half, refs[part][...].astype(F32), refs[2 + part][...].astype(F32)
            )
            for part in range(2)
        ],
        axis=1,
    )
    rows = refs[4].shape[0]
    refs[4][...] = whole[:rows]
    refs[5][...] = whole[rows:]


def finish_down(mine, own, other, expert_rows):
    rows, cols = own[0].shape
    shapes = ((expert_rows, 2 * cols), (2 * rows - expert_rows, 2 * cols))
    return pl.pallas_call(
        finish_down_kernel,
        out_shape=tuple(jax.ShapeDtypeStruct(shape, F32) for shape in shapes),
        grid_spec=pltpu.PrefetchScalarGridSpec(
            num_scalar_prefetch=1,
            grid=(2,),
            in_specs=[pl.BlockSpec((rows, cols), lambda i, _: (0, 0))] * 4,
            out_specs=tuple(
                pl.BlockSpec((shape[0] // 2, shape[1]), lambda i, _: (i, 0)) for shape in shapes
            ),
        ),
        compiler_params=pltpu.CompilerParams(vmem_limit_bytes=32 << 20),
        cost_estimate=pl.CostEstimate(flops=0, bytes_accessed=6 << 20, transcendentals=0),
        name="finish_down",
    )(mine, *own, *other)


def finish_dense_kernel(
    mine_ref, first_ref, first_other_ref, last_ref, last_other_ref, gain_ref, wq_ref, wk_ref, wv_ref,
    *refs
):
    *weight_refs, out_ref, gate_ref, up_ref, gain_one_ref, gain_two_ref, router_ref = refs[-9:]

    def pieces(own_ref, other_ref, mine, widths):
        own, other = (own_ref[...].astype(F32), other_ref[...].astype(F32))
        whole = jnp.concatenate(
            [jnp.where(mine == 0, own, other), jnp.where(mine == 0, other, own)], axis=0
        )
        at = 0
        for cols in widths:
            yield whole[:, at : at + cols]
            at += cols

    width = out_ref.shape[1]
    *weights, out = pieces(first_ref, first_other_ref, mine_ref[0], [width] * 3 + [width - 128])
    out_end, small, gate, up = pieces(
        last_ref, last_other_ref, mine_ref[1], [128] * 2 + [gate_ref.shape[1]] * 2
    )
    gain_grad = jnp.zeros(gain_ref.shape, F32)
    for total, w_ref, weight_ref in zip(weights, (wq_ref, wk_ref, wv_ref), weight_refs):
        weight_ref[...] = total * gain_ref[...]
        gain_grad += jnp.sum(total * w_ref[...].astype(F32), axis=1, keepdims=True)
    out_ref[...] = jnp.concatenate([out, out_end], axis=1)
    gate_ref[...], up_ref[...] = (gate, up)
    lane = lax.broadcasted_iota(jnp.int32, small.shape, 1)
    experts = router_ref.shape[0]
    rows = jnp.where(lane == experts + 1, gain_grad, small).T
    router_ref[...] = rows[:experts]
    gain_two_ref[...] = rows[experts : experts + 1]
    gain_one_ref[...] = rows[experts + 1 : experts + 2]


def finish_dense(mine, first, first_other, last, last_other, gain, weights, earlier, experts):
    rows, width = weights[0].shape
    half = (last.shape[1] - 256) // 2
    shapes = [(rows, width)] * 4 + [(rows, half)] * 2 + [(1, rows)] * 2 + [(experts, rows)]
    vmem = pl.BlockSpec(memory_space=pltpu.VMEM)
    return pl.pallas_call(
        finish_dense_kernel,
        out_shape=tuple(jax.ShapeDtypeStruct(shape, F32) for shape in shapes),
        in_specs=[pl.BlockSpec(memory_space=pltpu.SMEM)] + [vmem] * 8 + [IN_HBM] * len(earlier),
        out_specs=(vmem,) * len(shapes),
        compiler_params=pltpu.CompilerParams(vmem_limit_bytes=ALL_VMEM),
        name="finish_dense",
    )(mine, first, first_other, last, last_other, gain, *weights, *earlier)


def side_by_side_kernel(*refs, count):
    at = 0
    for ref in refs[:count]:
        end = at + ref.shape[2]
        refs[-1][:, :, at:end] = ref[...]
        at = end


def side_by_side(parts, earlier):
    vmem = pl.BlockSpec(memory_space=pltpu.VMEM)
    cols = sum(part.shape[2] for part in parts)
    return pl.pallas_call(
        functools.partial(side_by_side_kernel, count=len(parts)),
        out_shape=jax.ShapeDtypeStruct((*parts[0].shape[:2], cols), BF16),
        in_specs=[vmem] * len(parts) + [IN_HBM] * len(earlier),
        out_specs=vmem,
        compiler_params=pltpu.CompilerParams(vmem_limit_bytes=ALL_VMEM),
        name="side_by_side",
    )(*parts, *earlier)


def assemble_kernel(back_ref, *refs, offsets, width, window):
    first_ref, last_ref = refs[-2:]
    groups = back_ref.shape[0]
    back = [back_ref[d].astype(F32) for d in range(groups)]
    cols_dev, first_at = (width // groups, 3 * window)
    last_at = first_at + width - 128
    act_at = last_at + 256
    hidden = (back_ref.shape[2] - act_at) // 2
    columns = [
        back[d][:, part * window + offsets[d] : part * window + offsets[d] + cols_dev]
        for part in range(3)
        for d in range(groups)
    ]
    summed = back[0][:, first_at:act_at]
    for d in range(1, groups):
        summed += back[d][:, first_at:act_at]
    first_ref[...] = jnp.concatenate(columns + [summed[:, : last_at - first_at]], axis=1).astype(
        BF16
    )
    last_ref[...] = jnp.concatenate(
        [summed[:, last_at - first_at :]]
        + [
            back[d][:, act_at + part * hidden : act_at + (part + 1) * hidden]
            for part in range(2)
            for d in range(groups)
        ],
        axis=1,
    ).astype(BF16)


def assemble(back, offsets, width, hidden, window, earlier):
    groups, rows, cols = back.shape
    vmem = pl.BlockSpec(memory_space=pltpu.VMEM)
    return pl.pallas_call(
        functools.partial(
            assemble_kernel, offsets=tuple(offsets), width=width, window=window
        ),
        out_shape=(
            jax.ShapeDtypeStruct((rows, 4 * width - 128), BF16),
            jax.ShapeDtypeStruct((rows, 256 + 2 * groups * hidden), BF16),
        ),
        in_specs=[vmem] + [IN_HBM] * len(earlier),
        out_specs=(vmem, vmem),
        compiler_params=pltpu.CompilerParams(vmem_limit_bytes=ALL_VMEM),
        name="assemble",
    )(back, *earlier)


def finish_rows_kernel(
    info_ref, hidden_ref, branch_ref, grad_hidden_ref, grad_unit_ref, tokens_ref, out_ref, grad_ref
):
    rows = hidden_ref.shape[0]
    position = info_ref[1] * rows + lax.broadcasted_iota(jnp.int32, (rows, 1), 0)
    live = (position < info_ref[0]).astype(F32)
    out_ref[...] = (hidden_ref[...] + live * branch_ref[...].astype(F32)).astype(BF16)
    inputs = tokens_ref[...].astype(F32)
    grad_ref[...] = grad_hidden_ref[...] + rms_back(
        inputs, inv_rms(inputs), grad_unit_ref[...].astype(F32)
    )


def finish_rows(info, hidden, branch, grad_hidden, grad_unit, tokens):
    vmem = pl.BlockSpec(memory_space=pltpu.VMEM)
    return pl.pallas_call(
        finish_rows_kernel,
        out_shape=(
            jax.ShapeDtypeStruct(hidden.shape, BF16),
            jax.ShapeDtypeStruct(hidden.shape, F32),
        ),
        in_specs=[pl.BlockSpec(memory_space=pltpu.SMEM)] + [vmem] * 5,
        out_specs=(vmem, vmem),
        compiler_params=pltpu.CompilerParams(vmem_limit_bytes=ALL_VMEM),
        name="finish_rows",
    )(info, hidden, branch, grad_hidden, grad_unit, tokens)


def gather_rows(values):
    return lax.all_gather(values, "fsdp", axis=0, tiled=True)


def exchange(chunks):
    return lax.all_to_all(chunks, "fsdp", split_axis=0, concat_axis=0, tiled=True)


def scatter_sum(values):
    return lax.psum_scatter(values, "fsdp", scatter_dimension=0, tiled=True)


def after(values, mark):
    mark = mark[(slice(-1, None),) * mark.ndim].reshape(()).astype(F32)
    return jnp.where(mark < jnp.inf, values, jnp.zeros((), values.dtype))


def swap_rep(values, bit):
    count = lax.axis_size("rep")
    return lax.ppermute(values, "rep", [(i, i ^ (1 << bit)) for i in range(count)])


def rep_bits():
    count = lax.axis_size("rep")
    bits = count.bit_length() - 1
    assert count == 1 << bits
    return range(bits)


def rep_add(keep, send, bit, mark=None):
    if mark is not None:
        keep = after(keep, mark)
    return (keep.astype(F32) + swap_rep(send, bit).astype(F32)).astype(keep.dtype)


def rep_step(values, axis, bit, ready=None):
    half = values.shape[axis] // 2
    mine = (lax.axis_index("rep") >> bit) & 1
    keep = lax.dynamic_slice_in_dim(values, mine * half, half, axis)
    send = lax.dynamic_slice_in_dim(values, (1 - mine) * half, half, axis)
    if ready is not None:
        send = after(send, ready)
    return rep_add(keep, send, bit)


def rep_scatter_sum(values, axis, bits):
    for bit in bits:
        values = rep_step(values, axis, bit)
    return values


def rep_join(values, axis, bits=None):
    index = lax.axis_index("rep")
    for bit in reversed(rep_bits() if bits is None else bits):
        values = joined(values, swap_rep(values, bit), (index >> bit) & 1, axis)
    return values


def joined(own, other, mine, axis):
    return jnp.where(
        mine == 0,
        jnp.concatenate([own, other], axis=axis),
        jnp.concatenate([other, own], axis=axis),
    )


def on_device(
    tokens,
    cotangent,
    lengths,
    routes,
    gain_attn,
    gain_ffn,
    w_query,
    w_key,
    w_value,
    w_out,
    w_router,
    shared_gate,
    shared_up,
    shared_down,
    expert_gate,
    expert_up,
    expert_down,
):
    rows_dev, width = tokens.shape[1:]
    groups = lax.axis_size("fsdp")
    reps = lax.axis_size("rep")
    me = lax.axis_index("fsdp")
    seq_len = groups * rows_dev
    experts = w_router.shape[1]
    capacity = min(rows_dev, 5 * rows_dev // (2 * experts))
    length = lengths[0]
    my_rows = me * rows_dev
    live_all = jnp.arange(seq_len, dtype=jnp.int32) < length
    live_col = lax.dynamic_slice_in_dim(live_all, my_rows, rows_dev, 0).astype(F32)[:, None]

    cols_dev = width // groups
    first_heads = [d * cols_dev // HEAD_DIM for d in range(groups)]
    span = max(-(-(d + 1) * cols_dev // HEAD_DIM) - first_heads[d] for d in range(groups))
    first_heads = [min(head, HEADS - span) for head in first_heads]
    window = span * HEAD_DIM
    window_starts = [head * HEAD_DIM for head in first_heads]
    offsets = [d * cols_dev - window_starts[d] for d in range(groups)]
    my_offset = jnp.asarray(offsets, jnp.int32)[me]

    tokens_all = gather_rows(tokens[0])
    rep_rows = cols_dev // reps
    rep_at = lax.axis_index("rep") * rep_rows

    def rep_part(weight):
        return lax.dynamic_slice_in_dim(weight, rep_at, rep_rows, 0)

    gain_part = rep_part(gain_attn).astype(F32)[:, None]
    qkv_rows = [
        (rep_part(weight).astype(F32) * gain_part).astype(BF16)
        for weight in (w_query, w_key, w_value)
    ]
    qkv_chunks = jnp.stack(
        [
            jnp.concatenate([weight[:, at : at + window] for weight in qkv_rows], axis=1)
            for at in window_starts
        ]
    )
    qkv_part = exchange(qkv_chunks)
    qkv_cols = lax.all_gather(qkv_part, "rep", axis=0)
    qkv_cols = qkv_cols.transpose(1, 0, 2, 3).reshape(width, 3 * window)
    cosine, sine = rope_tables(seq_len)

    cotangent_all = gather_rows(after(cotangent[0], qkv_cols))
    shared_cols_dev = shared_gate.shape[1] // groups
    gate_chunks, up_chunks = [
        rep_part(weight).reshape(rep_rows, groups, shared_cols_dev).transpose(1, 0, 2)
        for weight in (shared_gate, shared_up)
    ]
    route_cols = -(-2 * rows_dev // rep_rows)
    route_chunk = jnp.pad(
        routes[0].astype(BF16).reshape(-1), (0, route_cols * rep_rows - 2 * rows_dev)
    ).reshape(rep_rows, route_cols)
    small_cols = experts + 1 + route_cols
    small = jnp.concatenate(
        [
            rep_part(w_router),
            rep_part(gain_ffn)[:, None],
            route_chunk,
            jnp.zeros((rep_rows, -small_cols % 128), BF16),
        ],
        axis=1,
    )
    packed_part = exchange(
        after(
            jnp.concatenate(
                [
                    jnp.broadcast_to(rep_part(w_out), (groups, rep_rows, width)),
                    gate_chunks,
                    up_chunks,
                    jnp.broadcast_to(small, (groups, *small.shape)),
                ],
                axis=2,
            ),
            qkv_cols,
        )
    )
    small_at = width + 2 * shared_cols_dev
    routes_all = (
        packed_part[:, :, small_at + experts + 1 : small_at + small_cols]
        .reshape(groups, rep_rows * route_cols)[:, : 2 * rows_dev]
        .reshape(groups, rows_dev, 2)
        .astype(jnp.int32)
    )
    packed_all = lax.psum(
        lax.dynamic_update_slice_in_dim(
            jnp.zeros((groups, cols_dev, small_at + 128), BF16),
            packed_part[:, :, : small_at + 128],
            rep_at,
            1,
        ),
        "rep",
    ).reshape(width, -1)
    routed = jnp.any(routes_all == me // 2, axis=2) & live_all.reshape(groups, rows_dev)
    rank = jnp.cumsum(routed.astype(jnp.int32), axis=1) - 1
    rank = jnp.where(routed, rank, -1)[:, None, :]

    inputs_all = tokens_all.astype(F32)
    unit = (inputs_all * inv_rms(inputs_all)).astype(BF16)
    qkv = contract(qkv_cols, unit, 0, 1)
    queries = (rotate_cols(qkv[:window], cosine, sine).astype(BF16).astype(F32) * 0.125).astype(
        BF16
    )
    keys = rotate_cols(qkv[window : 2 * window], cosine, sine).astype(BF16)
    values = qkv[2 * window :].astype(BF16)
    mixed_heads, log_norm = attn_forward(lengths, queries, keys, values)
    mixed_own = lax.dynamic_slice_in_dim(mixed_heads, my_offset, cols_dev, 0).astype(BF16)
    mixed_own = after(mixed_own, cotangent_all)
    mixed_all = gather_rows(mixed_own)

    orders = (list(rep_bits()), list(rep_bits())[::-1])
    mine, mine_next = [
        [(lax.axis_index("rep") >> order[step]) & 1 for order in orders] for step in range(2)
    ]
    info = jnp.stack([length, me, jnp.zeros((), jnp.int32), my_offset, *mine, *mine_next])
    (
        branch_part,
        grad_part,
        normed,
        shared_inner,
        shared_act_grad,
        rows_in,
        expert_inner,
        expert_gate_grad,
        expert_up_grad,
        grad_half,
    ) = run_branches(
        info,
        mixed_all,
        tokens_all,
        cotangent_all,
        rank,
        packed_all,
        shared_down,
        expert_gate,
        expert_up,
        expert_down,
        experts,
        capacity,
    )
    grad_own = scatter_sum(grad_part)

    half_cols = width // 2

    def half_grad(part, half):
        def of_rows(inner, grad):
            rows = inner.shape[1] // 2
            return matmul_tn(
                lax.dynamic_slice_in_dim(inner, half * rows, rows, 1),
                grad[:, part * half_cols : (part + 1) * half_cols],
            ).astype(BF16)

        return jnp.concatenate(
            [of_rows(expert_inner, grad_half), of_rows(shared_inner, cotangent_all)], axis=0
        )

    down_parts = [
        rep_scatter_sum(
            rep_add(half_grad(part, mine[part]), half_grad(part, 1 - mine[part]), order[0]),
            0,
            order[1:],
        )
        for part, order in enumerate(orders)
    ]
    whole_sums = lax.psum(
        (
            matmul_tn(rows_in, expert_gate_grad).astype(BF16),
            matmul_tn(rows_in, expert_up_grad).astype(BF16),
        ),
        "rep",
    )
    grad_shared = matmul_tn(normed, shared_act_grad).astype(BF16)
    mixed_rows = lax.dynamic_slice_in_dim(mixed_all, my_rows, rows_dev, 1)

    hidden, grad_hidden, grad_mixed, first_keep, first_send, last_keep, last_send = (
        own_rows(
            info,
            grad_own,
            mixed_rows,
            tokens[0],
            cotangent[0],
            packed_all,
            grad_shared,
            tuple(down_parts),
            experts,
            groups,
            window,
            window_starts,
        )
    )
    grad_mixed_cols = exchange(grad_mixed)
    branch_own = scatter_sum(passed_after(branch_part, grad_mixed_cols))
    grad_q, grad_k, grad_v = attn_backward(
        lengths,
        queries,
        keys,
        values,
        mixed_heads,
        log_norm,
        grad_mixed_cols,
        (),
    )
    (
        grad_unit_part,
        qkv_keep,
        qkv_send,
        first_keep,
        first_send,
        last_keep,
        last_send,
    ) = projections_backward(
        info,
        grad_q,
        grad_k,
        grad_v,
        cosine,
        sine,
        unit,
        qkv_cols,
        cols_dev,
        (
            first_keep,
            swap_rep(first_send, orders[0][0]),
            last_keep,
            swap_rep(last_send, orders[1][0]),
        ),
    )
    qkv_part = rep_add(qkv_keep, qkv_send, orders[0][0])
    dense_first = rep_scatter_sum(
        rep_add(first_keep, first_send, orders[0][1]), 1, orders[0][2:]
    )
    dense_last = rep_scatter_sum(rep_add(last_keep, last_send, orders[1][1]), 1, orders[1][2:])
    grad_unit = scatter_sum(grad_unit_part)
    output, input_grad = finish_rows(info, hidden, branch_own, grad_hidden, grad_unit, tokens[0])

    down_own = [rep_join(part, 0, order[1:]) for part, order in zip(down_parts, orders)]
    down_other = [swap_rep(own, order[0]) for own, order in zip(down_own, orders)]
    sum_edown, sum_down = finish_down(
        jnp.stack(mine), down_own, down_other, expert_inner.shape[1]
    )
    qkv_part = rep_scatter_sum(qkv_part, 1, orders[0][1:])
    back = exchange(
        side_by_side(
            (qkv_part, dense_first, dense_last), (*down_own, whole_sums[1], branch_own)
        )
    )
    sum_egate, sum_eup = [after(total, back).astype(F32) for total in whole_sums]
    first_part, last_part = assemble(back, offsets, width, shared_cols_dev, window, (sum_edown,))
    first_part = rep_join(first_part, 0, orders[0][1:])
    last_part = rep_join(last_part, 0, orders[1][1:])
    first_other = swap_rep(first_part, orders[0][0])
    last_other = swap_rep(last_part, orders[1][0])
    *sums_qkv, sum_out, sum_gate, sum_up, sum_gain_attn, sum_gain_ffn, sum_router = finish_dense(
        jnp.stack(mine),
        first_part,
        first_other,
        last_part,
        last_other,
        gain_attn.astype(F32)[:, None],
        (w_query, w_key, w_value),
        (sum_egate, sum_edown),
        experts,
    )
    return (
        output[None],
        input_grad[None],
        sum_gain_attn[0],
        sum_gain_ffn[0],
        *sums_qkv,
        sum_out,
        sum_router.T,
        sum_gate,
        sum_up,
        sum_down,
        sum_egate,
        sum_eup,
        sum_edown,
    )


def solution(mesh):
    in_specs = (
        P("rep", "fsdp", None),
        P("rep", "fsdp", None),
        P("rep"),
        P("rep", "fsdp", None),
        P("fsdp"),
        P("fsdp"),
        P("fsdp", None),
        P("fsdp", None),
        P("fsdp", None),
        P("fsdp", None),
        P("fsdp", None),
        P("fsdp", None),
        P("fsdp", None),
        P("fsdp", None),
        P(None, "fsdp"),
        P(None, "fsdp"),
        P("fsdp", None),
    )
    out_specs = (
        P("rep", "fsdp", None),
        P("rep", "fsdp", None),
        P("fsdp"),
        P("fsdp"),
        P("fsdp", None),
        P("fsdp", None),
        P("fsdp", None),
        P("fsdp", None),
        P("fsdp", None),
        P("fsdp", None),
        P("fsdp", None),
        P("fsdp", None),
        P(None, "fsdp"),
        P(None, "fsdp"),
        P("fsdp", None),
    )
    return jax.shard_map(
        on_device, mesh=mesh, in_specs=in_specs, out_specs=out_specs, check_vma=False
    )
```
